32 devices in a mesh: ctx: 8 (over z, y), tp: 4 (over x, core).
Axes of the slice: x: 2, y: 2, z: 4, core: 2. Of those that a mesh axis runs over, the one named last changes fastest.
Arguments:
- short_query: bfloat16 [1024, 2048], P('ctx', 'tp'), may hold values from -6 to 6
- short_key: bfloat16 [1024, 2048], P('ctx', 'tp'), may hold values from -6 to 6
- short_value: bfloat16 [1024, 2048], P('ctx', 'tp'), may hold values from -6 to 6
- short_filter: bfloat16 [128, 2048], P(None, 'tp'), may hold values from -0.5 to 0.5
- long_query: bfloat16 [1024, 2048], P('ctx', 'tp'), may hold values from -6 to 6
- long_key: bfloat16 [1024, 2048], P('ctx', 'tp'), may hold values from -6 to 6
- long_filter: bfloat16 [1024, 2048], P('ctx', 'tp'), may hold values from -0.1875 to 0.1875
- out_weight: bfloat16 [2048, 2048], P('tp'), may hold values from -0.125 to 0.125
- out_grad: bfloat16 [1024, 2048], P('ctx', 'tp'), may hold values from -6 to 6
Outputs:
- short_query_grad: bfloat16 [1024, 2048], P('ctx', 'tp')
- short_key_grad: bfloat16 [1024, 2048], P('ctx', 'tp')
- short_value_grad: bfloat16 [1024, 2048], P('ctx', 'tp')
- short_filter_grad: bfloat16 [128, 2048], P(None, 'tp')
- long_query_grad: bfloat16 [1024, 2048], P('ctx', 'tp')
- long_key_grad: bfloat16 [1024, 2048], P('ctx', 'tp')
- long_filter_grad: bfloat16 [1024, 2048], P('ctx', 'tp')
The draws below stay inside these ranges and needn't reach their ends.
All inputs are finite; a program needn't handle non-finite values.
Results may differ from the reference program's by a relative error of at most 0.015.
Values may be sent and summed in bfloat16 or wider, within the bound.
A program may use at most 64 MiB of HBM per device.

```python
import math
import jax
import jax.numpy as jnp
from jax import lax

D = 2048
TAPS = 128
SEQ = 1024


def level_of(key, dims, split, low, largest):
    gain = 1.0
    for position, shards_of in split:
        steps = jax.random.uniform(jax.random.fold_in(jax.random.fold_in(key, 6), position), (shards_of,), jnp.float32, low / len(split), largest / len(split))
        gain = gain * jnp.repeat(jnp.exp(steps), dims[position] // shards_of).reshape((-1,) + (1,) * (len(dims) - 1 - position))
    return gain


def normal_values(key, extent, spread, most, split=(), kind=jnp.bfloat16):
    drawn = spread * jax.random.normal(key, extent, jnp.float32)
    if split:
        drawn = drawn * level_of(key, extent, split, -0.22, 0.18)
    return jnp.clip(drawn, -most, most).astype(kind)


def setup_inputs(seed: int = 0) -> dict:
    seeds = jax.random.split(jax.random.key(seed), 10)
    return {
        "short_query": normal_values(seeds[0], (SEQ, D), 1.0, 6.0, ((0, 8), (1, 4))),
        "short_key": normal_values(seeds[1], (SEQ, D), 1.0, 6.0, ((0, 8), (1, 4))),
        "short_value": normal_values(seeds[2], (SEQ, D), 1.0, 6.0, ((0, 8), (1, 4))),
        "short_filter": normal_values(seeds[3], (TAPS, D), TAPS ** -0.5, 0.5, ((1, 4),)),
        "long_query": normal_values(seeds[4], (SEQ, D), 1.0, 6.0, ((0, 8), (1, 4))),
        "long_key": normal_values(seeds[5], (SEQ, D), 1.0, 6.0, ((0, 8), (1, 4))),
        "long_filter": normal_values(seeds[6], (SEQ, D), SEQ ** -0.5, 0.1875, ((0, 8), (1, 4))),
        "out_weight": normal_values(seeds[7], (D, D), D ** -0.5, 0.125, ((0, 4),)),
        "out_grad": normal_values(seeds[8], (SEQ, D), 1.0, 6.0, ((0, 8), (1, 4))),
    }


def causal_taps(values, weights):
    filter_taps = weights.shape[0]
    length = values.shape[0]
    padded = jnp.pad(values.astype(jnp.float32), ((filter_taps - 1, 0), (0, 0)))

    def add_tap(offset, total):
        place = jnp.asarray(offset).astype(jnp.int32)
        weight_row = lax.dynamic_index_in_dim(weights, place, 0, keepdims=False).astype(jnp.float32)
        shifted = lax.dynamic_slice_in_dim(padded, filter_taps - 1 - place, length, 0)
        return total + weight_row[None, :] * shifted
    return lax.fori_loop(0, filter_taps, add_tap, jnp.zeros(values.shape, jnp.float32))

def anti_taps(values, weights):
    filter_taps = weights.shape[0]
    length = values.shape[0]
    padded = jnp.pad(values.astype(jnp.float32), ((0, filter_taps - 1), (0, 0)))

    def add_tap(offset, total):
        place = jnp.asarray(offset).astype(jnp.int32)
        weight_row = lax.dynamic_index_in_dim(weights, place, 0, keepdims=False).astype(jnp.float32)
        shifted = lax.dynamic_slice_in_dim(padded, place, length, 0)
        return total + weight_row[None, :] * shifted
    return lax.fori_loop(0, filter_taps, add_tap, jnp.zeros(values.shape, jnp.float32))

def tap_products(grads, values, filter_taps):
    length = values.shape[0]
    padded = jnp.pad(values.astype(jnp.float32), ((filter_taps - 1, 0), (0, 0)))

    def one_tap(place):
        shifted = lax.dynamic_slice_in_dim(padded, filter_taps - 1 - place, length, 0)
        return lax.optimization_barrier(jnp.sum(grads * shifted, axis=0))
    return lax.map(one_tap, jnp.arange(filter_taps, dtype=jnp.int32))

def reference(short_query, short_key, short_value, short_filter, long_query, long_key, long_filter, out_weight, out_grad):
    product_one = (short_key.astype(jnp.float32) * short_value.astype(jnp.float32)).astype(jnp.bfloat16)
    short_mix = causal_taps(product_one, short_filter)
    mixed = (short_query.astype(jnp.float32) * short_mix).astype(jnp.bfloat16)
    product_two = (long_key.astype(jnp.float32) * mixed.astype(jnp.float32)).astype(jnp.bfloat16)
    grad_two = jnp.dot(out_grad, out_weight.T, preferred_element_type=jnp.float32).astype(jnp.bfloat16)
    gated_two = (grad_two.astype(jnp.float32) * long_query.astype(jnp.float32)).astype(jnp.bfloat16)
    points = 2 * SEQ
    spec_prod = jnp.fft.rfft(product_two.astype(jnp.float32), n=points, axis=0)
    spec_gated = jnp.fft.rfft(gated_two.astype(jnp.float32), n=points, axis=0)
    spec_filter = jnp.fft.rfft(long_filter.astype(jnp.float32), n=points, axis=0)
    long_mix = jnp.fft.irfft(spec_filter * spec_prod, n=points, axis=0)[:SEQ]
    back_two = jnp.fft.irfft(jnp.conj(spec_filter) * spec_gated, n=points, axis=0)[:SEQ]
    filter_two = jnp.fft.irfft(jnp.conj(spec_prod) * spec_gated, n=points, axis=0)[:SEQ]
    scaling = 1.0 / math.sqrt(SEQ)
    long_query_grad = (grad_two.astype(jnp.float32) * long_mix).astype(jnp.bfloat16)
    long_key_grad = (back_two * mixed.astype(jnp.float32)).astype(jnp.bfloat16)
    mixed_grad = (back_two * long_key.astype(jnp.float32)).astype(jnp.bfloat16)
    long_filter_grad = (filter_two * scaling).astype(jnp.bfloat16)
    gated_one = (mixed_grad.astype(jnp.float32) * short_query.astype(jnp.float32)).astype(jnp.bfloat16)
    short_query_grad = (mixed_grad.astype(jnp.float32) * short_mix).astype(jnp.bfloat16)
    back_one = anti_taps(gated_one, short_filter)
    short_key_grad = (back_one * short_value.astype(jnp.float32)).astype(jnp.bfloat16)
    short_value_grad = (back_one * short_key.astype(jnp.float32)).astype(jnp.bfloat16)
    filter_one = tap_products(gated_one.astype(jnp.float32), product_one, short_filter.shape[0])
    short_filter_grad = (filter_one * scaling).astype(jnp.bfloat16)
    return (short_query_grad, short_key_grad, short_value_grad, short_filter_grad, long_query_grad, long_key_grad, long_filter_grad)
```

```python
import functools
import math

import jax
import jax.numpy as jnp
import ml_dtypes
import numpy as np
from jax import lax
from jax.experimental import pallas as pl
from jax.experimental.pallas import tpu as pltpu
from jax.sharding import PartitionSpec as P

MESH = pl.DeviceIdType.MESH
BF16 = jnp.bfloat16
F32 = jnp.float32
LONGEST_DENSE = 2048
PARTS = ("prod", "gates", "grad", "smix", "lmix", "filt", "back", "bone", "taps")


def passed_along(block, axis, distance):
    devices = range(lax.axis_size(axis))
    route = [(i - distance, i) for i in devices if i - distance in devices]
    return lax.ppermute(block, axis, route)


def angle_tables(blocks, inner):
    size_one = 2 * blocks
    whole = size_one * inner
    first = (
        lax.broadcasted_iota(jnp.int32, (size_one, blocks), 0)
        * lax.broadcasted_iota(jnp.int32, (size_one, blocks), 1)
        % size_one
    )
    phase_one = first.astype(jnp.float32) * (2.0 * math.pi / size_one)
    twist = (
        lax.broadcasted_iota(jnp.int32, (size_one, inner), 0)
        * lax.broadcasted_iota(jnp.int32, (size_one, inner), 1)
        % whole
    )
    phase_twist = twist.astype(jnp.float32) * (2.0 * math.pi / whole)
    second = (
        lax.broadcasted_iota(jnp.int32, (inner, inner), 0)
        * lax.broadcasted_iota(jnp.int32, (inner, inner), 1)
        % inner
    )
    phase_two = second.astype(jnp.float32) * (2.0 * math.pi / inner)
    return (
        jnp.cos(phase_one),
        jnp.sin(phase_one),
        jnp.cos(phase_twist)[:, None, :],
        jnp.sin(phase_twist)[:, None, :],
        jnp.cos(phase_two),
        jnp.sin(phase_two),
        whole,
    )


def spectrum(values, tables):
    cos_one, sin_one, cos_twist, sin_twist, cos_two, sin_two, whole = tables
    highest = lax.Precision.HIGHEST
    real_a = jnp.einsum("kn,ncm->kcm", cos_one, values, precision=highest)
    imag_a = -jnp.einsum("kn,ncm->kcm", sin_one, values, precision=highest)
    real_b = real_a * cos_twist + imag_a * sin_twist
    imag_b = imag_a * cos_twist - real_a * sin_twist
    real_c = jnp.einsum("kcm,mq->kcq", real_b, cos_two, precision=highest) + jnp.einsum(
        "kcm,mq->kcq", imag_b, sin_two, precision=highest
    )
    imag_c = jnp.einsum("kcm,mq->kcq", imag_b, cos_two, precision=highest) - jnp.einsum(
        "kcm,mq->kcq", real_b, sin_two, precision=highest
    )
    return (real_c, imag_c)


def restore(real_in, imag_in, tables, both):
    cos_one, sin_one, cos_twist, sin_twist, cos_two, sin_two, whole = tables
    highest = lax.Precision.HIGHEST
    real_p = jnp.einsum("kcq,qm->kcm", real_in, cos_two, precision=highest) - jnp.einsum(
        "kcq,qm->kcm", imag_in, sin_two, precision=highest
    )
    imag_p = jnp.einsum("kcq,qm->kcm", imag_in, cos_two, precision=highest) + jnp.einsum(
        "kcq,qm->kcm", real_in, sin_two, precision=highest
    )
    real_q = real_p * cos_twist - imag_p * sin_twist
    imag_q = imag_p * cos_twist + real_p * sin_twist
    real_out = (
        jnp.einsum("kn,kcm->ncm", cos_one, real_q, precision=highest)
        - jnp.einsum("kn,kcm->ncm", sin_one, imag_q, precision=highest)
    ) / whole
    if both:
        imag_out = (
            jnp.einsum("kn,kcm->ncm", cos_one, imag_q, precision=highest)
            + jnp.einsum("kn,kcm->ncm", sin_one, real_q, precision=highest)
        ) / whole
        return (real_out, imag_out)
    return real_out


def spectral(product, gated, filter_in):
    blocks, count, inner = product.shape
    tables = angle_tables(blocks, inner)
    real_u, imag_u = spectrum(product.astype(jnp.float32), tables)
    real_g, imag_g = spectrum(gated.astype(jnp.float32), tables)
    real_h, imag_h = spectrum(filter_in.astype(jnp.float32), tables)
    real_pair = real_h * real_u - imag_h * imag_u - real_h * imag_g + imag_h * real_g
    imag_pair = real_h * imag_u + imag_h * real_u + real_h * real_g + imag_h * imag_g
    conv_part, back_part = restore(real_pair, imag_pair, tables, True)
    filter_part = restore(
        real_u * real_g + imag_u * imag_g, real_u * imag_g - imag_u * real_g, tables, False
    )
    return (conv_part, back_part, filter_part)


def tap_sum(extended, weights, token_rows, causal):
    filter_taps, channels = weights.shape

    def group_step(group, total):
        for inner in range(8):
            place = group * 8 + inner
            weight_row = lax.dynamic_index_in_dim(weights, place, 0, keepdims=False).astype(
                jnp.float32
            )
            start = filter_taps - 1 - place if causal else place
            shifted = lax.dynamic_slice_in_dim(extended, start, token_rows, 0).astype(jnp.float32)
            total = total + weight_row[None, :] * shifted
        return total

    return lax.fori_loop(
        0, filter_taps // 8, group_step, jnp.zeros((token_rows, channels), jnp.float32)
    )


def filter_terms(extended, grads, filter_taps):
    token_rows, channels = grads.shape

    def group_terms(group):
        partials = []
        for inner in range(8):
            place = group * 8 + inner
            shifted = lax.dynamic_slice_in_dim(
                extended, filter_taps - 1 - place, token_rows, 0
            ).astype(jnp.float32)
            partials.append(jnp.sum(grads * shifted, axis=0))
        return jnp.stack(partials)

    stacked = lax.map(group_terms, jnp.arange(filter_taps // 8, dtype=jnp.int32))
    return stacked.reshape(filter_taps, channels)


def general_body(
    short_query,
    short_key,
    short_value,
    short_filter,
    long_query,
    long_key,
    long_filter,
    out_weight,
    out_grad,
):
    token_rows, channels = short_query.shape
    groups = lax.axis_size("ctx")
    seq_len = token_rows * groups
    scaling = 1.0 / math.sqrt(seq_len)
    filter_taps = short_filter.shape[0]
    product_one = (short_key.astype(jnp.float32) * short_value.astype(jnp.float32)).astype(
        jnp.bfloat16
    )
    before = passed_along(product_one[token_rows - (filter_taps - 1) :], "ctx", 1)
    extended_prod = jnp.concatenate([before, product_one], axis=0)
    short_mix = tap_sum(extended_prod, short_filter, token_rows, True)
    mixed = (short_query.astype(jnp.float32) * short_mix).astype(jnp.bfloat16)
    grad_two = lax.dot_general(
        lax.all_gather(out_grad, "tp", axis=1, tiled=True),
        out_weight,
        (((1,), (1,)), ((), ())),
        preferred_element_type=jnp.float32,
    ).astype(jnp.bfloat16)

    def to_channels(values):
        return values.T.reshape(groups, channels // groups, token_rows)

    def to_tokens(values):
        return values.reshape(channels, token_rows).T

    product_two = (long_key.astype(jnp.float32) * mixed.astype(jnp.float32)).astype(jnp.bfloat16)
    gated_two = (grad_two.astype(jnp.float32) * long_query.astype(jnp.float32)).astype(jnp.bfloat16)
    conv_part, back_part, filter_part = spectral(
        lax.all_to_all(to_channels(product_two), "ctx", split_axis=0, concat_axis=0, tiled=True),
        lax.all_to_all(to_channels(gated_two), "ctx", split_axis=0, concat_axis=0, tiled=True),
        lax.all_to_all(to_channels(long_filter), "ctx", split_axis=0, concat_axis=0, tiled=True),
    )
    long_mix = lax.all_to_all(conv_part, "ctx", split_axis=0, concat_axis=0, tiled=True)
    back_two = lax.all_to_all(back_part, "ctx", split_axis=0, concat_axis=0, tiled=True)
    filter_two = lax.all_to_all(filter_part, "ctx", split_axis=0, concat_axis=0, tiled=True)
    long_mix = to_tokens(long_mix)
    back_two = to_tokens(back_two)
    filter_two = to_tokens(filter_two)
    long_query_grad = (grad_two.astype(jnp.float32) * long_mix).astype(jnp.bfloat16)
    long_key_grad = (back_two * mixed.astype(jnp.float32)).astype(jnp.bfloat16)
    mixed_grad = (back_two * long_key.astype(jnp.float32)).astype(jnp.bfloat16)
    long_filter_grad = (filter_two * scaling).astype(jnp.bfloat16)
    gated_one = (mixed_grad.astype(jnp.float32) * short_query.astype(jnp.float32)).astype(
        jnp.bfloat16
    )
    short_query_grad = (mixed_grad.astype(jnp.float32) * short_mix).astype(jnp.bfloat16)
    after = passed_along(gated_one[: filter_taps - 1], "ctx", -1)
    extended_grad = jnp.concatenate([gated_one, after], axis=0)
    back_one = tap_sum(extended_grad, short_filter, token_rows, False)
    short_key_grad = (back_one * short_value.astype(jnp.float32)).astype(jnp.bfloat16)
    short_value_grad = (back_one * short_key.astype(jnp.float32)).astype(jnp.bfloat16)
    local_terms = filter_terms(extended_prod, gated_one.astype(jnp.float32), filter_taps)
    filter_one = lax.psum(local_terms, "ctx")
    short_filter_grad = (filter_one * scaling).astype(jnp.bfloat16)
    return (
        short_query_grad,
        short_key_grad,
        short_value_grad,
        short_filter_grad,
        long_query_grad,
        long_key_grad,
        long_filter_grad,
    )


def wave_tables(seq_len):
    time = np.arange(seq_len, dtype=np.int64)[:, None]
    odd = 2 * np.arange(seq_len, dtype=np.int64)[None, :] + 1
    phase = (time * odd % (4 * seq_len)).astype(np.float64) * (math.pi / (2 * seq_len))
    forward = np.concatenate([np.cos(phase), np.sin(phase)], axis=1)
    return (
        forward.astype(ml_dtypes.bfloat16),
        np.ascontiguousarray(forward.T).astype(ml_dtypes.bfloat16),
    )


def dot(a, b):
    return jnp.dot(a, b, preferred_element_type=F32)


def flipped(block):
    return block.astype(F32).T.astype(BF16)


def operator_kernel(
    n, m,
    sq, sk, sv, sf, lq, lk, lf, og, weight, forward, inverse,
    grad_out, smix_out, lmix_out, filt_out, back_out, bone_out, taps_out,
    weight_v, fwd, inv, og_rx, tx_prod, tx_gates, tx_grad, rx_prod, rx_gates, rx_grad,
    tx_smix, tx_lmix, tx_filt, tx_back, tx_bone, tx_taps, filter_t, signals, smix,
    spec_prod, spec_sf, spec_u, spec_h, waves, load_sem, og_send, og_recv, send, recv,
):
    me = lax.axis_index("ctx")
    col = lax.axis_index("tp")
    rows, chans = sq.shape
    cb = chans // n
    taps = sf.shape[0]
    seq = rows * n
    tile = 2 * rows
    kt = 256

    loads = []
    for place, (source, target) in enumerate(((weight, weight_v), (forward, fwd), (inverse, inv))):
        load = pltpu.make_async_copy(source, target, load_sem.at[place])
        load.start()
        loads.append(load)

    barrier = pltpu.get_barrier_semaphore()
    for d in range(1, n):
        pl.semaphore_signal(
            barrier, inc=1, device_id=(lax.rem(me + d, n), col), device_id_type=MESH
        )
    for d in range(1, m):
        pl.semaphore_signal(
            barrier, inc=1, device_id=(me, lax.rem(col + d, m)), device_id_type=MESH
        )
    pl.semaphore_wait(barrier, n + m - 2)

    og_copies = []
    for d in range(1, m):
        copy = pltpu.make_async_remote_copy(
            src_ref=og,
            dst_ref=og_rx.at[d - 1],
            send_sem=og_send.at[d - 1],
            recv_sem=og_recv.at[d - 1],
            device_id=(me, lax.rem(col + d, m)),
            device_id_type=MESH,
        )
        copy.start()
        og_copies.append(copy)

    own_rows = pl.ds(pl.multiple_of(me * cb, cb), cb)
    sent = {}

    def exchange(part, source, target):
        place = PARTS.index(part)
        copies = []
        for d in range(1, n):
            peer = lax.rem(me + d, n)
            copy = pltpu.make_async_remote_copy(
                src_ref=source(peer),
                dst_ref=target,
                send_sem=send.at[place, d - 1],
                recv_sem=recv.at[place, d - 1],
                device_id=(peer, col),
                device_id_type=MESH,
            )
            copy.start()
            copies.append(copy)
        sent[part] = copies

    def arrived(part):
        for copy in sent[part]:
            copy.wait_recv()

    def row_block(peer):
        return pl.ds(pl.multiple_of(peer * cb, cb), cb)

    tx_prod[...] = (sk[...].astype(F32) * sv[...].astype(F32)).T.astype(BF16)
    exchange("prod", lambda peer: tx_prod.at[row_block(peer)], rx_prod.at[me])
    rx_prod[me] = tx_prod[own_rows]
    for place, gate in enumerate((sq, lk, lf)):
        tx_gates[place] = flipped(gate[...])
    exchange("gates", lambda peer: tx_gates.at[:, row_block(peer)], rx_gates.at[me])
    for place in range(3):
        rx_gates[me, place] = tx_gates[place, own_rows]
    filter_t[...] = flipped(sf[...])

    def tiles(k):
        start = pl.multiple_of(k * kt, kt)
        return pl.ds(start, kt), pl.ds(pl.multiple_of(seq + start, kt), kt)

    def halves(rows_in, depth, k):
        cos_at, sin_at = tiles(k)
        return dot(rows_in, fwd[:depth, cos_at]), dot(rows_in, fwd[:depth, sin_at])

    arrived("prod")
    for s in range(n):
        signals[0:cb, s * rows : (s + 1) * rows] = rx_prod[s]
    loads[1].wait()

    def short_step(k, carry):
        cos_at, sin_at = tiles(k)
        pc, ps = halves(signals[0:cb, :], seq, k)
        fc, fs = halves(filter_t[own_rows, :], taps, k)
        spec_prod[:, cos_at] = pc
        spec_prod[:, sin_at] = ps
        spec_sf[:, cos_at] = fc
        spec_sf[:, sin_at] = fs
        waves[0:cb, cos_at] = (pc * fc - ps * fs).astype(BF16)
        waves[0:cb, sin_at] = (pc * fs + ps * fc).astype(BF16)
        return carry

    lax.fori_loop(0, seq // kt, short_step, 0)
    loads[2].wait()

    def at_tokens(step):
        return pl.ds(pl.multiple_of(step * tile, tile), tile)

    def put(target, step, values):
        for b in range(2):
            target[step * 2 + b] = values[:, b * rows : (b + 1) * rows].astype(BF16)

    def short_back(step, carry):
        mix = dot(waves[0:cb, :], inv[:, at_tokens(step)]) * (1.0 / seq)
        smix[:, at_tokens(step)] = mix
        put(tx_smix, step, mix)
        return carry

    lax.fori_loop(0, n // 2, short_back, 0)

    loads[0].wait()
    total = jnp.zeros((chans, rows), F32)
    for d in range(m):
        if d > 0:
            og_copies[d - 1].wait_recv()
        owner = lax.rem(col + m - d, m)
        features = pl.ds(pl.multiple_of(owner * chans, chans), chans)
        block = og[...] if d == 0 else og_rx[d - 1]
        total = total + lax.dot_general(
            weight_v[:, features], block, (((1,), (1,)), ((), ())), preferred_element_type=F32
        )
    grad_out[...] = total.astype(BF16)
    tx_grad[...] = (
        total.astype(BF16).astype(F32) * lq[...].astype(F32).T
    ).astype(BF16)
    exchange("grad", lambda peer: tx_grad.at[row_block(peer)], rx_grad.at[me])
    rx_grad[me] = tx_grad[own_rows]
    exchange("smix", lambda peer: tx_smix.at[peer], smix_out.at[own_rows])
    smix_out[own_rows, :] = tx_smix[me]

    arrived("gates")
    for s in range(n):
        at = slice(s * rows, (s + 1) * rows)
        mixed = (rx_gates[s, 0].astype(F32) * smix[:, at]).astype(BF16)
        signals[0:cb, at] = (rx_gates[s, 1].astype(F32) * mixed.astype(F32)).astype(BF16)
        signals[cb : 2 * cb, at] = rx_gates[s, 2]

    def long_step(k, carry):
        cos_at, sin_at = tiles(k)
        c, s = halves(signals[0 : 2 * cb, :], seq, k)
        spec_u[:, cos_at] = c[0:cb]
        spec_u[:, sin_at] = s[0:cb]
        spec_h[:, cos_at] = c[cb:]
        spec_h[:, sin_at] = s[cb:]
        waves[0:cb, cos_at] = (c[0:cb] * c[cb:] - s[0:cb] * s[cb:]).astype(BF16)
        waves[0:cb, sin_at] = (c[0:cb] * s[cb:] + s[0:cb] * c[cb:]).astype(BF16)
        return carry

    lax.fori_loop(0, seq // kt, long_step, 0)

    arrived("grad")
    for s in range(n):
        signals[2 * cb : 3 * cb, s * rows : (s + 1) * rows] = rx_grad[s]

    def grad_step(k, carry):
        cos_at, sin_at = tiles(k)
        c, s = halves(signals[2 * cb : 3 * cb, :], seq, k)
        uc, us = spec_u[:, cos_at], spec_u[:, sin_at]
        hc, hs = spec_h[:, cos_at], spec_h[:, sin_at]
        waves[cb : 2 * cb, cos_at] = (hc * c + hs * s).astype(BF16)
        waves[cb : 2 * cb, sin_at] = (hc * s - hs * c).astype(BF16)
        waves[2 * cb : 3 * cb, cos_at] = (uc * c + us * s).astype(BF16)
        waves[2 * cb : 3 * cb, sin_at] = (uc * s - us * c).astype(BF16)
        return carry

    lax.fori_loop(0, seq // kt, grad_step, 0)

    def long_back(step, carry):
        mixes = dot(waves[...], inv[:, at_tokens(step)]) * (1.0 / seq)
        put(tx_lmix, step, mixes[0:cb])
        put(tx_back, step, mixes[cb : 2 * cb])
        put(tx_filt, step, mixes[2 * cb :] * (1.0 / math.sqrt(seq)))
        smix[:, at_tokens(step)] = mixes[cb : 2 * cb]
        return carry

    lax.fori_loop(0, n // 2, long_back, 0)
    for part, source, target in (
        ("back", tx_back, back_out), ("lmix", tx_lmix, lmix_out), ("filt", tx_filt, filt_out)
    ):
        exchange(part, lambda peer, source=source: source.at[peer], target.at[own_rows])
        target[own_rows, :] = source[me]

    for s in range(n):
        at = slice(s * rows, (s + 1) * rows)
        mixed_grad = (smix[:, at] * rx_gates[s, 1].astype(F32)).astype(BF16)
        signals[0:cb, at] = (mixed_grad.astype(F32) * rx_gates[s, 0].astype(F32)).astype(BF16)

    def gate_step(k, carry):
        cos_at, sin_at = tiles(k)
        c, s = halves(signals[0:cb, :], seq, k)
        pc, ps = spec_prod[:, cos_at], spec_prod[:, sin_at]
        fc, fs = spec_sf[:, cos_at], spec_sf[:, sin_at]
        waves[0:cb, cos_at] = (fc * c + fs * s).astype(BF16)
        waves[0:cb, sin_at] = (fc * s - fs * c).astype(BF16)
        waves[cb : 2 * cb, cos_at] = (pc * c + ps * s).astype(BF16)
        waves[cb : 2 * cb, sin_at] = (pc * s - ps * c).astype(BF16)
        return carry

    lax.fori_loop(0, seq // kt, gate_step, 0)

    def short_grad(step, carry):
        put(tx_bone, step, dot(waves[0:cb, :], inv[:, at_tokens(step)]) * (1.0 / seq))
        return carry

    lax.fori_loop(0, n // 2, short_grad, 0)
    exchange("bone", lambda peer: tx_bone.at[peer], bone_out.at[own_rows])
    bone_out[own_rows, :] = tx_bone[me]
    terms = dot(waves[cb : 2 * cb, :], inv[:, 0:taps]) * (1.0 / (seq * math.sqrt(seq)))
    tx_taps[...] = terms.astype(BF16)
    exchange("taps", lambda peer: tx_taps, taps_out.at[own_rows])
    taps_out[own_rows, :] = tx_taps[...]

    for part in PARTS[3:]:
        arrived(part)
    for part in PARTS:
        for copy in sent[part]:
            copy.wait_send()
    for copy in og_copies:
        copy.wait_send()


def finish_kernel(
    grad, smix, lmix, filt, back, bone, taps, sq, sk, sv, lk,
    sq_grad, sk_grad, sv_grad, sf_grad, lq_grad, lk_grad, lf_grad,
):
    def turned(ref):
        return ref[...].astype(F32).T

    short_mix, back_two, back_one = turned(smix), turned(back), turned(bone)
    mixed = (sq[...].astype(F32) * short_mix).astype(BF16).astype(F32)
    mixed_grad = (back_two * lk[...].astype(F32)).astype(BF16).astype(F32)
    sq_grad[...] = (mixed_grad * short_mix).astype(BF16)
    lk_grad[...] = (back_two * mixed).astype(BF16)
    sk_grad[...] = (back_one * sv[...].astype(F32)).astype(BF16)
    sv_grad[...] = (back_one * sk[...].astype(F32)).astype(BF16)
    lq_grad[...] = (turned(grad) * turned(lmix)).astype(BF16)
    lf_grad[...] = turned(filt).astype(BF16)
    sf_grad[...] = turned(taps).astype(BF16)


def dense_body(
    n, m, sq, sk, sv, sf, lq, lk, lf, weight, og
):
    rows, chans = sq.shape
    taps = sf.shape[0]
    seq = rows * n
    cb = chans // n
    forward, inverse = wave_tables(seq)
    vmem = pl.BlockSpec(memory_space=pltpu.VMEM)
    hbm = pl.BlockSpec(memory_space=pl.ANY)
    turned = jax.ShapeDtypeStruct((chans, rows), BF16)
    blocks = pltpu.VMEM((n, cb, rows), BF16)
    spectrum = pltpu.VMEM((cb, 2 * seq), F32)
    moved = pl.pallas_call(
        functools.partial(operator_kernel, n, m),
        out_shape=[turned] * 6 + [jax.ShapeDtypeStruct((chans, taps), BF16)],
        in_specs=[vmem] * 8 + [hbm] * 3,
        out_specs=[vmem] * 7,
        scratch_shapes=[
            pltpu.VMEM(weight.shape, BF16),
            pltpu.VMEM(forward.shape, BF16),
            pltpu.VMEM(inverse.shape, BF16),
            pltpu.VMEM((m - 1, rows, chans), BF16),
            pltpu.VMEM((chans, rows), BF16),
            pltpu.VMEM((3, chans, rows), BF16),
            pltpu.VMEM((chans, rows), BF16),
            blocks,
            pltpu.VMEM((n, 3, cb, rows), BF16),
            blocks,
            blocks, blocks, blocks, blocks, blocks,
            pltpu.VMEM((cb, taps), BF16),
            pltpu.VMEM((chans, taps), BF16),
            pltpu.VMEM((3 * cb, seq), BF16),
            pltpu.VMEM((cb, seq), F32),
            spectrum, spectrum, spectrum, spectrum,
            pltpu.VMEM((3 * cb, 2 * seq), BF16),
            pltpu.SemaphoreType.DMA((3,)),
            pltpu.SemaphoreType.DMA((m - 1,)),
            pltpu.SemaphoreType.DMA((m - 1,)),
            pltpu.SemaphoreType.DMA((len(PARTS), n - 1)),
            pltpu.SemaphoreType.DMA((len(PARTS), n - 1)),
        ],
        compiler_params=pltpu.CompilerParams(
            collective_id=0, has_side_effects=True, vmem_limit_bytes=40 * 1024 * 1024
        ),
    )(sq, sk, sv, sf, lq, lk, lf, og, weight, jnp.asarray(forward), jnp.asarray(inverse))
    tokens = jax.ShapeDtypeStruct((rows, chans), BF16)
    return pl.pallas_call(
        finish_kernel,
        out_shape=[tokens] * 3 + [jax.ShapeDtypeStruct((taps, chans), BF16)] + [tokens] * 3,
        in_specs=[vmem] * 11,
        out_specs=[vmem] * 7,
        compiler_params=pltpu.CompilerParams(vmem_limit_bytes=24 * 1024 * 1024),
    )(*moved, sq, sk, sv, lk)


def body(n, m, *arrays):
    rows, chans = arrays[0].shape
    taps = arrays[3].shape[0]
    dense = (
        rows * n <= LONGEST_DENSE
        and rows % 128 == 0
        and taps % 128 == 0
        and taps <= rows * n
        and n > 1
        and n % 2 == 0
        and m > 1
        and chans % (16 * n) == 0
        and chans % 128 == 0
    )
    if dense:
        return tuple(dense_body(n, m, *arrays))
    return general_body(*arrays)


def solution(mesh):
    in_specs = (
        P("ctx", "tp"),
        P("ctx", "tp"),
        P("ctx", "tp"),
        P(None, "tp"),
        P("ctx", "tp"),
        P("ctx", "tp"),
        P("ctx", "tp"),
        P("tp", None),
        P("ctx", "tp"),
    )
    out_specs = (
        P("ctx", "tp"),
        P("ctx", "tp"),
        P("ctx", "tp"),
        P(None, "tp"),
        P("ctx", "tp"),
        P("ctx", "tp"),
        P("ctx", "tp"),
    )
    return jax.shard_map(
        functools.partial(body, mesh.shape["ctx"], mesh.shape["tp"]), mesh=mesh, in_specs=in_specs, out_specs=out_specs, check_vma=False)
```

```python
import functools
import math

import jax
import jax.numpy as jnp
import ml_dtypes
import numpy as np
from jax import lax
from jax.experimental import pallas as pl
from jax.experimental.pallas import tpu as pltpu
from jax.sharding import PartitionSpec as P

MESH = pl.DeviceIdType.MESH
BF16 = jnp.bfloat16
F32 = jnp.float32
LONGEST_DENSE = 2048
VMEM_GRANT = 60 * 1024 * 1024
PARTS = ("prod", "gates", "grad", "smix", "lmix", "filt", "back", "bone", "taps")


def passed_along(block, axis, distance):
    devices = range(lax.axis_size(axis))
    route = [(i - distance, i) for i in devices if i - distance in devices]
    return lax.ppermute(block, axis, route)


def angle_tables(blocks, inner):
    size_one = 2 * blocks
    whole = size_one * inner
    first = (
        lax.broadcasted_iota(jnp.int32, (size_one, blocks), 0)
        * lax.broadcasted_iota(jnp.int32, (size_one, blocks), 1)
        % size_one
    )
    phase_one = first.astype(jnp.float32) * (2.0 * math.pi / size_one)
    twist = (
        lax.broadcasted_iota(jnp.int32, (size_one, inner), 0)
        * lax.broadcasted_iota(jnp.int32, (size_one, inner), 1)
        % whole
    )
    phase_twist = twist.astype(jnp.float32) * (2.0 * math.pi / whole)
    second = (
        lax.broadcasted_iota(jnp.int32, (inner, inner), 0)
        * lax.broadcasted_iota(jnp.int32, (inner, inner), 1)
        % inner
    )
    phase_two = second.astype(jnp.float32) * (2.0 * math.pi / inner)
    return (
        jnp.cos(phase_one),
        jnp.sin(phase_one),
        jnp.cos(phase_twist)[:, None, :],
        jnp.sin(phase_twist)[:, None, :],
        jnp.cos(phase_two),
        jnp.sin(phase_two),
        whole,
    )


def spectrum(values, tables):
    cos_one, sin_one, cos_twist, sin_twist, cos_two, sin_two, whole = tables
    highest = lax.Precision.HIGHEST
    real_a = jnp.einsum("kn,ncm->kcm", cos_one, values, precision=highest)
    imag_a = -jnp.einsum("kn,ncm->kcm", sin_one, values, precision=highest)
    real_b = real_a * cos_twist + imag_a * sin_twist
    imag_b = imag_a * cos_twist - real_a * sin_twist
    real_c = jnp.einsum("kcm,mq->kcq", real_b, cos_two, precision=highest) + jnp.einsum(
        "kcm,mq->kcq", imag_b, sin_two, precision=highest
    )
    imag_c = jnp.einsum("kcm,mq->kcq", imag_b, cos_two, precision=highest) - jnp.einsum(
        "kcm,mq->kcq", real_b, sin_two, precision=highest
    )
    return (real_c, imag_c)


def restore(real_in, imag_in, tables, both):
    cos_one, sin_one, cos_twist, sin_twist, cos_two, sin_two, whole = tables
    highest = lax.Precision.HIGHEST
    real_p = jnp.einsum("kcq,qm->kcm", real_in, cos_two, precision=highest) - jnp.einsum(
        "kcq,qm->kcm", imag_in, sin_two, precision=highest
    )
    imag_p = jnp.einsum("kcq,qm->kcm", imag_in, cos_two, precision=highest) + jnp.einsum(
        "kcq,qm->kcm", real_in, sin_two, precision=highest
    )
    real_q = real_p * cos_twist - imag_p * sin_twist
    imag_q = imag_p * cos_twist + real_p * sin_twist
    real_out = (
        jnp.einsum("kn,kcm->ncm", cos_one, real_q, precision=highest)
        - jnp.einsum("kn,kcm->ncm", sin_one, imag_q, precision=highest)
    ) / whole
    if both:
        imag_out = (
            jnp.einsum("kn,kcm->ncm", cos_one, imag_q, precision=highest)
            + jnp.einsum("kn,kcm->ncm", sin_one, real_q, precision=highest)
        ) / whole
        return (real_out, imag_out)
    return real_out


def spectral(product, gated, filter_in):
    blocks, count, inner = product.shape
    tables = angle_tables(blocks, inner)
    real_u, imag_u = spectrum(product.astype(jnp.float32), tables)
    real_g, imag_g = spectrum(gated.astype(jnp.float32), tables)
    real_h, imag_h = spectrum(filter_in.astype(jnp.float32), tables)
    real_pair = real_h * real_u - imag_h * imag_u - real_h * imag_g + imag_h * real_g
    imag_pair = real_h * imag_u + imag_h * real_u + real_h * real_g + imag_h * imag_g
    conv_part, back_part = restore(real_pair, imag_pair, tables, True)
    filter_part = restore(
        real_u * real_g + imag_u * imag_g, real_u * imag_g - imag_u * real_g, tables, False
    )
    return (conv_part, back_part, filter_part)


def tap_sum(extended, weights, token_rows, causal):
    filter_taps, channels = weights.shape

    def group_step(group, total):
        for inner in range(8):
            place = group * 8 + inner
            weight_row = lax.dynamic_index_in_dim(weights, place, 0, keepdims=False).astype(
                jnp.float32
            )
            start = filter_taps - 1 - place if causal else place
            shifted = lax.dynamic_slice_in_dim(extended, start, token_rows, 0).astype(jnp.float32)
            total = total + weight_row[None, :] * shifted
        return total

    return lax.fori_loop(
        0, filter_taps // 8, group_step, jnp.zeros((token_rows, channels), jnp.float32)
    )


def filter_terms(extended, grads, filter_taps):
    token_rows, channels = grads.shape

    def group_terms(group):
        partials = []
        for inner in range(8):
            place = group * 8 + inner
            shifted = lax.dynamic_slice_in_dim(
                extended, filter_taps - 1 - place, token_rows, 0
            ).astype(jnp.float32)
            partials.append(jnp.sum(grads * shifted, axis=0))
        return jnp.stack(partials)

    stacked = lax.map(group_terms, jnp.arange(filter_taps // 8, dtype=jnp.int32))
    return stacked.reshape(filter_taps, channels)


def general_body(
    short_query,
    short_key,
    short_value,
    short_filter,
    long_query,
    long_key,
    long_filter,
    out_weight,
    out_grad,
):
    token_rows, channels = short_query.shape
    groups = lax.axis_size("ctx")
    seq_len = token_rows * groups
    scaling = 1.0 / math.sqrt(seq_len)
    filter_taps = short_filter.shape[0]
    product_one = (short_key.astype(jnp.float32) * short_value.astype(jnp.float32)).astype(
        jnp.bfloat16
    )
    before = passed_along(product_one[token_rows - (filter_taps - 1) :], "ctx", 1)
    extended_prod = jnp.concatenate([before, product_one], axis=0)
    short_mix = tap_sum(extended_prod, short_filter, token_rows, True)
    mixed = (short_query.astype(jnp.float32) * short_mix).astype(jnp.bfloat16)
    grad_two = lax.dot_general(
        lax.all_gather(out_grad, "tp", axis=1, tiled=True),
        out_weight,
        (((1,), (1,)), ((), ())),
        preferred_element_type=jnp.float32,
    ).astype(jnp.bfloat16)

    def to_channels(values):
        return values.T.reshape(groups, channels // groups, token_rows)

    def to_tokens(values):
        return values.reshape(channels, token_rows).T

    product_two = (long_key.astype(jnp.float32) * mixed.astype(jnp.float32)).astype(jnp.bfloat16)
    gated_two = (grad_two.astype(jnp.float32) * long_query.astype(jnp.float32)).astype(jnp.bfloat16)
    conv_part, back_part, filter_part = spectral(
        lax.all_to_all(to_channels(product_two), "ctx", split_axis=0, concat_axis=0, tiled=True),
        lax.all_to_all(to_channels(gated_two), "ctx", split_axis=0, concat_axis=0, tiled=True),
        lax.all_to_all(to_channels(long_filter), "ctx", split_axis=0, concat_axis=0, tiled=True),
    )
    long_mix = lax.all_to_all(conv_part, "ctx", split_axis=0, concat_axis=0, tiled=True)
    back_two = lax.all_to_all(back_part, "ctx", split_axis=0, concat_axis=0, tiled=True)
    filter_two = lax.all_to_all(filter_part, "ctx", split_axis=0, concat_axis=0, tiled=True)
    long_mix = to_tokens(long_mix)
    back_two = to_tokens(back_two)
    filter_two = to_tokens(filter_two)
    long_query_grad = (grad_two.astype(jnp.float32) * long_mix).astype(jnp.bfloat16)
    long_key_grad = (back_two * mixed.astype(jnp.float32)).astype(jnp.bfloat16)
    mixed_grad = (back_two * long_key.astype(jnp.float32)).astype(jnp.bfloat16)
    long_filter_grad = (filter_two * scaling).astype(jnp.bfloat16)
    gated_one = (mixed_grad.astype(jnp.float32) * short_query.astype(jnp.float32)).astype(
        jnp.bfloat16
    )
    short_query_grad = (mixed_grad.astype(jnp.float32) * short_mix).astype(jnp.bfloat16)
    after = passed_along(gated_one[: filter_taps - 1], "ctx", -1)
    extended_grad = jnp.concatenate([gated_one, after], axis=0)
    back_one = tap_sum(extended_grad, short_filter, token_rows, False)
    short_key_grad = (back_one * short_value.astype(jnp.float32)).astype(jnp.bfloat16)
    short_value_grad = (back_one * short_key.astype(jnp.float32)).astype(jnp.bfloat16)
    local_terms = filter_terms(extended_prod, gated_one.astype(jnp.float32), filter_taps)
    filter_one = lax.psum(local_terms, "ctx")
    short_filter_grad = (filter_one * scaling).astype(jnp.bfloat16)
    return (
        short_query_grad,
        short_key_grad,
        short_value_grad,
        short_filter_grad,
        long_query_grad,
        long_key_grad,
        long_filter_grad,
    )


def wave_tables(seq_len):
    time = np.arange(seq_len, dtype=np.int64)[:, None]
    odd = 2 * np.arange(seq_len, dtype=np.int64)[None, :] + 1
    phase = (time * odd % (4 * seq_len)).astype(np.float64) * (math.pi / (2 * seq_len))
    forward = np.concatenate([np.cos(phase), np.sin(phase)], axis=1)
    return (
        forward.astype(ml_dtypes.bfloat16),
        np.ascontiguousarray(forward.T).astype(ml_dtypes.bfloat16),
    )


def dot(a, b):
    return jnp.dot(a, b, preferred_element_type=F32)


def flipped(block):
    return block.astype(F32).T.astype(BF16)


def operator_kernel(
    n, m,
    sq_in, sk_in, sv_in, sf_in, lq_in, lk_in, lf_in, og_in, weight, forward, inverse,
    grad_out, smix_out, lmix_out, filt_out, back_out, bone_out, taps_out,
    sq, sk, sv, lk, sf, lq, lf, og, grad, weight_v, fwd, inv, og_rx, tx_prod, tx_gates, tx_grad, rx_prod, rx_gates, rx_grad,
    tx_smix, tx_lmix, tx_filt, tx_back, tx_bone, tx_taps, filter_t, signals, smix,
    spec_prod, spec_sf, spec_u, spec_h, waves, load_sem, own_sem, og_send, og_recv, send, recv,
):
    me = lax.axis_index("ctx")
    col = lax.axis_index("tp")
    rows, chans = sq.shape
    cb = chans // n
    taps = sf.shape[0]
    seq = rows * n
    tile = 2 * rows
    kt = 256

    barrier = pltpu.get_barrier_semaphore()
    for d in range(1, n):
        pl.semaphore_signal(
            barrier, inc=1, device_id=(lax.rem(me + d, n), col), device_id_type=MESH
        )
    for d in range(1, m):
        pl.semaphore_signal(
            barrier, inc=1, device_id=(me, lax.rem(col + d, m)), device_id_type=MESH
        )

    loads = {}
    for place, (name, source, target) in enumerate((
        ("sk", sk_in, sk), ("sv", sv_in, sv), ("og", og_in, og), ("lf", lf_in, lf),
        ("lk", lk_in, lk), ("sq", sq_in, sq), ("sf", sf_in, sf), ("fwd", forward, fwd),
        ("lq", lq_in, lq), ("weight", weight, weight_v), ("inv", inverse, inv),
    )):
        loads[name] = pltpu.make_async_copy(source, target, load_sem.at[place])
        loads[name].start()

    loads["sk"].wait()
    loads["sv"].wait()
    tx_prod[...] = (sk[...].astype(F32) * sv[...].astype(F32)).T.astype(BF16)
    loads["og"].wait()
    pl.semaphore_wait(barrier, n + m - 2)

    og_copies = []
    for d in range(1, m):
        copy = pltpu.make_async_remote_copy(
            src_ref=og,
            dst_ref=og_rx.at[d - 1],
            send_sem=og_send.at[d - 1],
            recv_sem=og_recv.at[d - 1],
            device_id=(me, lax.rem(col + d, m)),
            device_id_type=MESH,
        )
        copy.start()
        og_copies.append(copy)

    own_rows = pl.ds(pl.multiple_of(me * cb, cb), cb)
    sent = {}

    def exchange(part, source, target):
        place = PARTS.index(part)
        copies = []
        for d in range(1, n):
            peer = lax.rem(me + d, n)
            copy = pltpu.make_async_remote_copy(
                src_ref=source(peer),
                dst_ref=target,
                send_sem=send.at[place, d - 1],
                recv_sem=recv.at[place, d - 1],
                device_id=(peer, col),
                device_id_type=MESH,
            )
            copy.start()
            copies.append(copy)
        sent[part] = copies

    kept = []

    def keep(source, target):
        copy = pltpu.make_async_copy(source, target, own_sem.at[len(kept)])
        copy.start()
        kept.append(copy)

    def arrived(part):
        for copy in sent[part]:
            copy.wait_recv()

    def row_block(peer):
        return pl.ds(pl.multiple_of(peer * cb, cb), cb)

    exchange("prod", lambda peer: tx_prod.at[row_block(peer)], rx_prod.at[me])
    rx_prod[me] = tx_prod[own_rows]
    loads["lf"].wait()
    tx_gates[0] = flipped(lf[...])
    loads["lk"].wait()
    loads["sq"].wait()
    tx_gates[1] = (lk[...].astype(F32) * sq[...].astype(F32)).T.astype(BF16)
    exchange("gates", lambda peer: tx_gates.at[:, row_block(peer)], rx_gates.at[me])
    for place in range(2):
        rx_gates[me, place] = tx_gates[place, own_rows]
    loads["sf"].wait()
    filter_t[...] = flipped(sf[...])

    def tiles(k):
        start = pl.multiple_of(k * kt, kt)
        return pl.ds(start, kt), pl.ds(pl.multiple_of(seq + start, kt), kt)

    def halves(rows_in, depth, k):
        cos_at, sin_at = tiles(k)
        return dot(rows_in, fwd[:depth, cos_at]), dot(rows_in, fwd[:depth, sin_at])

    arrived("prod")
    for s in range(n):
        signals[0:cb, s * rows : (s + 1) * rows] = rx_prod[s]
    loads["fwd"].wait()

    def short_step(k, carry):
        cos_at, sin_at = tiles(k)
        pc, ps = halves(signals[0:cb, :], seq, k)
        fc, fs = halves(filter_t[own_rows, :], taps, k)
        spec_prod[:, cos_at] = pc
        spec_prod[:, sin_at] = ps
        spec_sf[:, cos_at] = fc
        spec_sf[:, sin_at] = fs
        waves[0:cb, cos_at] = (pc * fc - ps * fs).astype(BF16)
        waves[0:cb, sin_at] = (pc * fs + ps * fc).astype(BF16)
        return carry

    lax.fori_loop(0, seq // kt, short_step, 0)
    loads["inv"].wait()

    def at_tokens(step):
        return pl.ds(pl.multiple_of(step * tile, tile), tile)

    def put(target, step, values):
        for b in range(2):
            target[step * 2 + b] = values[:, b * rows : (b + 1) * rows].astype(BF16)

    def short_back(step, carry):
        mix = dot(waves[0:cb, :], inv[:, at_tokens(step)]) * (1.0 / seq)
        smix[:, at_tokens(step)] = mix
        put(tx_smix, step, mix)
        return carry

    lax.fori_loop(0, n // 2, short_back, 0)

    loads["weight"].wait()
    loads["lq"].wait()
    total = jnp.zeros((chans, rows), F32)
    for d in range(m):
        if d > 0:
            og_copies[d - 1].wait_recv()
        owner = lax.rem(col + m - d, m)
        features = pl.ds(pl.multiple_of(owner * chans, chans), chans)
        block = og[...] if d == 0 else og_rx[d - 1]
        total = total + lax.dot_general(
            weight_v[:, features], block, (((1,), (1,)), ((), ())), preferred_element_type=F32
        )
    grad[...] = total.astype(BF16)
    tx_grad[...] = (grad[...].astype(F32) * lq[...].astype(F32).T).astype(BF16)
    exchange("grad", lambda peer: tx_grad.at[row_block(peer)], rx_grad.at[me])
    rx_grad[me] = tx_grad[own_rows]
    exchange("smix", lambda peer: tx_smix.at[peer], smix_out.at[own_rows])
    keep(tx_smix.at[me], smix_out.at[own_rows])
    keep(grad, grad_out)

    arrived("gates")
    for s in range(n):
        at = slice(s * rows, (s + 1) * rows)
        signals[0:cb, at] = (rx_gates[s, 1].astype(F32) * smix[:, at]).astype(BF16)
        signals[cb : 2 * cb, at] = rx_gates[s, 0]

    def long_step(k, carry):
        cos_at, sin_at = tiles(k)
        c, s = halves(signals[0 : 2 * cb, :], seq, k)
        spec_u[:, cos_at] = c[0:cb]
        spec_u[:, sin_at] = s[0:cb]
        spec_h[:, cos_at] = c[cb:]
        spec_h[:, sin_at] = s[cb:]
        waves[0:cb, cos_at] = (c[0:cb] * c[cb:] - s[0:cb] * s[cb:]).astype(BF16)
        waves[0:cb, sin_at] = (c[0:cb] * s[cb:] + s[0:cb] * c[cb:]).astype(BF16)
        return carry

    lax.fori_loop(0, seq // kt, long_step, 0)

    def mix_back(step, carry):
        put(tx_lmix, step, dot(waves[0:cb, :], inv[:, at_tokens(step)]) * (1.0 / seq))
        return carry

    lax.fori_loop(0, n // 2, mix_back, 0)
    exchange("lmix", lambda peer: tx_lmix.at[peer], lmix_out.at[own_rows])
    keep(tx_lmix.at[me], lmix_out.at[own_rows])

    arrived("grad")
    for s in range(n):
        signals[2 * cb : 3 * cb, s * rows : (s + 1) * rows] = rx_grad[s]

    def grad_step(k, carry):
        cos_at, sin_at = tiles(k)
        c, s = halves(signals[2 * cb : 3 * cb, :], seq, k)
        uc, us = spec_u[:, cos_at], spec_u[:, sin_at]
        hc, hs = spec_h[:, cos_at], spec_h[:, sin_at]
        waves[cb : 2 * cb, cos_at] = (hc * c + hs * s).astype(BF16)
        waves[cb : 2 * cb, sin_at] = (hc * s - hs * c).astype(BF16)
        waves[2 * cb : 3 * cb, cos_at] = (uc * c + us * s).astype(BF16)
        waves[2 * cb : 3 * cb, sin_at] = (uc * s - us * c).astype(BF16)
        return carry

    lax.fori_loop(0, seq // kt, grad_step, 0)

    def long_back(step, carry):
        mixes = dot(waves[cb:, :], inv[:, at_tokens(step)]) * (1.0 / seq)
        put(tx_back, step, mixes[0:cb])
        put(tx_filt, step, mixes[cb:] * (1.0 / math.sqrt(seq)))
        smix[:, at_tokens(step)] = mixes[0:cb]
        return carry

    lax.fori_loop(0, n // 2, long_back, 0)
    for part, source, target in (
        ("back", tx_back, back_out), ("filt", tx_filt, filt_out)
    ):
        exchange(part, lambda peer, source=source: source.at[peer], target.at[own_rows])
        keep(source.at[me], target.at[own_rows])

    for s in range(n):
        at = slice(s * rows, (s + 1) * rows)
        signals[0:cb, at] = (smix[:, at] * rx_gates[s, 1].astype(F32)).astype(BF16)

    def gate_step(k, carry):
        cos_at, sin_at = tiles(k)
        c, s = halves(signals[0:cb, :], seq, k)
        pc, ps = spec_prod[:, cos_at], spec_prod[:, sin_at]
        fc, fs = spec_sf[:, cos_at], spec_sf[:, sin_at]
        waves[0:cb, cos_at] = (fc * c + fs * s).astype(BF16)
        waves[0:cb, sin_at] = (fc * s - fs * c).astype(BF16)
        waves[cb : 2 * cb, cos_at] = (pc * c + ps * s).astype(BF16)
        waves[cb : 2 * cb, sin_at] = (pc * s - ps * c).astype(BF16)
        return carry

    lax.fori_loop(0, seq // kt, gate_step, 0)

    def short_grad(step, carry):
        put(tx_bone, step, dot(waves[0:cb, :], inv[:, at_tokens(step)]) * (1.0 / seq))
        return carry

    lax.fori_loop(0, n // 2, short_grad, 0)
    exchange("bone", lambda peer: tx_bone.at[peer], bone_out.at[own_rows])
    keep(tx_bone.at[me], bone_out.at[own_rows])
    terms = dot(waves[cb : 2 * cb, :], inv[:, 0:taps]) * (1.0 / (seq * math.sqrt(seq)))
    tx_taps[...] = terms.astype(BF16)
    exchange("taps", lambda peer: tx_taps, taps_out.at[own_rows])
    keep(tx_taps, taps_out.at[own_rows])

    for part in PARTS[3:]:
        arrived(part)
    for part in PARTS:
        for copy in sent[part]:
            copy.wait_send()
    for copy in og_copies:
        copy.wait_send()
    for copy in kept:
        copy.wait()


def finish_kernel(*refs):
    sources, targets = refs[:11], refs[11:18]
    held, results = refs[18:29], refs[29:36]
    load_sem, store_sem = refs[36:]
    loads = []
    for place in range(11):
        load = pltpu.make_async_copy(sources[place], held[place], load_sem.at[place])
        load.start()
        loads.append(load)
    stores = []

    def read(place):
        loads[place].wait()
        return held[place][...].astype(F32)

    def write(place, values):
        results[place][...] = values.astype(BF16)
        store = pltpu.make_async_copy(results[place], targets[place], store_sem.at[place])
        store.start()
        stores.append(store)

    short_mix, back_two = read(0).T, read(1).T
    mixed = (read(2) * short_mix).astype(BF16).astype(F32)
    write(5, back_two * mixed)
    mixed_grad = (back_two * read(3)).astype(BF16).astype(F32)
    write(0, mixed_grad * short_mix)
    back_one = read(4).T
    write(1, back_one * read(5))
    write(2, back_one * read(6))
    write(4, read(7).T * read(8).T)
    write(6, read(9).T)
    write(3, read(10).T)
    for store in stores:
        store.wait()


def dense_body(
    n, m, sq, sk, sv, sf, lq, lk, lf, weight, og
):
    rows, chans = sq.shape
    taps = sf.shape[0]
    seq = rows * n
    cb = chans // n
    forward, inverse = wave_tables(seq)
    hbm = pl.BlockSpec(memory_space=pltpu.HBM)
    tokens = jax.ShapeDtypeStruct((rows, chans), BF16)
    turned = jax.ShapeDtypeStruct((chans, rows), BF16)
    blocks = pltpu.VMEM((n, cb, rows), BF16)
    spectrum = pltpu.VMEM((cb, 2 * seq), F32)
    grad, smix, lmix, filt, back, bone, taps_grad = pl.pallas_call(
        functools.partial(operator_kernel, n, m),
        out_shape=[turned] * 6 + [jax.ShapeDtypeStruct((chans, taps), BF16)],
        in_specs=[hbm] * 11,
        out_specs=[hbm] * 7,
        scratch_shapes=[
            pltpu.VMEM((rows, chans), BF16),
            pltpu.VMEM((rows, chans), BF16),
            pltpu.VMEM((rows, chans), BF16),
            pltpu.VMEM((rows, chans), BF16),
            pltpu.VMEM((taps, chans), BF16),
            pltpu.VMEM((rows, chans), BF16),
            pltpu.VMEM((rows, chans), BF16),
            pltpu.VMEM((rows, chans), BF16),
            pltpu.VMEM((chans, rows), BF16),
            pltpu.VMEM(weight.shape, BF16),
            pltpu.VMEM(forward.shape, BF16),
            pltpu.VMEM(inverse.shape, BF16),
            pltpu.VMEM((m - 1, rows, chans), BF16),
            pltpu.VMEM((chans, rows), BF16),
            pltpu.VMEM((2, chans, rows), BF16),
            pltpu.VMEM((chans, rows), BF16),
            blocks,
            pltpu.VMEM((n, 2, cb, rows), BF16),
            blocks,
            blocks, blocks, blocks, blocks, blocks,
            pltpu.VMEM((cb, taps), BF16),
            pltpu.VMEM((chans, taps), BF16),
            pltpu.VMEM((3 * cb, seq), BF16),
            pltpu.VMEM((cb, seq), F32),
            spectrum, spectrum, spectrum, spectrum,
            pltpu.VMEM((3 * cb, 2 * seq), BF16),
            pltpu.SemaphoreType.DMA((11,)),
            pltpu.SemaphoreType.DMA((7,)),
            pltpu.SemaphoreType.DMA((m - 1,)),
            pltpu.SemaphoreType.DMA((m - 1,)),
            pltpu.SemaphoreType.DMA((len(PARTS), n - 1)),
            pltpu.SemaphoreType.DMA((len(PARTS), n - 1)),
        ],
        compiler_params=pltpu.CompilerParams(
            collective_id=0, has_side_effects=True, vmem_limit_bytes=VMEM_GRANT
        ),
    )(sq, sk, sv, sf, lq, lk, lf, og, weight, jnp.asarray(forward), jnp.asarray(inverse))
    operands = (smix, back, sq, lk, bone, sv, sk, grad, lmix, filt, taps_grad)
    results = [tokens] * 3 + [jax.ShapeDtypeStruct((taps, chans), BF16)] + [tokens] * 3
    return pl.pallas_call(
        finish_kernel,
        out_shape=results,
        in_specs=[hbm] * 11,
        out_specs=[hbm] * 7,
        scratch_shapes=[
            *(pltpu.VMEM(a.shape, BF16) for a in operands),
            *(pltpu.VMEM(a.shape, BF16) for a in results),
            pltpu.SemaphoreType.DMA((11,)),
            pltpu.SemaphoreType.DMA((7,)),
        ],
        compiler_params=pltpu.CompilerParams(vmem_limit_bytes=VMEM_GRANT),
    )(*operands)


def body(n, m, *arrays):
    rows, chans = arrays[0].shape
    taps = arrays[3].shape[0]
    dense = (
        rows * n <= LONGEST_DENSE
        and rows % 128 == 0
        and taps % 128 == 0
        and taps <= rows * n
        and n > 1
        and n % 2 == 0
        and m > 1
        and chans % (16 * n) == 0
        and chans % 128 == 0
    )
    if dense:
        return tuple(dense_body(n, m, *arrays))
    return general_body(*arrays)


def solution(mesh):
    in_specs = (
        P("ctx", "tp"),
        P("ctx", "tp"),
        P("ctx", "tp"),
        P(None, "tp"),
        P("ctx", "tp"),
        P("ctx", "tp"),
        P("ctx", "tp"),
        P("tp", None),
        P("ctx", "tp"),
    )
    out_specs = (
        P("ctx", "tp"),
        P("ctx", "tp"),
        P("ctx", "tp"),
        P(None, "tp"),
        P("ctx", "tp"),
        P("ctx", "tp"),
        P("ctx", "tp"),
    )
    return jax.shard_map(
        functools.partial(body, mesh.shape["ctx"], mesh.shape["tp"]), mesh=mesh, in_specs=in_specs, out_specs=out_specs, check_vma=False)
```

```python
import functools
import math

import jax
import jax.numpy as jnp
import ml_dtypes
import numpy as np
from jax import lax
from jax.experimental import pallas as pl
from jax.experimental.pallas import tpu as pltpu
from jax.sharding import PartitionSpec as P

MESH = pl.DeviceIdType.MESH
BF16 = jnp.bfloat16
F32 = jnp.float32
LONGEST_DENSE = 2048
VMEM_GRANT = 60 * 1024 * 1024
PARTS = ("prod", "gates", "grad", "smix", "lmix", "filt", "back", "bone")


def passed_along(block, axis, distance):
    devices = range(lax.axis_size(axis))
    route = [(i - distance, i) for i in devices if i - distance in devices]
    return lax.ppermute(block, axis, route)


def angle_tables(blocks, inner):
    size_one = 2 * blocks
    whole = size_one * inner
    first = (
        lax.broadcasted_iota(jnp.int32, (size_one, blocks), 0)
        * lax.broadcasted_iota(jnp.int32, (size_one, blocks), 1)
        % size_one
    )
    phase_one = first.astype(jnp.float32) * (2.0 * math.pi / size_one)
    twist = (
        lax.broadcasted_iota(jnp.int32, (size_one, inner), 0)
        * lax.broadcasted_iota(jnp.int32, (size_one, inner), 1)
        % whole
    )
    phase_twist = twist.astype(jnp.float32) * (2.0 * math.pi / whole)
    second = (
        lax.broadcasted_iota(jnp.int32, (inner, inner), 0)
        * lax.broadcasted_iota(jnp.int32, (inner, inner), 1)
        % inner
    )
    phase_two = second.astype(jnp.float32) * (2.0 * math.pi / inner)
    return (
        jnp.cos(phase_one),
        jnp.sin(phase_one),
        jnp.cos(phase_twist)[:, None, :],
        jnp.sin(phase_twist)[:, None, :],
        jnp.cos(phase_two),
        jnp.sin(phase_two),
        whole,
    )


def spectrum(values, tables):
    cos_one, sin_one, cos_twist, sin_twist, cos_two, sin_two, whole = tables
    highest = lax.Precision.HIGHEST
    real_a = jnp.einsum("kn,ncm->kcm", cos_one, values, precision=highest)
    imag_a = -jnp.einsum("kn,ncm->kcm", sin_one, values, precision=highest)
    real_b = real_a * cos_twist + imag_a * sin_twist
    imag_b = imag_a * cos_twist - real_a * sin_twist
    real_c = jnp.einsum("kcm,mq->kcq", real_b, cos_two, precision=highest) + jnp.einsum(
        "kcm,mq->kcq", imag_b, sin_two, precision=highest
    )
    imag_c = jnp.einsum("kcm,mq->kcq", imag_b, cos_two, precision=highest) - jnp.einsum(
        "kcm,mq->kcq", real_b, sin_two, precision=highest
    )
    return (real_c, imag_c)


def restore(real_in, imag_in, tables, both):
    cos_one, sin_one, cos_twist, sin_twist, cos_two, sin_two, whole = tables
    highest = lax.Precision.HIGHEST
    real_p = jnp.einsum("kcq,qm->kcm", real_in, cos_two, precision=highest) - jnp.einsum(
        "kcq,qm->kcm", imag_in, sin_two, precision=highest
    )
    imag_p = jnp.einsum("kcq,qm->kcm", imag_in, cos_two, precision=highest) + jnp.einsum(
        "kcq,qm->kcm", real_in, sin_two, precision=highest
    )
    real_q = real_p * cos_twist - imag_p * sin_twist
    imag_q = imag_p * cos_twist + real_p * sin_twist
    real_out = (
        jnp.einsum("kn,kcm->ncm", cos_one, real_q, precision=highest)
        - jnp.einsum("kn,kcm->ncm", sin_one, imag_q, precision=highest)
    ) / whole
    if both:
        imag_out = (
            jnp.einsum("kn,kcm->ncm", cos_one, imag_q, precision=highest)
            + jnp.einsum("kn,kcm->ncm", sin_one, real_q, precision=highest)
        ) / whole
        return (real_out, imag_out)
    return real_out


def spectral(product, gated, filter_in):
    blocks, count, inner = product.shape
    tables = angle_tables(blocks, inner)
    real_u, imag_u = spectrum(product.astype(jnp.float32), tables)
    real_g, imag_g = spectrum(gated.astype(jnp.float32), tables)
    real_h, imag_h = spectrum(filter_in.astype(jnp.float32), tables)
    real_pair = real_h * real_u - imag_h * imag_u - real_h * imag_g + imag_h * real_g
    imag_pair = real_h * imag_u + imag_h * real_u + real_h * real_g + imag_h * imag_g
    conv_part, back_part = restore(real_pair, imag_pair, tables, True)
    filter_part = restore(
        real_u * real_g + imag_u * imag_g, real_u * imag_g - imag_u * real_g, tables, False
    )
    return (conv_part, back_part, filter_part)


def tap_sum(extended, weights, token_rows, causal):
    filter_taps, channels = weights.shape

    def group_step(group, total):
        for inner in range(8):
            place = group * 8 + inner
            weight_row = lax.dynamic_index_in_dim(weights, place, 0, keepdims=False).astype(
                jnp.float32
            )
            start = filter_taps - 1 - place if causal else place
            shifted = lax.dynamic_slice_in_dim(extended, start, token_rows, 0).astype(jnp.float32)
            total = total + weight_row[None, :] * shifted
        return total

    return lax.fori_loop(
        0, filter_taps // 8, group_step, jnp.zeros((token_rows, channels), jnp.float32)
    )


def filter_terms(extended, grads, filter_taps):
    token_rows, channels = grads.shape

    def group_terms(group):
        partials = []
        for inner in range(8):
            place = group * 8 + inner
            shifted = lax.dynamic_slice_in_dim(
                extended, filter_taps - 1 - place, token_rows, 0
            ).astype(jnp.float32)
            partials.append(jnp.sum(grads * shifted, axis=0))
        return jnp.stack(partials)

    stacked = lax.map(group_terms, jnp.arange(filter_taps // 8, dtype=jnp.int32))
    return stacked.reshape(filter_taps, channels)


def general_body(
    short_query,
    short_key,
    short_value,
    short_filter,
    long_query,
    long_key,
    long_filter,
    out_weight,
    out_grad,
):
    token_rows, channels = short_query.shape
    groups = lax.axis_size("ctx")
    seq_len = token_rows * groups
    scaling = 1.0 / math.sqrt(seq_len)
    filter_taps = short_filter.shape[0]
    product_one = (short_key.astype(jnp.float32) * short_value.astype(jnp.float32)).astype(
        jnp.bfloat16
    )
    before = passed_along(product_one[token_rows - (filter_taps - 1) :], "ctx", 1)
    extended_prod = jnp.concatenate([before, product_one], axis=0)
    short_mix = tap_sum(extended_prod, short_filter, token_rows, True)
    mixed = (short_query.astype(jnp.float32) * short_mix).astype(jnp.bfloat16)
    grad_two = lax.dot_general(
        lax.all_gather(out_grad, "tp", axis=1, tiled=True),
        out_weight,
        (((1,), (1,)), ((), ())),
        preferred_element_type=jnp.float32,
    ).astype(jnp.bfloat16)

    def to_channels(values):
        return values.T.reshape(groups, channels // groups, token_rows)

    def to_tokens(values):
        return values.reshape(channels, token_rows).T

    product_two = (long_key.astype(jnp.float32) * mixed.astype(jnp.float32)).astype(jnp.bfloat16)
    gated_two = (grad_two.astype(jnp.float32) * long_query.astype(jnp.float32)).astype(jnp.bfloat16)
    conv_part, back_part, filter_part = spectral(
        lax.all_to_all(to_channels(product_two), "ctx", split_axis=0, concat_axis=0, tiled=True),
        lax.all_to_all(to_channels(gated_two), "ctx", split_axis=0, concat_axis=0, tiled=True),
        lax.all_to_all(to_channels(long_filter), "ctx", split_axis=0, concat_axis=0, tiled=True),
    )
    long_mix = lax.all_to_all(conv_part, "ctx", split_axis=0, concat_axis=0, tiled=True)
    back_two = lax.all_to_all(back_part, "ctx", split_axis=0, concat_axis=0, tiled=True)
    filter_two = lax.all_to_all(filter_part, "ctx", split_axis=0, concat_axis=0, tiled=True)
    long_mix = to_tokens(long_mix)
    back_two = to_tokens(back_two)
    filter_two = to_tokens(filter_two)
    long_query_grad = (grad_two.astype(jnp.float32) * long_mix).astype(jnp.bfloat16)
    long_key_grad = (back_two * mixed.astype(jnp.float32)).astype(jnp.bfloat16)
    mixed_grad = (back_two * long_key.astype(jnp.float32)).astype(jnp.bfloat16)
    long_filter_grad = (filter_two * scaling).astype(jnp.bfloat16)
    gated_one = (mixed_grad.astype(jnp.float32) * short_query.astype(jnp.float32)).astype(
        jnp.bfloat16
    )
    short_query_grad = (mixed_grad.astype(jnp.float32) * short_mix).astype(jnp.bfloat16)
    after = passed_along(gated_one[: filter_taps - 1], "ctx", -1)
    extended_grad = jnp.concatenate([gated_one, after], axis=0)
    back_one = tap_sum(extended_grad, short_filter, token_rows, False)
    short_key_grad = (back_one * short_value.astype(jnp.float32)).astype(jnp.bfloat16)
    short_value_grad = (back_one * short_key.astype(jnp.float32)).astype(jnp.bfloat16)
    local_terms = filter_terms(extended_prod, gated_one.astype(jnp.float32), filter_taps)
    filter_one = lax.psum(local_terms, "ctx")
    short_filter_grad = (filter_one * scaling).astype(jnp.bfloat16)
    return (
        short_query_grad,
        short_key_grad,
        short_value_grad,
        short_filter_grad,
        long_query_grad,
        long_key_grad,
        long_filter_grad,
    )


def wave_tables(seq_len):
    time = np.arange(seq_len, dtype=np.int64)[:, None]
    odd = 2 * np.arange(seq_len, dtype=np.int64)[None, :] + 1
    phase = (time * odd % (4 * seq_len)).astype(np.float64) * (math.pi / (2 * seq_len))
    forward = np.concatenate([np.cos(phase), np.sin(phase)], axis=1)
    return (
        forward.astype(ml_dtypes.bfloat16),
        np.ascontiguousarray(forward.T).astype(ml_dtypes.bfloat16),
    )


def dot(a, b):
    return jnp.dot(a, b, preferred_element_type=F32)


def flipped(block):
    return block.astype(F32).T.astype(BF16)


def operator_kernel(
    n, m,
    sq_in, sk_in, sv_in, sf_in, lq_in, lk_in, lf_in, og_in, weight, forward, inverse,
    sq_grad, lq_grad, lk_grad, lf_grad, bone_out, taps_out,
    smix_rx, lmix_rx, filt_rx, back_rx, taps_rx, results, sq, sk, sv, lk, sf, lq, lf, og, grad, weight_v, fwd, inv, og_rx, tx_prod, tx_gates, tx_grad, rx_prod, rx_gates, rx_grad,
    tx_smix, tx_lmix, tx_filt, tx_back, tx_bone, tx_taps, filter_t, signals, smix,
    spec_prod, spec_sf, spec_u, spec_h, waves, load_sem, own_sem, og_send, og_recv, taps_send, taps_recv,
    send, recv,
):
    me = lax.axis_index("ctx")
    col = lax.axis_index("tp")
    rows, chans = sq.shape
    cb = chans // n
    taps = sf.shape[0]
    seq = rows * n
    tile = 2 * rows
    kt = 256

    barrier = pltpu.get_barrier_semaphore()
    for d in range(1, n):
        pl.semaphore_signal(
            barrier, inc=1, device_id=(lax.rem(me + d, n), col), device_id_type=MESH
        )
    for d in range(1, m):
        pl.semaphore_signal(
            barrier, inc=1, device_id=(me, lax.rem(col + d, m)), device_id_type=MESH
        )

    loads = {}
    for place, (name, source, target) in enumerate((
        ("sk", sk_in, sk), ("sv", sv_in, sv), ("og", og_in, og), ("lf", lf_in, lf),
        ("lk", lk_in, lk), ("sq", sq_in, sq), ("sf", sf_in, sf), ("fwd", forward, fwd),
        ("lq", lq_in, lq), ("weight", weight, weight_v), ("inv", inverse, inv),
    )):
        loads[name] = pltpu.make_async_copy(source, target, load_sem.at[place])
        loads[name].start()

    loads["sk"].wait()
    loads["sv"].wait()
    tx_prod[...] = (sk[...].astype(F32) * sv[...].astype(F32)).T.astype(BF16)
    loads["og"].wait()
    pl.semaphore_wait(barrier, n + m - 2)

    og_copies = []
    for d in range(1, m):
        copy = pltpu.make_async_remote_copy(
            src_ref=og,
            dst_ref=og_rx.at[d - 1],
            send_sem=og_send.at[d - 1],
            recv_sem=og_recv.at[d - 1],
            device_id=(me, lax.rem(col + d, m)),
            device_id_type=MESH,
        )
        copy.start()
        og_copies.append(copy)

    own_rows = pl.ds(pl.multiple_of(me * cb, cb), cb)
    sent = {}

    def exchange(part, source, target):
        place = PARTS.index(part)
        copies = []
        for d in range(1, n):
            peer = lax.rem(me + d, n)
            copy = pltpu.make_async_remote_copy(
                src_ref=source(peer),
                dst_ref=target,
                send_sem=send.at[place, d - 1],
                recv_sem=recv.at[place, d - 1],
                device_id=(peer, col),
                device_id_type=MESH,
            )
            copy.start()
            copies.append(copy)
        sent[part] = copies

    kept = []

    def keep(source, target):
        copy = pltpu.make_async_copy(source, target, own_sem.at[len(kept)])
        copy.start()
        kept.append(copy)

    def arrived(part):
        for copy in sent[part]:
            copy.wait_recv()

    def row_block(peer):
        return pl.ds(pl.multiple_of(peer * cb, cb), cb)

    exchange("prod", lambda peer: tx_prod.at[row_block(peer)], rx_prod.at[me])
    rx_prod[me] = tx_prod[own_rows]
    loads["lf"].wait()
    tx_gates[0] = flipped(lf[...])
    loads["lk"].wait()
    loads["sq"].wait()
    tx_gates[1] = (lk[...].astype(F32) * sq[...].astype(F32)).T.astype(BF16)
    exchange("gates", lambda peer: tx_gates.at[:, row_block(peer)], rx_gates.at[me])
    for place in range(2):
        rx_gates[me, place] = tx_gates[place, own_rows]
    loads["sf"].wait()
    filter_t[...] = flipped(sf[...])

    def tiles(k):
        start = pl.multiple_of(k * kt, kt)
        return pl.ds(start, kt), pl.ds(pl.multiple_of(seq + start, kt), kt)

    def halves(rows_in, depth, k):
        cos_at, sin_at = tiles(k)
        return dot(rows_in, fwd[:depth, cos_at]), dot(rows_in, fwd[:depth, sin_at])

    arrived("prod")
    for s in range(n):
        signals[0:cb, s * rows : (s + 1) * rows] = rx_prod[s]
    loads["fwd"].wait()

    def short_step(k, carry):
        cos_at, sin_at = tiles(k)
        pc, ps = halves(signals[0:cb, :], seq, k)
        fc, fs = halves(filter_t[own_rows, :], taps, k)
        spec_prod[:, cos_at] = pc
        spec_prod[:, sin_at] = ps
        spec_sf[:, cos_at] = fc
        spec_sf[:, sin_at] = fs
        waves[0:cb, cos_at] = (pc * fc - ps * fs).astype(BF16)
        waves[0:cb, sin_at] = (pc * fs + ps * fc).astype(BF16)
        return carry

    lax.fori_loop(0, seq // kt, short_step, 0)
    loads["inv"].wait()

    def at_tokens(step):
        return pl.ds(pl.multiple_of(step * tile, tile), tile)

    def put(target, step, values):
        for b in range(2):
            target[step * 2 + b] = values[:, b * rows : (b + 1) * rows].astype(BF16)

    def short_back(step, carry):
        mix = dot(waves[0:cb, :], inv[:, at_tokens(step)]) * (1.0 / seq)
        smix[:, at_tokens(step)] = mix
        put(tx_smix, step, mix)
        return carry

    lax.fori_loop(0, n // 2, short_back, 0)

    loads["weight"].wait()
    loads["lq"].wait()
    total = jnp.zeros((chans, rows), F32)
    for d in range(m):
        if d > 0:
            og_copies[d - 1].wait_recv()
        owner = lax.rem(col + m - d, m)
        features = pl.ds(pl.multiple_of(owner * chans, chans), chans)
        block = og[...] if d == 0 else og_rx[d - 1]
        total = total + lax.dot_general(
            weight_v[:, features], block, (((1,), (1,)), ((), ())), preferred_element_type=F32
        )
    grad[...] = total.astype(BF16)
    tx_grad[...] = (grad[...].astype(F32) * lq[...].astype(F32).T).astype(BF16)
    exchange("grad", lambda peer: tx_grad.at[row_block(peer)], rx_grad.at[me])
    rx_grad[me] = tx_grad[own_rows]
    exchange("smix", lambda peer: tx_smix.at[peer], smix_rx.at[own_rows])
    smix_rx[own_rows, :] = tx_smix[me]

    arrived("gates")
    for s in range(n):
        at = slice(s * rows, (s + 1) * rows)
        signals[0:cb, at] = (rx_gates[s, 1].astype(F32) * smix[:, at]).astype(BF16)
        signals[cb : 2 * cb, at] = rx_gates[s, 0]

    def long_step(k, carry):
        cos_at, sin_at = tiles(k)
        c, s = halves(signals[0 : 2 * cb, :], seq, k)
        spec_u[:, cos_at] = c[0:cb]
        spec_u[:, sin_at] = s[0:cb]
        spec_h[:, cos_at] = c[cb:]
        spec_h[:, sin_at] = s[cb:]
        waves[0:cb, cos_at] = (c[0:cb] * c[cb:] - s[0:cb] * s[cb:]).astype(BF16)
        waves[0:cb, sin_at] = (c[0:cb] * s[cb:] + s[0:cb] * c[cb:]).astype(BF16)
        return carry

    lax.fori_loop(0, seq // kt, long_step, 0)

    def mix_back(step, carry):
        put(tx_lmix, step, dot(waves[0:cb, :], inv[:, at_tokens(step)]) * (1.0 / seq))
        return carry

    lax.fori_loop(0, n // 2, mix_back, 0)
    exchange("lmix", lambda peer: tx_lmix.at[peer], lmix_rx.at[own_rows])
    lmix_rx[own_rows, :] = tx_lmix[me]

    arrived("grad")
    for s in range(n):
        signals[2 * cb : 3 * cb, s * rows : (s + 1) * rows] = rx_grad[s]

    def grad_step(k, carry):
        cos_at, sin_at = tiles(k)
        c, s = halves(signals[2 * cb : 3 * cb, :], seq, k)
        uc, us = spec_u[:, cos_at], spec_u[:, sin_at]
        hc, hs = spec_h[:, cos_at], spec_h[:, sin_at]
        waves[cb : 2 * cb, cos_at] = (hc * c + hs * s).astype(BF16)
        waves[cb : 2 * cb, sin_at] = (hc * s - hs * c).astype(BF16)
        waves[2 * cb : 3 * cb, cos_at] = (uc * c + us * s).astype(BF16)
        waves[2 * cb : 3 * cb, sin_at] = (uc * s - us * c).astype(BF16)
        return carry

    lax.fori_loop(0, seq // kt, grad_step, 0)

    def long_back(step, carry):
        mixes = dot(waves[cb:, :], inv[:, at_tokens(step)]) * (1.0 / seq)
        put(tx_back, step, mixes[0:cb])
        put(tx_filt, step, mixes[cb:] * (1.0 / math.sqrt(seq)))
        smix[:, at_tokens(step)] = mixes[0:cb]
        return carry

    lax.fori_loop(0, n // 2, long_back, 0)
    for part, source, target in (
        ("back", tx_back, back_rx), ("filt", tx_filt, filt_rx)
    ):
        exchange(part, lambda peer, source=source: source.at[peer], target.at[own_rows])
        target[own_rows, :] = source[me]

    for s in range(n):
        at = slice(s * rows, (s + 1) * rows)
        signals[0:cb, at] = (smix[:, at] * rx_gates[s, 1].astype(F32)).astype(BF16)

    def gate_step(k, carry):
        cos_at, sin_at = tiles(k)
        c, s = halves(signals[0:cb, :], seq, k)
        pc, ps = spec_prod[:, cos_at], spec_prod[:, sin_at]
        fc, fs = spec_sf[:, cos_at], spec_sf[:, sin_at]
        waves[0:cb, cos_at] = (fc * c + fs * s).astype(BF16)
        waves[0:cb, sin_at] = (fc * s - fs * c).astype(BF16)
        waves[cb : 2 * cb, cos_at] = (pc * c + ps * s).astype(BF16)
        waves[cb : 2 * cb, sin_at] = (pc * s - ps * c).astype(BF16)
        return carry

    lax.fori_loop(0, seq // kt, gate_step, 0)

    terms = dot(waves[cb : 2 * cb, :], inv[:, 0:taps]) * (1.0 / (seq * math.sqrt(seq)))
    tx_taps[...] = terms.astype(BF16)
    taps_rx[own_rows, :] = tx_taps[...]
    pair = me + 1 - 2 * lax.rem(me, 2)

    def taps_copy(place, source, target_rows, peer):
        copy = pltpu.make_async_remote_copy(
            src_ref=source,
            dst_ref=taps_rx.at[target_rows],
            send_sem=taps_send.at[place],
            recv_sem=taps_recv.at[place],
            device_id=(peer, col),
            device_id_type=MESH,
        )
        copy.start()
        return copy

    far = [
        taps_copy(d - 1, tx_taps, own_rows, lax.rem(me + 2 * d, n)) for d in range(1, n // 2)
    ]
    near = [taps_copy(n // 2 - 1, tx_taps, own_rows, pair)]

    def short_grad(step, carry):
        put(tx_bone, step, dot(waves[0:cb, :], inv[:, at_tokens(step)]) * (1.0 / seq))
        return carry

    lax.fori_loop(0, n // 2, short_grad, 0)
    exchange("bone", lambda peer: tx_bone.at[peer], bone_out.at[own_rows])
    keep(tx_bone.at[me], bone_out.at[own_rows])

    def finish(place, target, values):
        results[place] = values.T.astype(BF16)
        keep(results.at[place], target)

    arrived("smix")
    arrived("lmix")
    finish(0, lq_grad, grad[...].astype(F32) * lmix_rx[...].astype(F32))
    arrived("back")
    back = back_rx[...].astype(F32).T
    mix = smix_rx[...].astype(F32).T
    mixed = (sq[...].astype(F32) * mix).astype(BF16).astype(F32)
    results[1] = (back * mixed).astype(BF16)
    keep(results.at[1], lk_grad)
    mixed_grad = (back * lk[...].astype(F32)).astype(BF16).astype(F32)
    results[2] = (mixed_grad * mix).astype(BF16)
    keep(results.at[2], sq_grad)
    arrived("filt")
    finish(3, lf_grad, filt_rx[...].astype(F32))

    for d in range(1, n // 2):
        far[d - 1].wait_recv()
        source = row_block(lax.rem(me + n - 2 * d, n))
        near.append(taps_copy(n // 2 - 1 + d, taps_rx.at[source], source, pair))
    for copy in near:
        copy.wait_recv()
    keep(taps_rx, taps_out)

    arrived("bone")
    for part in PARTS:
        for copy in sent[part]:
            copy.wait_send()
    for copy in og_copies + far + near:
        copy.wait_send()
    for copy in kept:
        copy.wait()


def finish_kernel(
    sq_done, lq_done, lk_done, lf_done, bone, taps, sk, sv,
    sq_grad, sk_grad, sv_grad, sf_grad, lq_grad, lk_grad, lf_grad,
    bone_v, taps_v, sk_v, sv_v, sk_out, sv_out, sf_out, move_sem,
):
    def move(place, source, target):
        copy = pltpu.make_async_copy(source, target, move_sem.at[place])
        copy.start()
        return copy

    loads = [
        move(place, source, target)
        for place, (source, target) in enumerate(
            ((bone, bone_v), (sv, sv_v), (sk, sk_v), (taps, taps_v))
        )
    ]
    moves = [
        move(4 + place, source, target)
        for place, (source, target) in enumerate(
            ((sq_done, sq_grad), (lq_done, lq_grad), (lk_done, lk_grad), (lf_done, lf_grad))
        )
    ]
    loads[0].wait()
    back_one = bone_v[...].astype(F32).T
    loads[1].wait()
    sk_out[...] = (back_one * sv_v[...].astype(F32)).astype(BF16)
    moves.append(move(8, sk_out, sk_grad))
    loads[2].wait()
    sv_out[...] = (back_one * sk_v[...].astype(F32)).astype(BF16)
    moves.append(move(9, sv_out, sv_grad))
    loads[3].wait()
    sf_out[...] = flipped(taps_v[...])
    moves.append(move(10, sf_out, sf_grad))
    for copy in moves:
        copy.wait()


def dense_body(
    n, m, sq, sk, sv, sf, lq, lk, lf, weight, og
):
    rows, chans = sq.shape
    taps = sf.shape[0]
    seq = rows * n
    cb = chans // n
    forward, inverse = wave_tables(seq)
    hbm = pl.BlockSpec(memory_space=pltpu.HBM)
    tokens = jax.ShapeDtypeStruct((rows, chans), BF16)
    turned = jax.ShapeDtypeStruct((chans, rows), BF16)
    blocks = pltpu.VMEM((n, cb, rows), BF16)
    spectrum = pltpu.VMEM((cb, 2 * seq), F32)
    sent_on = pl.pallas_call(
        functools.partial(operator_kernel, n, m),
        out_shape=[tokens] * 4 + [turned, jax.ShapeDtypeStruct((chans, taps), BF16)],
        in_specs=[hbm] * 11,
        out_specs=[hbm] * 6,
        scratch_shapes=[
            pltpu.VMEM((chans, rows), BF16),
            pltpu.VMEM((chans, rows), BF16),
            pltpu.VMEM((chans, rows), BF16),
            pltpu.VMEM((chans, rows), BF16),
            pltpu.VMEM((chans, taps), BF16),
            pltpu.VMEM((4, rows, chans), BF16),
            pltpu.VMEM((rows, chans), BF16),
            pltpu.VMEM((rows, chans), BF16),
            pltpu.VMEM((rows, chans), BF16),
            pltpu.VMEM((rows, chans), BF16),
            pltpu.VMEM((taps, chans), BF16),
            pltpu.VMEM((rows, chans), BF16),
            pltpu.VMEM((rows, chans), BF16),
            pltpu.VMEM((rows, chans), BF16),
            pltpu.VMEM((chans, rows), BF16),
            pltpu.VMEM(weight.shape, BF16),
            pltpu.VMEM(forward.shape, BF16),
            pltpu.VMEM(inverse.shape, BF16),
            pltpu.VMEM((m - 1, rows, chans), BF16),
            pltpu.VMEM((chans, rows), BF16),
            pltpu.VMEM((2, chans, rows), BF16),
            pltpu.VMEM((chans, rows), BF16),
            blocks,
            pltpu.VMEM((n, 2, cb, rows), BF16),
            blocks,
            blocks, blocks, blocks, blocks, blocks,
            pltpu.VMEM((cb, taps), BF16),
            pltpu.VMEM((chans, taps), BF16),
            pltpu.VMEM((3 * cb, seq), BF16),
            pltpu.VMEM((cb, seq), F32),
            spectrum, spectrum, spectrum, spectrum,
            pltpu.VMEM((3 * cb, 2 * seq), BF16),
            pltpu.SemaphoreType.DMA((11,)),
            pltpu.SemaphoreType.DMA((6,)),
            pltpu.SemaphoreType.DMA((m - 1,)),
            pltpu.SemaphoreType.DMA((m - 1,)),
            pltpu.SemaphoreType.DMA((n - 1,)),
            pltpu.SemaphoreType.DMA((n - 1,)),
            pltpu.SemaphoreType.DMA((len(PARTS), n - 1)),
            pltpu.SemaphoreType.DMA((len(PARTS), n - 1)),
        ],
        compiler_params=pltpu.CompilerParams(
            collective_id=0, has_side_effects=True, vmem_limit_bytes=VMEM_GRANT
        ),
    )(sq, sk, sv, sf, lq, lk, lf, og, weight, jnp.asarray(forward), jnp.asarray(inverse))
    short = jax.ShapeDtypeStruct((taps, chans), BF16)
    return pl.pallas_call(
        finish_kernel,
        out_shape=[tokens] * 3 + [short] + [tokens] * 3,
        in_specs=[hbm] * 8,
        out_specs=[hbm] * 7,
        scratch_shapes=[
            pltpu.VMEM((chans, rows), BF16),
            pltpu.VMEM((chans, taps), BF16),
            pltpu.VMEM((rows, chans), BF16),
            pltpu.VMEM((rows, chans), BF16),
            pltpu.VMEM((rows, chans), BF16),
            pltpu.VMEM((rows, chans), BF16),
            pltpu.VMEM((taps, chans), BF16),
            pltpu.SemaphoreType.DMA((11,)),
        ],
        compiler_params=pltpu.CompilerParams(vmem_limit_bytes=VMEM_GRANT),
    )(*sent_on, sk, sv)


def body(n, m, *arrays):
    rows, chans = arrays[0].shape
    taps = arrays[3].shape[0]
    dense = (
        rows * n <= LONGEST_DENSE
        and rows % 128 == 0
        and taps % 128 == 0
        and taps <= rows * n
        and n > 1
        and n % 2 == 0
        and m > 1
        and chans % (16 * n) == 0
        and chans % 128 == 0
    )
    if dense:
        return tuple(dense_body(n, m, *arrays))
    return general_body(*arrays)


def solution(mesh):
    in_specs = (
        P("ctx", "tp"),
        P("ctx", "tp"),
        P("ctx", "tp"),
        P(None, "tp"),
        P("ctx", "tp"),
        P("ctx", "tp"),
        P("ctx", "tp"),
        P("tp", None),
        P("ctx", "tp"),
    )
    out_specs = (
        P("ctx", "tp"),
        P("ctx", "tp"),
        P("ctx", "tp"),
        P(None, "tp"),
        P("ctx", "tp"),
        P("ctx", "tp"),
        P("ctx", "tp"),
    )
    return jax.shard_map(
        functools.partial(body, mesh.shape["ctx"], mesh.shape["tp"]), mesh=mesh, in_specs=in_specs, out_specs=out_specs, check_vma=False)
```

```python
import functools
import math

import jax
import jax.numpy as jnp
import ml_dtypes
import numpy as np
from jax import lax
from jax.experimental import pallas as pl
from jax.experimental.pallas import tpu as pltpu
from jax.sharding import PartitionSpec as P

MESH = pl.DeviceIdType.MESH
BF16 = jnp.bfloat16
F32 = jnp.float32
LONGEST_DENSE = 2048
VMEM_GRANT = 60 * 1024 * 1024
PARTS = ("prod", "gates", "grad", "smix", "lmix", "filt", "back", "bone")


def passed_along(block, axis, distance):
    devices = range(lax.axis_size(axis))
    route = [(i - distance, i) for i in devices if i - distance in devices]
    return lax.ppermute(block, axis, route)


def angle_tables(blocks, inner):
    size_one = 2 * blocks
    whole = size_one * inner
    first = (
        lax.broadcasted_iota(jnp.int32, (size_one, blocks), 0)
        * lax.broadcasted_iota(jnp.int32, (size_one, blocks), 1)
        % size_one
    )
    phase_one = first.astype(jnp.float32) * (2.0 * math.pi / size_one)
    twist = (
        lax.broadcasted_iota(jnp.int32, (size_one, inner), 0)
        * lax.broadcasted_iota(jnp.int32, (size_one, inner), 1)
        % whole
    )
    phase_twist = twist.astype(jnp.float32) * (2.0 * math.pi / whole)
    second = (
        lax.broadcasted_iota(jnp.int32, (inner, inner), 0)
        * lax.broadcasted_iota(jnp.int32, (inner, inner), 1)
        % inner
    )
    phase_two = second.astype(jnp.float32) * (2.0 * math.pi / inner)
    return (
        jnp.cos(phase_one),
        jnp.sin(phase_one),
        jnp.cos(phase_twist)[:, None, :],
        jnp.sin(phase_twist)[:, None, :],
        jnp.cos(phase_two),
        jnp.sin(phase_two),
        whole,
    )


def spectrum(values, tables):
    cos_one, sin_one, cos_twist, sin_twist, cos_two, sin_two, whole = tables
    highest = lax.Precision.HIGHEST
    real_a = jnp.einsum("kn,ncm->kcm", cos_one, values, precision=highest)
    imag_a = -jnp.einsum("kn,ncm->kcm", sin_one, values, precision=highest)
    real_b = real_a * cos_twist + imag_a * sin_twist
    imag_b = imag_a * cos_twist - real_a * sin_twist
    real_c = jnp.einsum("kcm,mq->kcq", real_b, cos_two, precision=highest) + jnp.einsum(
        "kcm,mq->kcq", imag_b, sin_two, precision=highest
    )
    imag_c = jnp.einsum("kcm,mq->kcq", imag_b, cos_two, precision=highest) - jnp.einsum(
        "kcm,mq->kcq", real_b, sin_two, precision=highest
    )
    return (real_c, imag_c)


def restore(real_in, imag_in, tables, both):
    cos_one, sin_one, cos_twist, sin_twist, cos_two, sin_two, whole = tables
    highest = lax.Precision.HIGHEST
    real_p = jnp.einsum("kcq,qm->kcm", real_in, cos_two, precision=highest) - jnp.einsum(
        "kcq,qm->kcm", imag_in, sin_two, precision=highest
    )
    imag_p = jnp.einsum("kcq,qm->kcm", imag_in, cos_two, precision=highest) + jnp.einsum(
        "kcq,qm->kcm", real_in, sin_two, precision=highest
    )
    real_q = real_p * cos_twist - imag_p * sin_twist
    imag_q = imag_p * cos_twist + real_p * sin_twist
    real_out = (
        jnp.einsum("kn,kcm->ncm", cos_one, real_q, precision=highest)
        - jnp.einsum("kn,kcm->ncm", sin_one, imag_q, precision=highest)
    ) / whole
    if both:
        imag_out = (
            jnp.einsum("kn,kcm->ncm", cos_one, imag_q, precision=highest)
            + jnp.einsum("kn,kcm->ncm", sin_one, real_q, precision=highest)
        ) / whole
        return (real_out, imag_out)
    return real_out


def spectral(product, gated, filter_in):
    blocks, count, inner = product.shape
    tables = angle_tables(blocks, inner)
    real_u, imag_u = spectrum(product.astype(jnp.float32), tables)
    real_g, imag_g = spectrum(gated.astype(jnp.float32), tables)
    real_h, imag_h = spectrum(filter_in.astype(jnp.float32), tables)
    real_pair = real_h * real_u - imag_h * imag_u - real_h * imag_g + imag_h * real_g
    imag_pair = real_h * imag_u + imag_h * real_u + real_h * real_g + imag_h * imag_g
    conv_part, back_part = restore(real_pair, imag_pair, tables, True)
    filter_part = restore(
        real_u * real_g + imag_u * imag_g, real_u * imag_g - imag_u * real_g, tables, False
    )
    return (conv_part, back_part, filter_part)


def tap_sum(extended, weights, token_rows, causal):
    filter_taps, channels = weights.shape

    def group_step(group, total):
        for inner in range(8):
            place = group * 8 + inner
            weight_row = lax.dynamic_index_in_dim(weights, place, 0, keepdims=False).astype(
                jnp.float32
            )
            start = filter_taps - 1 - place if causal else place
            shifted = lax.dynamic_slice_in_dim(extended, start, token_rows, 0).astype(jnp.float32)
            total = total + weight_row[None, :] * shifted
        return total

    return lax.fori_loop(
        0, filter_taps // 8, group_step, jnp.zeros((token_rows, channels), jnp.float32)
    )


def filter_terms(extended, grads, filter_taps):
    token_rows, channels = grads.shape

    def group_terms(group):
        partials = []
        for inner in range(8):
            place = group * 8 + inner
            shifted = lax.dynamic_slice_in_dim(
                extended, filter_taps - 1 - place, token_rows, 0
            ).astype(jnp.float32)
            partials.append(jnp.sum(grads * shifted, axis=0))
        return jnp.stack(partials)

    stacked = lax.map(group_terms, jnp.arange(filter_taps // 8, dtype=jnp.int32))
    return stacked.reshape(filter_taps, channels)


def general_body(
    short_query,
    short_key,
    short_value,
    short_filter,
    long_query,
    long_key,
    long_filter,
    out_weight,
    out_grad,
):
    token_rows, channels = short_query.shape
    groups = lax.axis_size("ctx")
    seq_len = token_rows * groups
    scaling = 1.0 / math.sqrt(seq_len)
    filter_taps = short_filter.shape[0]
    product_one = (short_key.astype(jnp.float32) * short_value.astype(jnp.float32)).astype(
        jnp.bfloat16
    )
    before = passed_along(product_one[token_rows - (filter_taps - 1) :], "ctx", 1)
    extended_prod = jnp.concatenate([before, product_one], axis=0)
    short_mix = tap_sum(extended_prod, short_filter, token_rows, True)
    mixed = (short_query.astype(jnp.float32) * short_mix).astype(jnp.bfloat16)
    grad_two = lax.dot_general(
        lax.all_gather(out_grad, "tp", axis=1, tiled=True),
        out_weight,
        (((1,), (1,)), ((), ())),
        preferred_element_type=jnp.float32,
    ).astype(jnp.bfloat16)

    def to_channels(values):
        return values.T.reshape(groups, channels // groups, token_rows)

    def to_tokens(values):
        return values.reshape(channels, token_rows).T

    product_two = (long_key.astype(jnp.float32) * mixed.astype(jnp.float32)).astype(jnp.bfloat16)
    gated_two = (grad_two.astype(jnp.float32) * long_query.astype(jnp.float32)).astype(jnp.bfloat16)
    conv_part, back_part, filter_part = spectral(
        lax.all_to_all(to_channels(product_two), "ctx", split_axis=0, concat_axis=0, tiled=True),
        lax.all_to_all(to_channels(gated_two), "ctx", split_axis=0, concat_axis=0, tiled=True),
        lax.all_to_all(to_channels(long_filter), "ctx", split_axis=0, concat_axis=0, tiled=True),
    )
    long_mix = lax.all_to_all(conv_part, "ctx", split_axis=0, concat_axis=0, tiled=True)
    back_two = lax.all_to_all(back_part, "ctx", split_axis=0, concat_axis=0, tiled=True)
    filter_two = lax.all_to_all(filter_part, "ctx", split_axis=0, concat_axis=0, tiled=True)
    long_mix = to_tokens(long_mix)
    back_two = to_tokens(back_two)
    filter_two = to_tokens(filter_two)
    long_query_grad = (grad_two.astype(jnp.float32) * long_mix).astype(jnp.bfloat16)
    long_key_grad = (back_two * mixed.astype(jnp.float32)).astype(jnp.bfloat16)
    mixed_grad = (back_two * long_key.astype(jnp.float32)).astype(jnp.bfloat16)
    long_filter_grad = (filter_two * scaling).astype(jnp.bfloat16)
    gated_one = (mixed_grad.astype(jnp.float32) * short_query.astype(jnp.float32)).astype(
        jnp.bfloat16
    )
    short_query_grad = (mixed_grad.astype(jnp.float32) * short_mix).astype(jnp.bfloat16)
    after = passed_along(gated_one[: filter_taps - 1], "ctx", -1)
    extended_grad = jnp.concatenate([gated_one, after], axis=0)
    back_one = tap_sum(extended_grad, short_filter, token_rows, False)
    short_key_grad = (back_one * short_value.astype(jnp.float32)).astype(jnp.bfloat16)
    short_value_grad = (back_one * short_key.astype(jnp.float32)).astype(jnp.bfloat16)
    local_terms = filter_terms(extended_prod, gated_one.astype(jnp.float32), filter_taps)
    filter_one = lax.psum(local_terms, "ctx")
    short_filter_grad = (filter_one * scaling).astype(jnp.bfloat16)
    return (
        short_query_grad,
        short_key_grad,
        short_value_grad,
        short_filter_grad,
        long_query_grad,
        long_key_grad,
        long_filter_grad,
    )


def wave_tables(seq_len):
    time = np.arange(seq_len, dtype=np.int64)[:, None]
    odd = 2 * np.arange(seq_len, dtype=np.int64)[None, :] + 1
    phase = (time * odd % (4 * seq_len)).astype(np.float64) * (math.pi / (2 * seq_len))
    forward = np.concatenate([np.cos(phase), np.sin(phase)], axis=1)
    return (
        forward.astype(ml_dtypes.bfloat16),
        np.ascontiguousarray(forward.T).astype(ml_dtypes.bfloat16),
    )


def dot(a, b):
    return jnp.dot(a, b, preferred_element_type=F32)


def flipped(block):
    return block.astype(F32).T.astype(BF16)


def operator_kernel(
    n, m,
    sq_in, sk_in, sv_in, sf_in, lq_in, lk_in, lf_in, og_in, weight, forward, inverse,
    sq_grad, lq_grad, lk_grad, lf_grad, bone_out, taps_out,
    smix_rx, lmix_rx, filt_rx, back_rx, taps_rx, results, sq, sk, sv, lk, sf, lq, lf, og, grad, weight_v, fwd, inv, og_rx, tx_prod, tx_gates, tx_grad, rx_prod, rx_gates, rx_grad,
    tx_smix, tx_lmix, tx_filt, tx_back, tx_bone, tx_taps, filter_t, signals, smix,
    spec_prod, spec_sf, spec_u, spec_h, waves, load_sem, own_sem, og_send, og_recv, taps_send, taps_recv,
    send, recv,
):
    me = lax.axis_index("ctx")
    col = lax.axis_index("tp")
    rows, chans = sq.shape
    cb = chans // n
    taps = sf.shape[0]
    seq = rows * n
    tile = 2 * rows
    kt = 256

    barrier = pltpu.get_barrier_semaphore()
    for d in range(1, n):
        pl.semaphore_signal(
            barrier, inc=1, device_id=(lax.rem(me + d, n), col), device_id_type=MESH
        )
    for d in range(1, m):
        pl.semaphore_signal(
            barrier, inc=1, device_id=(me, lax.rem(col + d, m)), device_id_type=MESH
        )

    loads = {}
    for place, (name, source, target) in enumerate((
        ("sk", sk_in, sk), ("sv", sv_in, sv), ("og", og_in, og), ("lf", lf_in, lf),
        ("lk", lk_in, lk), ("sq", sq_in, sq), ("sf", sf_in, sf), ("fwd", forward, fwd),
        ("lq", lq_in, lq), ("weight", weight, weight_v), ("inv", inverse, inv),
    )):
        loads[name] = pltpu.make_async_copy(source, target, load_sem.at[place])
        loads[name].start()

    loads["sk"].wait()
    loads["sv"].wait()
    tx_prod[...] = (sk[...].astype(F32) * sv[...].astype(F32)).T.astype(BF16)
    loads["og"].wait()
    pl.semaphore_wait(barrier, n + m - 2)

    col_pair = col + 1 - 2 * lax.rem(col, 2)

    def og_copy(slot, source, peer):
        copy = pltpu.make_async_remote_copy(
            src_ref=source,
            dst_ref=og_rx.at[slot],
            send_sem=og_send.at[slot],
            recv_sem=og_recv.at[slot],
            device_id=(me, peer),
            device_id_type=MESH,
        )
        copy.start()
        return copy

    og_far = [og_copy(d, og, lax.rem(col + 2 * d, m)) for d in range(1, m // 2)]
    og_near = [og_copy(0, og, col_pair)]

    own_rows = pl.ds(pl.multiple_of(me * cb, cb), cb)
    sent = {}

    def exchange(part, source, target):
        place = PARTS.index(part)
        copies = []
        for d in range(1, n):
            peer = lax.rem(me + d, n)
            copy = pltpu.make_async_remote_copy(
                src_ref=source(peer),
                dst_ref=target,
                send_sem=send.at[place, d - 1],
                recv_sem=recv.at[place, d - 1],
                device_id=(peer, col),
                device_id_type=MESH,
            )
            copy.start()
            copies.append(copy)
        sent[part] = copies

    kept = []

    def keep(source, target):
        copy = pltpu.make_async_copy(source, target, own_sem.at[len(kept)])
        copy.start()
        kept.append(copy)

    def arrived(part):
        for copy in sent[part]:
            copy.wait_recv()

    def row_block(peer):
        return pl.ds(pl.multiple_of(peer * cb, cb), cb)

    exchange("prod", lambda peer: tx_prod.at[row_block(peer)], rx_prod.at[me])
    rx_prod[me] = tx_prod[own_rows]
    loads["lf"].wait()
    tx_gates[0] = flipped(lf[...])
    loads["lk"].wait()
    loads["sq"].wait()
    tx_gates[1] = (lk[...].astype(F32) * sq[...].astype(F32)).T.astype(BF16)
    exchange("gates", lambda peer: tx_gates.at[:, row_block(peer)], rx_gates.at[me])
    for place in range(2):
        rx_gates[me, place] = tx_gates[place, own_rows]
    loads["sf"].wait()
    filter_t[...] = flipped(sf[...])

    def tiles(k):
        start = pl.multiple_of(k * kt, kt)
        return pl.ds(start, kt), pl.ds(pl.multiple_of(seq + start, kt), kt)

    def halves(rows_in, depth, k):
        cos_at, sin_at = tiles(k)
        return dot(rows_in, fwd[:depth, cos_at]), dot(rows_in, fwd[:depth, sin_at])

    for d in range(1, m // 2):
        og_far[d - 1].wait_recv()
        og_near.append(og_copy(m // 2 - 1 + d, og_rx.at[d], col_pair))

    arrived("prod")
    for s in range(n):
        signals[0:cb, s * rows : (s + 1) * rows] = rx_prod[s]
    loads["fwd"].wait()

    def short_step(k, carry):
        cos_at, sin_at = tiles(k)
        pc, ps = halves(signals[0:cb, :], seq, k)
        fc, fs = halves(filter_t[own_rows, :], taps, k)
        spec_prod[:, cos_at] = pc
        spec_prod[:, sin_at] = ps
        spec_sf[:, cos_at] = fc
        spec_sf[:, sin_at] = fs
        waves[0:cb, cos_at] = (pc * fc - ps * fs).astype(BF16)
        waves[0:cb, sin_at] = (pc * fs + ps * fc).astype(BF16)
        return carry

    lax.fori_loop(0, seq // kt, short_step, 0, unroll=True)
    loads["inv"].wait()

    def at_tokens(step):
        return pl.ds(pl.multiple_of(step * tile, tile), tile)

    def put(target, step, values):
        for b in range(2):
            target[step * 2 + b] = values[:, b * rows : (b + 1) * rows].astype(BF16)

    def short_back(step, carry):
        mix = dot(waves[0:cb, :], inv[:, at_tokens(step)]) * (1.0 / seq)
        smix[:, at_tokens(step)] = mix
        put(tx_smix, step, mix)
        return carry

    lax.fori_loop(0, n // 2, short_back, 0, unroll=True)

    loads["weight"].wait()
    loads["lq"].wait()
    def projected(owner, block):
        features = pl.ds(pl.multiple_of(owner * chans, chans), chans)
        return lax.dot_general(
            weight_v[:, features], block, (((1,), (1,)), ((), ())), preferred_element_type=F32
        )

    total = projected(col, og[...])
    for d in range(1, m // 2):
        total = total + projected(lax.rem(col + m - 2 * d, m), og_rx[d])
    for place, copy in enumerate(og_near):
        copy.wait_recv()
        owner = lax.rem(col_pair + m - 2 * place, m)
        total = total + projected(owner, og_rx[0 if place == 0 else m // 2 - 1 + place])
    grad[...] = total.astype(BF16)
    tx_grad[...] = (grad[...].astype(F32) * lq[...].astype(F32).T).astype(BF16)
    exchange("grad", lambda peer: tx_grad.at[row_block(peer)], rx_grad.at[me])
    rx_grad[me] = tx_grad[own_rows]
    exchange("smix", lambda peer: tx_smix.at[peer], smix_rx.at[own_rows])
    smix_rx[own_rows, :] = tx_smix[me]

    arrived("gates")
    for s in range(n):
        at = slice(s * rows, (s + 1) * rows)
        signals[0:cb, at] = (rx_gates[s, 1].astype(F32) * smix[:, at]).astype(BF16)
        signals[cb : 2 * cb, at] = rx_gates[s, 0]

    def long_step(k, carry):
        cos_at, sin_at = tiles(k)
        c, s = halves(signals[0 : 2 * cb, :], seq, k)
        spec_u[:, cos_at] = c[0:cb]
        spec_u[:, sin_at] = s[0:cb]
        spec_h[:, cos_at] = c[cb:]
        spec_h[:, sin_at] = s[cb:]
        waves[0:cb, cos_at] = (c[0:cb] * c[cb:] - s[0:cb] * s[cb:]).astype(BF16)
        waves[0:cb, sin_at] = (c[0:cb] * s[cb:] + s[0:cb] * c[cb:]).astype(BF16)
        return carry

    lax.fori_loop(0, seq // kt, long_step, 0, unroll=True)

    def mix_back(step, carry):
        put(tx_lmix, step, dot(waves[0:cb, :], inv[:, at_tokens(step)]) * (1.0 / seq))
        return carry

    lax.fori_loop(0, n // 2, mix_back, 0, unroll=True)
    exchange("lmix", lambda peer: tx_lmix.at[peer], lmix_rx.at[own_rows])
    lmix_rx[own_rows, :] = tx_lmix[me]

    arrived("grad")
    for s in range(n):
        signals[2 * cb : 3 * cb, s * rows : (s + 1) * rows] = rx_grad[s]

    def grad_step(k, carry):
        cos_at, sin_at = tiles(k)
        c, s = halves(signals[2 * cb : 3 * cb, :], seq, k)
        uc, us = spec_u[:, cos_at], spec_u[:, sin_at]
        hc, hs = spec_h[:, cos_at], spec_h[:, sin_at]
        waves[cb : 2 * cb, cos_at] = (hc * c + hs * s).astype(BF16)
        waves[cb : 2 * cb, sin_at] = (hc * s - hs * c).astype(BF16)
        waves[2 * cb : 3 * cb, cos_at] = (uc * c + us * s).astype(BF16)
        waves[2 * cb : 3 * cb, sin_at] = (uc * s - us * c).astype(BF16)
        return carry

    lax.fori_loop(0, seq // kt, grad_step, 0, unroll=True)

    def long_back(step, carry):
        mixes = dot(waves[cb:, :], inv[:, at_tokens(step)]) * (1.0 / seq)
        put(tx_back, step, mixes[0:cb])
        put(tx_filt, step, mixes[cb:] * (1.0 / math.sqrt(seq)))
        smix[:, at_tokens(step)] = mixes[0:cb]
        return carry

    lax.fori_loop(0, n // 2, long_back, 0, unroll=True)
    for part, source, target in (
        ("back", tx_back, back_rx), ("filt", tx_filt, filt_rx)
    ):
        exchange(part, lambda peer, source=source: source.at[peer], target.at[own_rows])
        target[own_rows, :] = source[me]

    for s in range(n):
        at = slice(s * rows, (s + 1) * rows)
        signals[0:cb, at] = (smix[:, at] * rx_gates[s, 1].astype(F32)).astype(BF16)

    def gate_step(k, carry):
        cos_at, sin_at = tiles(k)
        c, s = halves(signals[0:cb, :], seq, k)
        pc, ps = spec_prod[:, cos_at], spec_prod[:, sin_at]
        fc, fs = spec_sf[:, cos_at], spec_sf[:, sin_at]
        waves[0:cb, cos_at] = (fc * c + fs * s).astype(BF16)
        waves[0:cb, sin_at] = (fc * s - fs * c).astype(BF16)
        waves[cb : 2 * cb, cos_at] = (pc * c + ps * s).astype(BF16)
        waves[cb : 2 * cb, sin_at] = (pc * s - ps * c).astype(BF16)
        return carry

    lax.fori_loop(0, seq // kt, gate_step, 0, unroll=True)

    terms = dot(waves[cb : 2 * cb, :], inv[:, 0:taps]) * (1.0 / (seq * math.sqrt(seq)))
    tx_taps[...] = terms.astype(BF16)
    taps_rx[own_rows, :] = tx_taps[...]
    pair = me + 1 - 2 * lax.rem(me, 2)

    def taps_copy(place, source, target_rows, peer):
        copy = pltpu.make_async_remote_copy(
            src_ref=source,
            dst_ref=taps_rx.at[target_rows],
            send_sem=taps_send.at[place],
            recv_sem=taps_recv.at[place],
            device_id=(peer, col),
            device_id_type=MESH,
        )
        copy.start()
        return copy

    far = [
        taps_copy(d - 1, tx_taps, own_rows, lax.rem(me + 2 * d, n)) for d in range(1, n // 2)
    ]
    near = [taps_copy(n // 2 - 1, tx_taps, own_rows, pair)]

    def short_grad(step, carry):
        put(tx_bone, step, dot(waves[0:cb, :], inv[:, at_tokens(step)]) * (1.0 / seq))
        return carry

    lax.fori_loop(0, n // 2, short_grad, 0, unroll=True)
    exchange("bone", lambda peer: tx_bone.at[peer], bone_out.at[own_rows])
    keep(tx_bone.at[me], bone_out.at[own_rows])

    def finish(place, target, values):
        results[place] = values.T.astype(BF16)
        keep(results.at[place], target)

    arrived("smix")
    arrived("lmix")
    finish(0, lq_grad, grad[...].astype(F32) * lmix_rx[...].astype(F32))
    arrived("back")
    back = back_rx[...].astype(F32).T
    mix = smix_rx[...].astype(F32).T
    mixed = (sq[...].astype(F32) * mix).astype(BF16).astype(F32)
    results[1] = (back * mixed).astype(BF16)
    keep(results.at[1], lk_grad)
    mixed_grad = (back * lk[...].astype(F32)).astype(BF16).astype(F32)
    results[2] = (mixed_grad * mix).astype(BF16)
    keep(results.at[2], sq_grad)
    arrived("filt")
    finish(3, lf_grad, filt_rx[...].astype(F32))

    for d in range(1, n // 2):
        far[d - 1].wait_recv()
        source = row_block(lax.rem(me + n - 2 * d, n))
        near.append(taps_copy(n // 2 - 1 + d, taps_rx.at[source], source, pair))
    for copy in near:
        copy.wait_recv()
    keep(taps_rx, taps_out)

    arrived("bone")
    for part in PARTS:
        for copy in sent[part]:
            copy.wait_send()
    for copy in og_far + og_near + far + near:
        copy.wait_send()
    for copy in kept:
        copy.wait()


def finish_kernel(
    sq_done, lq_done, lk_done, lf_done, bone, taps, sk, sv,
    sq_grad, sk_grad, sv_grad, sf_grad, lq_grad, lk_grad, lf_grad,
    bone_v, taps_v, sk_v, sv_v, sk_out, sv_out, sf_out, done_v, move_sem,
):
    def move(place, source, target):
        copy = pltpu.make_async_copy(source, target, move_sem.at[place])
        copy.start()
        return copy

    loads = [
        move(place, source, target)
        for place, (source, target) in enumerate(
            ((bone, bone_v), (sv, sv_v), (sk, sk_v), (taps, taps_v))
        )
    ]
    done = [
        move(4 + place, source, done_v.at[place])
        for place, source in enumerate((sq_done, lq_done, lk_done, lf_done))
    ]
    moves = []
    for place, target in enumerate((sq_grad, lq_grad, lk_grad, lf_grad)):
        done[place].wait()
        moves.append(move(11 + place, done_v.at[place], target))
    loads[0].wait()
    back_one = bone_v[...].astype(F32).T
    loads[1].wait()
    sk_out[...] = (back_one * sv_v[...].astype(F32)).astype(BF16)
    moves.append(move(8, sk_out, sk_grad))
    loads[2].wait()
    sv_out[...] = (back_one * sk_v[...].astype(F32)).astype(BF16)
    moves.append(move(9, sv_out, sv_grad))
    loads[3].wait()
    sf_out[...] = flipped(taps_v[...])
    moves.append(move(10, sf_out, sf_grad))
    for copy in moves:
        copy.wait()


def dense_body(
    n, m, sq, sk, sv, sf, lq, lk, lf, weight, og
):
    rows, chans = sq.shape
    taps = sf.shape[0]
    seq = rows * n
    cb = chans // n
    forward, inverse = wave_tables(seq)
    hbm = pl.BlockSpec(memory_space=pltpu.HBM)
    tokens = jax.ShapeDtypeStruct((rows, chans), BF16)
    turned = jax.ShapeDtypeStruct((chans, rows), BF16)
    blocks = pltpu.VMEM((n, cb, rows), BF16)
    spectrum = pltpu.VMEM((cb, 2 * seq), F32)
    sent_on = pl.pallas_call(
        functools.partial(operator_kernel, n, m),
        out_shape=[tokens] * 4 + [turned, jax.ShapeDtypeStruct((chans, taps), BF16)],
        in_specs=[hbm] * 11,
        out_specs=[hbm] * 6,
        scratch_shapes=[
            pltpu.VMEM((chans, rows), BF16),
            pltpu.VMEM((chans, rows), BF16),
            pltpu.VMEM((chans, rows), BF16),
            pltpu.VMEM((chans, rows), BF16),
            pltpu.VMEM((chans, taps), BF16),
            pltpu.VMEM((4, rows, chans), BF16),
            pltpu.VMEM((rows, chans), BF16),
            pltpu.VMEM((rows, chans), BF16),
            pltpu.VMEM((rows, chans), BF16),
            pltpu.VMEM((rows, chans), BF16),
            pltpu.VMEM((taps, chans), BF16),
            pltpu.VMEM((rows, chans), BF16),
            pltpu.VMEM((rows, chans), BF16),
            pltpu.VMEM((rows, chans), BF16),
            pltpu.VMEM((chans, rows), BF16),
            pltpu.VMEM(weight.shape, BF16),
            pltpu.VMEM(forward.shape, BF16),
            pltpu.VMEM(inverse.shape, BF16),
            pltpu.VMEM((m - 1, rows, chans), BF16),
            pltpu.VMEM((chans, rows), BF16),
            pltpu.VMEM((2, chans, rows), BF16),
            pltpu.VMEM((chans, rows), BF16),
            blocks,
            pltpu.VMEM((n, 2, cb, rows), BF16),
            blocks,
            blocks, blocks, blocks, blocks, blocks,
            pltpu.VMEM((cb, taps), BF16),
            pltpu.VMEM((chans, taps), BF16),
            pltpu.VMEM((3 * cb, seq), BF16),
            pltpu.VMEM((cb, seq), F32),
            spectrum, spectrum, spectrum, spectrum,
            pltpu.VMEM((3 * cb, 2 * seq), BF16),
            pltpu.SemaphoreType.DMA((11,)),
            pltpu.SemaphoreType.DMA((6,)),
            pltpu.SemaphoreType.DMA((m - 1,)),
            pltpu.SemaphoreType.DMA((m - 1,)),
            pltpu.SemaphoreType.DMA((n - 1,)),
            pltpu.SemaphoreType.DMA((n - 1,)),
            pltpu.SemaphoreType.DMA((len(PARTS), n - 1)),
            pltpu.SemaphoreType.DMA((len(PARTS), n - 1)),
        ],
        compiler_params=pltpu.CompilerParams(
            collective_id=0, has_side_effects=True, vmem_limit_bytes=VMEM_GRANT
        ),
    )(sq, sk, sv, sf, lq, lk, lf, og, weight, jnp.asarray(forward), jnp.asarray(inverse))
    short = jax.ShapeDtypeStruct((taps, chans), BF16)
    return pl.pallas_call(
        finish_kernel,
        out_shape=[tokens] * 3 + [short] + [tokens] * 3,
        in_specs=[hbm] * 8,
        out_specs=[hbm] * 7,
        scratch_shapes=[
            pltpu.VMEM((chans, rows), BF16),
            pltpu.VMEM((chans, taps), BF16),
            pltpu.VMEM((rows, chans), BF16),
            pltpu.VMEM((rows, chans), BF16),
            pltpu.VMEM((rows, chans), BF16),
            pltpu.VMEM((rows, chans), BF16),
            pltpu.VMEM((taps, chans), BF16),
            pltpu.VMEM((4, rows, chans), BF16),
            pltpu.SemaphoreType.DMA((15,)),
        ],
        compiler_params=pltpu.CompilerParams(vmem_limit_bytes=VMEM_GRANT),
    )(*sent_on, sk, sv)


def body(n, m, *arrays):
    rows, chans = arrays[0].shape
    taps = arrays[3].shape[0]
    dense = (
        rows * n <= LONGEST_DENSE
        and rows % 128 == 0
        and taps % 128 == 0
        and taps <= rows * n
        and n > 1
        and n % 2 == 0
        and m > 1
        and m % 2 == 0
        and chans % (16 * n) == 0
        and chans % 128 == 0
    )
    if dense:
        return tuple(dense_body(n, m, *arrays))
    return general_body(*arrays)


def solution(mesh):
    in_specs = (
        P("ctx", "tp"),
        P("ctx", "tp"),
        P("ctx", "tp"),
        P(None, "tp"),
        P("ctx", "tp"),
        P("ctx", "tp"),
        P("ctx", "tp"),
        P("tp", None),
        P("ctx", "tp"),
    )
    out_specs = (
        P("ctx", "tp"),
        P("ctx", "tp"),
        P("ctx", "tp"),
        P(None, "tp"),
        P("ctx", "tp"),
        P("ctx", "tp"),
        P("ctx", "tp"),
    )
    return jax.shard_map(
        functools.partial(body, mesh.shape["ctx"], mesh.shape["tp"]), mesh=mesh, in_specs=in_specs, out_specs=out_specs, check_vma=False)
```

```python
import functools
import math

import jax
import jax.numpy as jnp
import ml_dtypes
import numpy as np
from jax import lax
from jax.experimental import pallas as pl
from jax.experimental.pallas import tpu as pltpu
from jax.sharding import PartitionSpec as P

MESH = pl.DeviceIdType.MESH
BF16 = jnp.bfloat16
F32 = jnp.float32
LONGEST_DENSE = 2048
VMEM_GRANT = 60 * 1024 * 1024
PARTS = ("prod", "gates", "grad", "smix", "lmix", "filt", "back", "bone")


def passed_along(block, axis, distance):
    devices = range(lax.axis_size(axis))
    route = [(i - distance, i) for i in devices if i - distance in devices]
    return lax.ppermute(block, axis, route)


def angle_tables(blocks, inner):
    size_one = 2 * blocks
    whole = size_one * inner
    first = (
        lax.broadcasted_iota(jnp.int32, (size_one, blocks), 0)
        * lax.broadcasted_iota(jnp.int32, (size_one, blocks), 1)
        % size_one
    )
    phase_one = first.astype(jnp.float32) * (2.0 * math.pi / size_one)
    twist = (
        lax.broadcasted_iota(jnp.int32, (size_one, inner), 0)
        * lax.broadcasted_iota(jnp.int32, (size_one, inner), 1)
        % whole
    )
    phase_twist = twist.astype(jnp.float32) * (2.0 * math.pi / whole)
    second = (
        lax.broadcasted_iota(jnp.int32, (inner, inner), 0)
        * lax.broadcasted_iota(jnp.int32, (inner, inner), 1)
        % inner
    )
    phase_two = second.astype(jnp.float32) * (2.0 * math.pi / inner)
    return (
        jnp.cos(phase_one),
        jnp.sin(phase_one),
        jnp.cos(phase_twist)[:, None, :],
        jnp.sin(phase_twist)[:, None, :],
        jnp.cos(phase_two),
        jnp.sin(phase_two),
        whole,
    )


def spectrum(values, tables):
    cos_one, sin_one, cos_twist, sin_twist, cos_two, sin_two, whole = tables
    highest = lax.Precision.HIGHEST
    real_a = jnp.einsum("kn,ncm->kcm", cos_one, values, precision=highest)
    imag_a = -jnp.einsum("kn,ncm->kcm", sin_one, values, precision=highest)
    real_b = real_a * cos_twist + imag_a * sin_twist
    imag_b = imag_a * cos_twist - real_a * sin_twist
    real_c = jnp.einsum("kcm,mq->kcq", real_b, cos_two, precision=highest) + jnp.einsum(
        "kcm,mq->kcq", imag_b, sin_two, precision=highest
    )
    imag_c = jnp.einsum("kcm,mq->kcq", imag_b, cos_two, precision=highest) - jnp.einsum(
        "kcm,mq->kcq", real_b, sin_two, precision=highest
    )
    return (real_c, imag_c)


def restore(real_in, imag_in, tables, both):
    cos_one, sin_one, cos_twist, sin_twist, cos_two, sin_two, whole = tables
    highest = lax.Precision.HIGHEST
    real_p = jnp.einsum("kcq,qm->kcm", real_in, cos_two, precision=highest) - jnp.einsum(
        "kcq,qm->kcm", imag_in, sin_two, precision=highest
    )
    imag_p = jnp.einsum("kcq,qm->kcm", imag_in, cos_two, precision=highest) + jnp.einsum(
        "kcq,qm->kcm", real_in, sin_two, precision=highest
    )
    real_q = real_p * cos_twist - imag_p * sin_twist
    imag_q = imag_p * cos_twist + real_p * sin_twist
    real_out = (
        jnp.einsum("kn,kcm->ncm", cos_one, real_q, precision=highest)
        - jnp.einsum("kn,kcm->ncm", sin_one, imag_q, precision=highest)
    ) / whole
    if both:
        imag_out = (
            jnp.einsum("kn,kcm->ncm", cos_one, imag_q, precision=highest)
            + jnp.einsum("kn,kcm->ncm", sin_one, real_q, precision=highest)
        ) / whole
        return (real_out, imag_out)
    return real_out


def spectral(product, gated, filter_in):
    blocks, count, inner = product.shape
    tables = angle_tables(blocks, inner)
    real_u, imag_u = spectrum(product.astype(jnp.float32), tables)
    real_g, imag_g = spectrum(gated.astype(jnp.float32), tables)
    real_h, imag_h = spectrum(filter_in.astype(jnp.float32), tables)
    real_pair = real_h * real_u - imag_h * imag_u - real_h * imag_g + imag_h * real_g
    imag_pair = real_h * imag_u + imag_h * real_u + real_h * real_g + imag_h * imag_g
    conv_part, back_part = restore(real_pair, imag_pair, tables, True)
    filter_part = restore(
        real_u * real_g + imag_u * imag_g, real_u * imag_g - imag_u * real_g, tables, False
    )
    return (conv_part, back_part, filter_part)


def tap_sum(extended, weights, token_rows, causal):
    filter_taps, channels = weights.shape

    def group_step(group, total):
        for inner in range(8):
            place = group * 8 + inner
            weight_row = lax.dynamic_index_in_dim(weights, place, 0, keepdims=False).astype(
                jnp.float32
            )
            start = filter_taps - 1 - place if causal else place
            shifted = lax.dynamic_slice_in_dim(extended, start, token_rows, 0).astype(jnp.float32)
            total = total + weight_row[None, :] * shifted
        return total

    return lax.fori_loop(
        0, filter_taps // 8, group_step, jnp.zeros((token_rows, channels), jnp.float32)
    )


def filter_terms(extended, grads, filter_taps):
    token_rows, channels = grads.shape

    def group_terms(group):
        partials = []
        for inner in range(8):
            place = group * 8 + inner
            shifted = lax.dynamic_slice_in_dim(
                extended, filter_taps - 1 - place, token_rows, 0
            ).astype(jnp.float32)
            partials.append(jnp.sum(grads * shifted, axis=0))
        return jnp.stack(partials)

    stacked = lax.map(group_terms, jnp.arange(filter_taps // 8, dtype=jnp.int32))
    return stacked.reshape(filter_taps, channels)


def general_body(
    short_query,
    short_key,
    short_value,
    short_filter,
    long_query,
    long_key,
    long_filter,
    out_weight,
    out_grad,
):
    token_rows, channels = short_query.shape
    groups = lax.axis_size("ctx")
    seq_len = token_rows * groups
    scaling = 1.0 / math.sqrt(seq_len)
    filter_taps = short_filter.shape[0]
    product_one = (short_key.astype(jnp.float32) * short_value.astype(jnp.float32)).astype(
        jnp.bfloat16
    )
    before = passed_along(product_one[token_rows - (filter_taps - 1) :], "ctx", 1)
    extended_prod = jnp.concatenate([before, product_one], axis=0)
    short_mix = tap_sum(extended_prod, short_filter, token_rows, True)
    mixed = (short_query.astype(jnp.float32) * short_mix).astype(jnp.bfloat16)
    grad_two = lax.dot_general(
        lax.all_gather(out_grad, "tp", axis=1, tiled=True),
        out_weight,
        (((1,), (1,)), ((), ())),
        preferred_element_type=jnp.float32,
    ).astype(jnp.bfloat16)

    def to_channels(values):
        return values.T.reshape(groups, channels // groups, token_rows)

    def to_tokens(values):
        return values.reshape(channels, token_rows).T

    product_two = (long_key.astype(jnp.float32) * mixed.astype(jnp.float32)).astype(jnp.bfloat16)
    gated_two = (grad_two.astype(jnp.float32) * long_query.astype(jnp.float32)).astype(jnp.bfloat16)
    conv_part, back_part, filter_part = spectral(
        lax.all_to_all(to_channels(product_two), "ctx", split_axis=0, concat_axis=0, tiled=True),
        lax.all_to_all(to_channels(gated_two), "ctx", split_axis=0, concat_axis=0, tiled=True),
        lax.all_to_all(to_channels(long_filter), "ctx", split_axis=0, concat_axis=0, tiled=True),
    )
    long_mix = lax.all_to_all(conv_part, "ctx", split_axis=0, concat_axis=0, tiled=True)
    back_two = lax.all_to_all(back_part, "ctx", split_axis=0, concat_axis=0, tiled=True)
    filter_two = lax.all_to_all(filter_part, "ctx", split_axis=0, concat_axis=0, tiled=True)
    long_mix = to_tokens(long_mix)
    back_two = to_tokens(back_two)
    filter_two = to_tokens(filter_two)
    long_query_grad = (grad_two.astype(jnp.float32) * long_mix).astype(jnp.bfloat16)
    long_key_grad = (back_two * mixed.astype(jnp.float32)).astype(jnp.bfloat16)
    mixed_grad = (back_two * long_key.astype(jnp.float32)).astype(jnp.bfloat16)
    long_filter_grad = (filter_two * scaling).astype(jnp.bfloat16)
    gated_one = (mixed_grad.astype(jnp.float32) * short_query.astype(jnp.float32)).astype(
        jnp.bfloat16
    )
    short_query_grad = (mixed_grad.astype(jnp.float32) * short_mix).astype(jnp.bfloat16)
    after = passed_along(gated_one[: filter_taps - 1], "ctx", -1)
    extended_grad = jnp.concatenate([gated_one, after], axis=0)
    back_one = tap_sum(extended_grad, short_filter, token_rows, False)
    short_key_grad = (back_one * short_value.astype(jnp.float32)).astype(jnp.bfloat16)
    short_value_grad = (back_one * short_key.astype(jnp.float32)).astype(jnp.bfloat16)
    local_terms = filter_terms(extended_prod, gated_one.astype(jnp.float32), filter_taps)
    filter_one = lax.psum(local_terms, "ctx")
    short_filter_grad = (filter_one * scaling).astype(jnp.bfloat16)
    return (
        short_query_grad,
        short_key_grad,
        short_value_grad,
        short_filter_grad,
        long_query_grad,
        long_key_grad,
        long_filter_grad,
    )


def wave_tables(seq_len):
    time = np.arange(seq_len, dtype=np.int64)[:, None]
    odd = 2 * np.arange(seq_len, dtype=np.int64)[None, :] + 1
    phase = (time * odd % (4 * seq_len)).astype(np.float64) * (math.pi / (2 * seq_len))
    forward = np.concatenate([np.cos(phase), np.sin(phase)], axis=1)
    return (
        forward.astype(ml_dtypes.bfloat16),
        np.ascontiguousarray(forward.T).astype(ml_dtypes.bfloat16),
    )


def dot(a, b):
    return jnp.dot(a, b, preferred_element_type=F32)


def partner(index, step, size):
    bit = 1
    while bit < size:
        if step & bit:
            index = index + bit - 2 * bit * lax.rem(lax.div(index, bit), 2)
        bit *= 2
    return index


def steps_of(size):
    far, near = list(range(size // 2, size)), list(range(1, size // 2))
    return [step for pair in zip(far, near + [0]) for step in pair if step > 0]


def flipped(block):
    return block.astype(F32).T.astype(BF16)


def operator_kernel(
    n, m,
    sq_in, sk_in, sv_in, sf_in, lq_in, lk_in, lf_in, og_in, weight, forward, inverse,
    sq_grad, lq_grad, lk_grad, lf_grad, bone_out, taps_out,
    smix_rx, lmix_rx, filt_rx, back_rx, taps_rx, results, sq, sk, sv, lk, sf, lq, lf, og, grad, weight_v, fwd, inv, og_rx, tx_prod, tx_gates, tx_grad, rx_prod, rx_gates, rx_grad,
    tx_smix, tx_lmix, tx_filt, tx_back, tx_bone, tx_taps, filter_t, signals, smix,
    spec_prod, spec_sf, spec_u, spec_h, waves, load_sem, own_sem, og_send, og_recv, taps_send, taps_recv,
    send, recv,
):
    me = lax.axis_index("ctx")
    col = lax.axis_index("tp")
    rows, chans = sq.shape
    cb = chans // n
    taps = sf.shape[0]
    seq = rows * n
    tile = 2 * rows
    kt = 256

    barrier = pltpu.get_barrier_semaphore()
    for d in range(1, n):
        pl.semaphore_signal(
            barrier, inc=1, device_id=(lax.rem(me + d, n), col), device_id_type=MESH
        )
    for d in range(1, m):
        pl.semaphore_signal(
            barrier, inc=1, device_id=(me, lax.rem(col + d, m)), device_id_type=MESH
        )

    loads = {}
    for place, (name, source, target) in enumerate((
        ("sk", sk_in, sk), ("sv", sv_in, sv), ("og", og_in, og), ("lf", lf_in, lf),
        ("lk", lk_in, lk), ("sq", sq_in, sq), ("sf", sf_in, sf), ("fwd", forward, fwd),
        ("lq", lq_in, lq), ("weight", weight, weight_v), ("inv", inverse, inv),
    )):
        loads[name] = pltpu.make_async_copy(source, target, load_sem.at[place])
        loads[name].start()

    loads["sk"].wait()
    loads["sv"].wait()
    tx_prod[...] = (sk[...].astype(F32) * sv[...].astype(F32)).T.astype(BF16)
    loads["og"].wait()
    pl.semaphore_wait(barrier, n + m - 2)

    col_pair = col + 1 - 2 * lax.rem(col, 2)

    def og_copy(slot, source, peer):
        copy = pltpu.make_async_remote_copy(
            src_ref=source,
            dst_ref=og_rx.at[slot],
            send_sem=og_send.at[slot],
            recv_sem=og_recv.at[slot],
            device_id=(me, peer),
            device_id_type=MESH,
        )
        copy.start()
        return copy

    og_far = [og_copy(d, og, lax.rem(col + 2 * d, m)) for d in range(1, m // 2)]
    og_near = [og_copy(0, og, col_pair)]

    own_rows = pl.ds(pl.multiple_of(me * cb, cb), cb)
    sent = {}

    def exchange(part, source, target):
        place = PARTS.index(part)
        copies = []
        for d in steps_of(n):
            peer = partner(me, d, n)
            copy = pltpu.make_async_remote_copy(
                src_ref=source(peer),
                dst_ref=target,
                send_sem=send.at[place, d - 1],
                recv_sem=recv.at[place, d - 1],
                device_id=(peer, col),
                device_id_type=MESH,
            )
            copy.start()
            copies.append(copy)
        sent[part] = copies

    kept = []

    def keep(source, target):
        copy = pltpu.make_async_copy(source, target, own_sem.at[len(kept)])
        copy.start()
        kept.append(copy)

    def arrived(part):
        for copy in sent[part]:
            copy.wait_recv()

    def row_block(peer):
        return pl.ds(pl.multiple_of(peer * cb, cb), cb)

    exchange("prod", lambda peer: tx_prod.at[row_block(peer)], rx_prod.at[me])
    rx_prod[me] = tx_prod[own_rows]
    loads["lf"].wait()
    tx_gates[0] = flipped(lf[...])
    loads["lk"].wait()
    loads["sq"].wait()
    tx_gates[1] = (lk[...].astype(F32) * sq[...].astype(F32)).T.astype(BF16)
    exchange("gates", lambda peer: tx_gates.at[:, row_block(peer)], rx_gates.at[me])
    for place in range(2):
        rx_gates[me, place] = tx_gates[place, own_rows]
    loads["sf"].wait()
    filter_t[...] = flipped(sf[...])

    def tiles(k):
        start = pl.multiple_of(k * kt, kt)
        return pl.ds(start, kt), pl.ds(pl.multiple_of(seq + start, kt), kt)

    def halves(rows_in, depth, k):
        cos_at, sin_at = tiles(k)
        return dot(rows_in, fwd[:depth, cos_at]), dot(rows_in, fwd[:depth, sin_at])

    for d in range(1, m // 2):
        og_far[d - 1].wait_recv()
        og_near.append(og_copy(m // 2 - 1 + d, og_rx.at[d], col_pair))

    arrived("prod")
    for s in range(n):
        signals[0:cb, s * rows : (s + 1) * rows] = rx_prod[s]
    loads["fwd"].wait()

    def short_step(k, carry):
        cos_at, sin_at = tiles(k)
        pc, ps = halves(signals[0:cb, :], seq, k)
        fc, fs = halves(filter_t[own_rows, :], taps, k)
        spec_prod[:, cos_at] = pc
        spec_prod[:, sin_at] = ps
        spec_sf[:, cos_at] = fc
        spec_sf[:, sin_at] = fs
        waves[0:cb, cos_at] = (pc * fc - ps * fs).astype(BF16)
        waves[0:cb, sin_at] = (pc * fs + ps * fc).astype(BF16)
        return carry

    lax.fori_loop(0, seq // kt, short_step, 0, unroll=True)
    loads["inv"].wait()

    def at_tokens(step):
        return pl.ds(pl.multiple_of(step * tile, tile), tile)

    def put(target, step, values):
        for b in range(2):
            target[step * 2 + b] = values[:, b * rows : (b + 1) * rows].astype(BF16)

    def short_back(step, carry):
        mix = dot(waves[0:cb, :], inv[:, at_tokens(step)]) * (1.0 / seq)
        smix[:, at_tokens(step)] = mix
        put(tx_smix, step, mix)
        return carry

    lax.fori_loop(0, n // 2, short_back, 0, unroll=True)

    loads["weight"].wait()
    loads["lq"].wait()
    def projected(owner, block):
        features = pl.ds(pl.multiple_of(owner * chans, chans), chans)
        return lax.dot_general(
            weight_v[:, features], block, (((1,), (1,)), ((), ())), preferred_element_type=F32
        )

    total = projected(col, og[...])
    for d in range(1, m // 2):
        total = total + projected(lax.rem(col + m - 2 * d, m), og_rx[d])
    for place, copy in enumerate(og_near):
        copy.wait_recv()
        owner = lax.rem(col_pair + m - 2 * place, m)
        total = total + projected(owner, og_rx[0 if place == 0 else m // 2 - 1 + place])
    grad[...] = total.astype(BF16)
    tx_grad[...] = (grad[...].astype(F32) * lq[...].astype(F32).T).astype(BF16)
    exchange("grad", lambda peer: tx_grad.at[row_block(peer)], rx_grad.at[me])
    rx_grad[me] = tx_grad[own_rows]
    exchange("smix", lambda peer: tx_smix.at[peer], smix_rx.at[own_rows])
    smix_rx[own_rows, :] = tx_smix[me]

    arrived("gates")
    for s in range(n):
        at = slice(s * rows, (s + 1) * rows)
        signals[0:cb, at] = (rx_gates[s, 1].astype(F32) * smix[:, at]).astype(BF16)
        signals[cb : 2 * cb, at] = rx_gates[s, 0]

    def long_step(k, carry):
        cos_at, sin_at = tiles(k)
        c, s = halves(signals[0 : 2 * cb, :], seq, k)
        spec_u[:, cos_at] = c[0:cb]
        spec_u[:, sin_at] = s[0:cb]
        spec_h[:, cos_at] = c[cb:]
        spec_h[:, sin_at] = s[cb:]
        waves[0:cb, cos_at] = (c[0:cb] * c[cb:] - s[0:cb] * s[cb:]).astype(BF16)
        waves[0:cb, sin_at] = (c[0:cb] * s[cb:] + s[0:cb] * c[cb:]).astype(BF16)
        return carry

    lax.fori_loop(0, seq // kt, long_step, 0, unroll=True)

    def mix_back(step, carry):
        put(tx_lmix, step, dot(waves[0:cb, :], inv[:, at_tokens(step)]) * (1.0 / seq))
        return carry

    lax.fori_loop(0, n // 2, mix_back, 0, unroll=True)
    exchange("lmix", lambda peer: tx_lmix.at[peer], lmix_rx.at[own_rows])
    lmix_rx[own_rows, :] = tx_lmix[me]

    arrived("grad")
    for s in range(n):
        signals[2 * cb : 3 * cb, s * rows : (s + 1) * rows] = rx_grad[s]

    def grad_step(k, carry):
        cos_at, sin_at = tiles(k)
        c, s = halves(signals[2 * cb : 3 * cb, :], seq, k)
        uc, us = spec_u[:, cos_at], spec_u[:, sin_at]
        hc, hs = spec_h[:, cos_at], spec_h[:, sin_at]
        waves[cb : 2 * cb, cos_at] = (hc * c + hs * s).astype(BF16)
        waves[cb : 2 * cb, sin_at] = (hc * s - hs * c).astype(BF16)
        waves[2 * cb : 3 * cb, cos_at] = (uc * c + us * s).astype(BF16)
        waves[2 * cb : 3 * cb, sin_at] = (uc * s - us * c).astype(BF16)
        return carry

    lax.fori_loop(0, seq // kt, grad_step, 0, unroll=True)

    def long_back(step, carry):
        mixes = dot(waves[cb:, :], inv[:, at_tokens(step)]) * (1.0 / seq)
        put(tx_back, step, mixes[0:cb])
        put(tx_filt, step, mixes[cb:] * (1.0 / math.sqrt(seq)))
        smix[:, at_tokens(step)] = mixes[0:cb]
        return carry

    lax.fori_loop(0, n // 2, long_back, 0, unroll=True)
    for part, source, target in (
        ("back", tx_back, back_rx), ("filt", tx_filt, filt_rx)
    ):
        exchange(part, lambda peer, source=source: source.at[peer], target.at[own_rows])
        target[own_rows, :] = source[me]

    for s in range(n):
        at = slice(s * rows, (s + 1) * rows)
        signals[0:cb, at] = (smix[:, at] * rx_gates[s, 1].astype(F32)).astype(BF16)

    def gate_step(k, carry):
        cos_at, sin_at = tiles(k)
        c, s = halves(signals[0:cb, :], seq, k)
        pc, ps = spec_prod[:, cos_at], spec_prod[:, sin_at]
        fc, fs = spec_sf[:, cos_at], spec_sf[:, sin_at]
        waves[0:cb, cos_at] = (fc * c + fs * s).astype(BF16)
        waves[0:cb, sin_at] = (fc * s - fs * c).astype(BF16)
        waves[cb : 2 * cb, cos_at] = (pc * c + ps * s).astype(BF16)
        waves[cb : 2 * cb, sin_at] = (pc * s - ps * c).astype(BF16)
        return carry

    lax.fori_loop(0, seq // kt, gate_step, 0, unroll=True)

    terms = dot(waves[cb : 2 * cb, :], inv[:, 0:taps]) * (1.0 / (seq * math.sqrt(seq)))
    tx_taps[...] = terms.astype(BF16)
    taps_rx[own_rows, :] = tx_taps[...]
    pair = me + 1 - 2 * lax.rem(me, 2)

    def taps_copy(place, source, target_rows, peer):
        copy = pltpu.make_async_remote_copy(
            src_ref=source,
            dst_ref=taps_rx.at[target_rows],
            send_sem=taps_send.at[place],
            recv_sem=taps_recv.at[place],
            device_id=(peer, col),
            device_id_type=MESH,
        )
        copy.start()
        return copy

    far = [
        taps_copy(d - 1, tx_taps, own_rows, partner(me, 2 * d, n))
        for d in range(n // 2 - 1, 0, -1)
    ]
    near = [taps_copy(n // 2 - 1, tx_taps, own_rows, pair)]

    def short_grad(step, carry):
        put(tx_bone, step, dot(waves[0:cb, :], inv[:, at_tokens(step)]) * (1.0 / seq))
        return carry

    lax.fori_loop(0, n // 2, short_grad, 0, unroll=True)
    exchange("bone", lambda peer: tx_bone.at[peer], bone_out.at[own_rows])
    keep(tx_bone.at[me], bone_out.at[own_rows])

    def finish(place, target, values):
        results[place] = values.T.astype(BF16)
        keep(results.at[place], target)

    arrived("smix")
    arrived("lmix")
    finish(0, lq_grad, grad[...].astype(F32) * lmix_rx[...].astype(F32))
    arrived("back")
    back = back_rx[...].astype(F32).T
    mix = smix_rx[...].astype(F32).T
    mixed = (sq[...].astype(F32) * mix).astype(BF16).astype(F32)
    results[1] = (back * mixed).astype(BF16)
    keep(results.at[1], lk_grad)
    mixed_grad = (back * lk[...].astype(F32)).astype(BF16).astype(F32)
    results[2] = (mixed_grad * mix).astype(BF16)
    keep(results.at[2], sq_grad)
    arrived("filt")
    finish(3, lf_grad, filt_rx[...].astype(F32))

    for d in range(1, n // 2):
        far[n // 2 - 1 - d].wait_recv()
        source = row_block(partner(me, 2 * d, n))
        near.append(taps_copy(n // 2 - 1 + d, taps_rx.at[source], source, pair))
    for copy in near:
        copy.wait_recv()
    keep(taps_rx, taps_out)

    arrived("bone")
    for part in PARTS:
        for copy in sent[part]:
            copy.wait_send()
    for copy in og_far + og_near + far + near:
        copy.wait_send()
    for copy in kept:
        copy.wait()


def finish_kernel(
    sq_done, lq_done, lk_done, lf_done, bone, taps, sk, sv,
    sq_grad, sk_grad, sv_grad, sf_grad, lq_grad, lk_grad, lf_grad,
    bone_v, taps_v, sk_v, sv_v, sk_out, sv_out, sf_out, done_v, move_sem,
):
    def move(place, source, target):
        copy = pltpu.make_async_copy(source, target, move_sem.at[place])
        copy.start()
        return copy

    loads = [
        move(place, source, target)
        for place, (source, target) in enumerate(
            ((bone, bone_v), (sv, sv_v), (sk, sk_v), (taps, taps_v))
        )
    ]
    done = [
        move(4 + place, source, done_v.at[place])
        for place, source in enumerate((sq_done, lq_done, lk_done, lf_done))
    ]
    moves = []
    for place, target in enumerate((sq_grad, lq_grad, lk_grad, lf_grad)):
        done[place].wait()
        moves.append(move(11 + place, done_v.at[place], target))
    loads[0].wait()
    back_one = bone_v[...].astype(F32).T
    loads[1].wait()
    sk_out[...] = (back_one * sv_v[...].astype(F32)).astype(BF16)
    moves.append(move(8, sk_out, sk_grad))
    loads[2].wait()
    sv_out[...] = (back_one * sk_v[...].astype(F32)).astype(BF16)
    moves.append(move(9, sv_out, sv_grad))
    loads[3].wait()
    sf_out[...] = flipped(taps_v[...])
    moves.append(move(10, sf_out, sf_grad))
    for copy in moves:
        copy.wait()


def dense_body(
    n, m, sq, sk, sv, sf, lq, lk, lf, weight, og
):
    rows, chans = sq.shape
    taps = sf.shape[0]
    seq = rows * n
    cb = chans // n
    forward, inverse = wave_tables(seq)
    hbm = pl.BlockSpec(memory_space=pltpu.HBM)
    tokens = jax.ShapeDtypeStruct((rows, chans), BF16)
    turned = jax.ShapeDtypeStruct((chans, rows), BF16)
    blocks = pltpu.VMEM((n, cb, rows), BF16)
    spectrum = pltpu.VMEM((cb, 2 * seq), F32)
    sent_on = pl.pallas_call(
        functools.partial(operator_kernel, n, m),
        out_shape=[tokens] * 4 + [turned, jax.ShapeDtypeStruct((chans, taps), BF16)],
        in_specs=[hbm] * 11,
        out_specs=[hbm] * 6,
        scratch_shapes=[
            pltpu.VMEM((chans, rows), BF16),
            pltpu.VMEM((chans, rows), BF16),
            pltpu.VMEM((chans, rows), BF16),
            pltpu.VMEM((chans, rows), BF16),
            pltpu.VMEM((chans, taps), BF16),
            pltpu.VMEM((4, rows, chans), BF16),
            pltpu.VMEM((rows, chans), BF16),
            pltpu.VMEM((rows, chans), BF16),
            pltpu.VMEM((rows, chans), BF16),
            pltpu.VMEM((rows, chans), BF16),
            pltpu.VMEM((taps, chans), BF16),
            pltpu.VMEM((rows, chans), BF16),
            pltpu.VMEM((rows, chans), BF16),
            pltpu.VMEM((rows, chans), BF16),
            pltpu.VMEM((chans, rows), BF16),
            pltpu.VMEM(weight.shape, BF16),
            pltpu.VMEM(forward.shape, BF16),
            pltpu.VMEM(inverse.shape, BF16),
            pltpu.VMEM((m - 1, rows, chans), BF16),
            pltpu.VMEM((chans, rows), BF16),
            pltpu.VMEM((2, chans, rows), BF16),
            pltpu.VMEM((chans, rows), BF16),
            blocks,
            pltpu.VMEM((n, 2, cb, rows), BF16),
            blocks,
            blocks, blocks, blocks, blocks, blocks,
            pltpu.VMEM((cb, taps), BF16),
            pltpu.VMEM((chans, taps), BF16),
            pltpu.VMEM((3 * cb, seq), BF16),
            pltpu.VMEM((cb, seq), F32),
            spectrum, spectrum, spectrum, spectrum,
            pltpu.VMEM((3 * cb, 2 * seq), BF16),
            pltpu.SemaphoreType.DMA((11,)),
            pltpu.SemaphoreType.DMA((6,)),
            pltpu.SemaphoreType.DMA((m - 1,)),
            pltpu.SemaphoreType.DMA((m - 1,)),
            pltpu.SemaphoreType.DMA((n - 1,)),
            pltpu.SemaphoreType.DMA((n - 1,)),
            pltpu.SemaphoreType.DMA((len(PARTS), n - 1)),
            pltpu.SemaphoreType.DMA((len(PARTS), n - 1)),
        ],
        compiler_params=pltpu.CompilerParams(
            collective_id=0, has_side_effects=True, vmem_limit_bytes=VMEM_GRANT
        ),
    )(sq, sk, sv, sf, lq, lk, lf, og, weight, jnp.asarray(forward), jnp.asarray(inverse))
    short = jax.ShapeDtypeStruct((taps, chans), BF16)
    return pl.pallas_call(
        finish_kernel,
        out_shape=[tokens] * 3 + [short] + [tokens] * 3,
        in_specs=[hbm] * 8,
        out_specs=[hbm] * 7,
        scratch_shapes=[
            pltpu.VMEM((chans, rows), BF16),
            pltpu.VMEM((chans, taps), BF16),
            pltpu.VMEM((rows, chans), BF16),
            pltpu.VMEM((rows, chans), BF16),
            pltpu.VMEM((rows, chans), BF16),
            pltpu.VMEM((rows, chans), BF16),
            pltpu.VMEM((taps, chans), BF16),
            pltpu.VMEM((4, rows, chans), BF16),
            pltpu.SemaphoreType.DMA((15,)),
        ],
        compiler_params=pltpu.CompilerParams(vmem_limit_bytes=VMEM_GRANT),
    )(*sent_on, sk, sv)


def body(n, m, *arrays):
    rows, chans = arrays[0].shape
    taps = arrays[3].shape[0]
    dense = (
        rows * n <= LONGEST_DENSE
        and rows % 128 == 0
        and taps % 128 == 0
        and taps <= rows * n
        and n > 1
        and n & (n - 1) == 0
        and m > 1
        and m % 2 == 0
        and chans % (16 * n) == 0
        and chans % 128 == 0
    )
    if dense:
        return tuple(dense_body(n, m, *arrays))
    return general_body(*arrays)


def solution(mesh):
    in_specs = (
        P("ctx", "tp"),
        P("ctx", "tp"),
        P("ctx", "tp"),
        P(None, "tp"),
        P("ctx", "tp"),
        P("ctx", "tp"),
        P("ctx", "tp"),
        P("tp", None),
        P("ctx", "tp"),
    )
    out_specs = (
        P("ctx", "tp"),
        P("ctx", "tp"),
        P("ctx", "tp"),
        P(None, "tp"),
        P("ctx", "tp"),
        P("ctx", "tp"),
        P("ctx", "tp"),
    )
    return jax.shard_map(
        functools.partial(body, mesh.shape["ctx"], mesh.shape["tp"]), mesh=mesh, in_specs=in_specs, out_specs=out_specs, check_vma=False)
```

```python
import functools
import math

import jax
import jax.numpy as jnp
import ml_dtypes
import numpy as np
from jax import lax
from jax.experimental import pallas as pl
from jax.experimental.pallas import tpu as pltpu
from jax.sharding import PartitionSpec as P

MESH = pl.DeviceIdType.MESH
BF16 = jnp.bfloat16
F32 = jnp.float32
LONGEST_DENSE = 2048
VMEM_GRANT = 60 * 1024 * 1024
PARTS = ("pair", "gate", "grad", "smix", "lmix", "filt", "back", "bone")


def passed_along(block, axis, distance):
    devices = range(lax.axis_size(axis))
    route = [(i - distance, i) for i in devices if i - distance in devices]
    return lax.ppermute(block, axis, route)


def angle_tables(blocks, inner):
    size_one = 2 * blocks
    whole = size_one * inner
    first = (
        lax.broadcasted_iota(jnp.int32, (size_one, blocks), 0)
        * lax.broadcasted_iota(jnp.int32, (size_one, blocks), 1)
        % size_one
    )
    phase_one = first.astype(jnp.float32) * (2.0 * math.pi / size_one)
    twist = (
        lax.broadcasted_iota(jnp.int32, (size_one, inner), 0)
        * lax.broadcasted_iota(jnp.int32, (size_one, inner), 1)
        % whole
    )
    phase_twist = twist.astype(jnp.float32) * (2.0 * math.pi / whole)
    second = (
        lax.broadcasted_iota(jnp.int32, (inner, inner), 0)
        * lax.broadcasted_iota(jnp.int32, (inner, inner), 1)
        % inner
    )
    phase_two = second.astype(jnp.float32) * (2.0 * math.pi / inner)
    return (
        jnp.cos(phase_one),
        jnp.sin(phase_one),
        jnp.cos(phase_twist)[:, None, :],
        jnp.sin(phase_twist)[:, None, :],
        jnp.cos(phase_two),
        jnp.sin(phase_two),
        whole,
    )


def spectrum(values, tables):
    cos_one, sin_one, cos_twist, sin_twist, cos_two, sin_two, whole = tables
    highest = lax.Precision.HIGHEST
    real_a = jnp.einsum("kn,ncm->kcm", cos_one, values, precision=highest)
    imag_a = -jnp.einsum("kn,ncm->kcm", sin_one, values, precision=highest)
    real_b = real_a * cos_twist + imag_a * sin_twist
    imag_b = imag_a * cos_twist - real_a * sin_twist
    real_c = jnp.einsum("kcm,mq->kcq", real_b, cos_two, precision=highest) + jnp.einsum(
        "kcm,mq->kcq", imag_b, sin_two, precision=highest
    )
    imag_c = jnp.einsum("kcm,mq->kcq", imag_b, cos_two, precision=highest) - jnp.einsum(
        "kcm,mq->kcq", real_b, sin_two, precision=highest
    )
    return (real_c, imag_c)


def restore(real_in, imag_in, tables, both):
    cos_one, sin_one, cos_twist, sin_twist, cos_two, sin_two, whole = tables
    highest = lax.Precision.HIGHEST
    real_p = jnp.einsum("kcq,qm->kcm", real_in, cos_two, precision=highest) - jnp.einsum(
        "kcq,qm->kcm", imag_in, sin_two, precision=highest
    )
    imag_p = jnp.einsum("kcq,qm->kcm", imag_in, cos_two, precision=highest) + jnp.einsum(
        "kcq,qm->kcm", real_in, sin_two, precision=highest
    )
    real_q = real_p * cos_twist - imag_p * sin_twist
    imag_q = imag_p * cos_twist + real_p * sin_twist
    real_out = (
        jnp.einsum("kn,kcm->ncm", cos_one, real_q, precision=highest)
        - jnp.einsum("kn,kcm->ncm", sin_one, imag_q, precision=highest)
    ) / whole
    if both:
        imag_out = (
            jnp.einsum("kn,kcm->ncm", cos_one, imag_q, precision=highest)
            + jnp.einsum("kn,kcm->ncm", sin_one, real_q, precision=highest)
        ) / whole
        return (real_out, imag_out)
    return real_out


def spectral(product, gated, filter_in):
    blocks, count, inner = product.shape
    tables = angle_tables(blocks, inner)
    real_u, imag_u = spectrum(product.astype(jnp.float32), tables)
    real_g, imag_g = spectrum(gated.astype(jnp.float32), tables)
    real_h, imag_h = spectrum(filter_in.astype(jnp.float32), tables)
    real_pair = real_h * real_u - imag_h * imag_u - real_h * imag_g + imag_h * real_g
    imag_pair = real_h * imag_u + imag_h * real_u + real_h * real_g + imag_h * imag_g
    conv_part, back_part = restore(real_pair, imag_pair, tables, True)
    filter_part = restore(
        real_u * real_g + imag_u * imag_g, real_u * imag_g - imag_u * real_g, tables, False
    )
    return (conv_part, back_part, filter_part)


def tap_sum(extended, weights, token_rows, causal):
    filter_taps, channels = weights.shape

    def group_step(group, total):
        for inner in range(8):
            place = group * 8 + inner
            weight_row = lax.dynamic_index_in_dim(weights, place, 0, keepdims=False).astype(
                jnp.float32
            )
            start = filter_taps - 1 - place if causal else place
            shifted = lax.dynamic_slice_in_dim(extended, start, token_rows, 0).astype(jnp.float32)
            total = total + weight_row[None, :] * shifted
        return total

    return lax.fori_loop(
        0, filter_taps // 8, group_step, jnp.zeros((token_rows, channels), jnp.float32)
    )


def filter_terms(extended, grads, filter_taps):
    token_rows, channels = grads.shape

    def group_terms(group):
        partials = []
        for inner in range(8):
            place = group * 8 + inner
            shifted = lax.dynamic_slice_in_dim(
                extended, filter_taps - 1 - place, token_rows, 0
            ).astype(jnp.float32)
            partials.append(jnp.sum(grads * shifted, axis=0))
        return jnp.stack(partials)

    stacked = lax.map(group_terms, jnp.arange(filter_taps // 8, dtype=jnp.int32))
    return stacked.reshape(filter_taps, channels)


def general_body(
    short_query,
    short_key,
    short_value,
    short_filter,
    long_query,
    long_key,
    long_filter,
    out_weight,
    out_grad,
):
    token_rows, channels = short_query.shape
    groups = lax.axis_size("ctx")
    seq_len = token_rows * groups
    scaling = 1.0 / math.sqrt(seq_len)
    filter_taps = short_filter.shape[0]
    product_one = (short_key.astype(jnp.float32) * short_value.astype(jnp.float32)).astype(
        jnp.bfloat16
    )
    before = passed_along(product_one[token_rows - (filter_taps - 1) :], "ctx", 1)
    extended_prod = jnp.concatenate([before, product_one], axis=0)
    short_mix = tap_sum(extended_prod, short_filter, token_rows, True)
    mixed = (short_query.astype(jnp.float32) * short_mix).astype(jnp.bfloat16)
    grad_two = lax.dot_general(
        lax.all_gather(out_grad, "tp", axis=1, tiled=True),
        out_weight,
        (((1,), (1,)), ((), ())),
        preferred_element_type=jnp.float32,
    ).astype(jnp.bfloat16)

    def to_channels(values):
        return values.T.reshape(groups, channels // groups, token_rows)

    def to_tokens(values):
        return values.reshape(channels, token_rows).T

    product_two = (long_key.astype(jnp.float32) * mixed.astype(jnp.float32)).astype(jnp.bfloat16)
    gated_two = (grad_two.astype(jnp.float32) * long_query.astype(jnp.float32)).astype(jnp.bfloat16)
    conv_part, back_part, filter_part = spectral(
        lax.all_to_all(to_channels(product_two), "ctx", split_axis=0, concat_axis=0, tiled=True),
        lax.all_to_all(to_channels(gated_two), "ctx", split_axis=0, concat_axis=0, tiled=True),
        lax.all_to_all(to_channels(long_filter), "ctx", split_axis=0, concat_axis=0, tiled=True),
    )
    long_mix = lax.all_to_all(conv_part, "ctx", split_axis=0, concat_axis=0, tiled=True)
    back_two = lax.all_to_all(back_part, "ctx", split_axis=0, concat_axis=0, tiled=True)
    filter_two = lax.all_to_all(filter_part, "ctx", split_axis=0, concat_axis=0, tiled=True)
    long_mix = to_tokens(long_mix)
    back_two = to_tokens(back_two)
    filter_two = to_tokens(filter_two)
    long_query_grad = (grad_two.astype(jnp.float32) * long_mix).astype(jnp.bfloat16)
    long_key_grad = (back_two * mixed.astype(jnp.float32)).astype(jnp.bfloat16)
    mixed_grad = (back_two * long_key.astype(jnp.float32)).astype(jnp.bfloat16)
    long_filter_grad = (filter_two * scaling).astype(jnp.bfloat16)
    gated_one = (mixed_grad.astype(jnp.float32) * short_query.astype(jnp.float32)).astype(
        jnp.bfloat16
    )
    short_query_grad = (mixed_grad.astype(jnp.float32) * short_mix).astype(jnp.bfloat16)
    after = passed_along(gated_one[: filter_taps - 1], "ctx", -1)
    extended_grad = jnp.concatenate([gated_one, after], axis=0)
    back_one = tap_sum(extended_grad, short_filter, token_rows, False)
    short_key_grad = (back_one * short_value.astype(jnp.float32)).astype(jnp.bfloat16)
    short_value_grad = (back_one * short_key.astype(jnp.float32)).astype(jnp.bfloat16)
    local_terms = filter_terms(extended_prod, gated_one.astype(jnp.float32), filter_taps)
    filter_one = lax.psum(local_terms, "ctx")
    short_filter_grad = (filter_one * scaling).astype(jnp.bfloat16)
    return (
        short_query_grad,
        short_key_grad,
        short_value_grad,
        short_filter_grad,
        long_query_grad,
        long_key_grad,
        long_filter_grad,
    )


def wave_tables(seq_len):
    time = np.arange(seq_len, dtype=np.int64)[:, None]
    odd = 2 * np.arange(seq_len, dtype=np.int64)[None, :] + 1
    phase = (time * odd % (4 * seq_len)).astype(np.float64) * (math.pi / (2 * seq_len))
    forward = np.concatenate([np.cos(phase), np.sin(phase)], axis=1)
    return (
        forward.astype(ml_dtypes.bfloat16),
        np.ascontiguousarray(forward.T).astype(ml_dtypes.bfloat16),
    )


def dot(a, b):
    return jnp.dot(a, b, preferred_element_type=F32)


def flipped(block):
    return block.astype(F32).T.astype(BF16)


def operator_kernel(
    n, m,
    sq_in, sk_in, sv_in, sf_in, lq_in, lk_in, lf_in, og_in, weight, forward, inverse,
    sq_grad, lq_grad, lk_grad, lf_grad, bone_out, taps_out,
    smix_rx, lmix_rx, filt_rx, back_rx, taps_rx, results, sq, sk, sv, lk, sf, lq, lf, og, grad, weight_v, fwd, inv, og_rx, tx_gate, tx_pair, tx_grad, rx_gate, rx_pair, rx_grad,
    tx_smix, tx_lmix, tx_filt, tx_back, tx_bone, tx_taps, filter_t, signals, smix,
    spec_prod, spec_sf, spec_h, waves, load_sem, own_sem, og_send, og_recv, taps_send, taps_recv,
    send, recv,
):
    me = lax.axis_index("ctx")
    col = lax.axis_index("tp")
    rows, chans = sq.shape
    cb = chans // n
    taps = sf.shape[0]
    seq = rows * n
    tile = 2 * rows
    kt = 256

    barrier = pltpu.get_barrier_semaphore()
    for d in range(1, n):
        pl.semaphore_signal(
            barrier, inc=1, device_id=(lax.rem(me + d, n), col), device_id_type=MESH
        )
    for d in range(1, m):
        pl.semaphore_signal(
            barrier, inc=1, device_id=(me, lax.rem(col + d, m)), device_id_type=MESH
        )

    loads = {}
    for place, (name, source, target) in enumerate((
        ("sk", sk_in, sk), ("sv", sv_in, sv), ("og", og_in, og), ("lf", lf_in, lf),
        ("lk", lk_in, lk), ("sq", sq_in, sq), ("sf", sf_in, sf), ("fwd", forward, fwd),
        ("lq", lq_in, lq), ("weight", weight, weight_v), ("inv", inverse, inv),
    )):
        loads[name] = pltpu.make_async_copy(source, target, load_sem.at[place])
        loads[name].start()

    loads["sk"].wait()
    loads["sv"].wait()
    tx_pair[0] = (sk[...].astype(F32) * sv[...].astype(F32)).T.astype(BF16)
    loads["lf"].wait()
    tx_pair[1] = flipped(lf[...])
    loads["og"].wait()
    pl.semaphore_wait(barrier, n + m - 2)

    col_pair = col + 1 - 2 * lax.rem(col, 2)

    def og_copy(slot, source, peer):
        copy = pltpu.make_async_remote_copy(
            src_ref=source,
            dst_ref=og_rx.at[slot],
            send_sem=og_send.at[slot],
            recv_sem=og_recv.at[slot],
            device_id=(me, peer),
            device_id_type=MESH,
        )
        copy.start()
        return copy

    og_far = [og_copy(d, og, lax.rem(col + 2 * d, m)) for d in range(1, m // 2)]
    og_near = [og_copy(0, og, col_pair)]

    own_rows = pl.ds(pl.multiple_of(me * cb, cb), cb)
    sent = {}

    def exchange(part, source, target):
        place = PARTS.index(part)
        copies = []
        for d in range(1, n):
            peer = lax.rem(me + d, n)
            copy = pltpu.make_async_remote_copy(
                src_ref=source(peer),
                dst_ref=target,
                send_sem=send.at[place, d - 1],
                recv_sem=recv.at[place, d - 1],
                device_id=(peer, col),
                device_id_type=MESH,
            )
            copy.start()
            copies.append(copy)
        sent[part] = copies

    kept = []

    def keep(source, target):
        copy = pltpu.make_async_copy(source, target, own_sem.at[len(kept)])
        copy.start()
        kept.append(copy)

    def arrived(part):
        for copy in sent[part]:
            copy.wait_recv()

    def row_block(peer):
        return pl.ds(pl.multiple_of(peer * cb, cb), cb)

    exchange("pair", lambda peer: tx_pair.at[:, row_block(peer)], rx_pair.at[me])
    for place in range(2):
        rx_pair[me, place] = tx_pair[place, own_rows]
    loads["lk"].wait()
    loads["sq"].wait()
    tx_gate[...] = (lk[...].astype(F32) * sq[...].astype(F32)).T.astype(BF16)
    exchange("gate", lambda peer: tx_gate.at[row_block(peer)], rx_gate.at[me])
    rx_gate[me] = tx_gate[own_rows]
    loads["sf"].wait()
    filter_t[...] = flipped(sf[...])

    def tiles(k):
        start = pl.multiple_of(k * kt, kt)
        return pl.ds(start, kt), pl.ds(pl.multiple_of(seq + start, kt), kt)

    def halves(rows_in, depth, k):
        cos_at, sin_at = tiles(k)
        return dot(rows_in, fwd[:depth, cos_at]), dot(rows_in, fwd[:depth, sin_at])

    for d in range(1, m // 2):
        og_far[d - 1].wait_recv()
        og_near.append(og_copy(m // 2 - 1 + d, og_rx.at[d], col_pair))

    arrived("pair")
    for s in range(n):
        for place in range(2):
            signals[place * cb : (place + 1) * cb, s * rows : (s + 1) * rows] = rx_pair[s, place]
    loads["fwd"].wait()

    def short_step(k, carry):
        cos_at, sin_at = tiles(k)
        c, s = halves(signals[0 : 2 * cb, :], seq, k)
        pc, ps = c[0:cb], s[0:cb]
        spec_h[:, cos_at] = c[cb:]
        spec_h[:, sin_at] = s[cb:]
        fc, fs = halves(filter_t[own_rows, :], taps, k)
        spec_prod[:, cos_at] = pc
        spec_prod[:, sin_at] = ps
        spec_sf[:, cos_at] = fc
        spec_sf[:, sin_at] = fs
        waves[0:cb, cos_at] = (pc * fc - ps * fs).astype(BF16)
        waves[0:cb, sin_at] = (pc * fs + ps * fc).astype(BF16)
        return carry

    lax.fori_loop(0, seq // kt, short_step, 0, unroll=True)
    loads["inv"].wait()

    def at_tokens(step):
        return pl.ds(pl.multiple_of(step * tile, tile), tile)

    def put(target, step, values):
        for b in range(2):
            target[step * 2 + b] = values[:, b * rows : (b + 1) * rows].astype(BF16)

    def short_back(step, carry):
        mix = dot(waves[0:cb, :], inv[:, at_tokens(step)]) * (1.0 / seq)
        smix[:, at_tokens(step)] = mix
        put(tx_smix, step, mix)
        return carry

    lax.fori_loop(0, n // 2, short_back, 0, unroll=True)

    loads["weight"].wait()
    loads["lq"].wait()
    def projected(owner, block):
        features = pl.ds(pl.multiple_of(owner * chans, chans), chans)
        return lax.dot_general(
            weight_v[:, features], block, (((1,), (1,)), ((), ())), preferred_element_type=F32
        )

    total = projected(col, og[...])
    for d in range(1, m // 2):
        total = total + projected(lax.rem(col + m - 2 * d, m), og_rx[d])
    for place, copy in enumerate(og_near):
        copy.wait_recv()
        owner = lax.rem(col_pair + m - 2 * place, m)
        total = total + projected(owner, og_rx[0 if place == 0 else m // 2 - 1 + place])
    grad[...] = total.astype(BF16)
    tx_grad[...] = (grad[...].astype(F32) * lq[...].astype(F32).T).astype(BF16)
    exchange("grad", lambda peer: tx_grad.at[row_block(peer)], rx_grad.at[me])
    rx_grad[me] = tx_grad[own_rows]
    exchange("smix", lambda peer: tx_smix.at[peer], smix_rx.at[own_rows])
    smix_rx[own_rows, :] = tx_smix[me]

    arrived("gate")
    for s in range(n):
        at = slice(s * rows, (s + 1) * rows)
        signals[0:cb, at] = (rx_gate[s].astype(F32) * smix[:, at]).astype(BF16)
    arrived("grad")
    for s in range(n):
        signals[cb : 2 * cb, s * rows : (s + 1) * rows] = rx_grad[s]

    def long_step(k, carry):
        cos_at, sin_at = tiles(k)
        c, s = halves(signals[...], seq, k)
        uc, us, gc, gs = c[0:cb], s[0:cb], c[cb:], s[cb:]
        hc, hs = spec_h[:, cos_at], spec_h[:, sin_at]
        waves[0:cb, cos_at] = (hc * uc - hs * us).astype(BF16)
        waves[0:cb, sin_at] = (hc * us + hs * uc).astype(BF16)
        waves[cb : 2 * cb, cos_at] = (hc * gc + hs * gs).astype(BF16)
        waves[cb : 2 * cb, sin_at] = (hc * gs - hs * gc).astype(BF16)
        waves[2 * cb : 3 * cb, cos_at] = (uc * gc + us * gs).astype(BF16)
        waves[2 * cb : 3 * cb, sin_at] = (uc * gs - us * gc).astype(BF16)
        return carry

    lax.fori_loop(0, seq // kt, long_step, 0, unroll=True)

    def long_back(step, carry):
        mixes = dot(waves[...], inv[:, at_tokens(step)]) * (1.0 / seq)
        put(tx_lmix, step, mixes[0:cb])
        put(tx_back, step, mixes[cb : 2 * cb])
        put(tx_filt, step, mixes[2 * cb :] * (1.0 / math.sqrt(seq)))
        smix[:, at_tokens(step)] = mixes[cb : 2 * cb]
        return carry

    lax.fori_loop(0, n // 2, long_back, 0, unroll=True)
    for part, source, target in (
        ("back", tx_back, back_rx), ("lmix", tx_lmix, lmix_rx), ("filt", tx_filt, filt_rx)
    ):
        exchange(part, lambda peer, source=source: source.at[peer], target.at[own_rows])
        target[own_rows, :] = source[me]

    for s in range(n):
        at = slice(s * rows, (s + 1) * rows)
        signals[0:cb, at] = (smix[:, at] * rx_gate[s].astype(F32)).astype(BF16)

    def gate_step(k, carry):
        cos_at, sin_at = tiles(k)
        c, s = halves(signals[0:cb, :], seq, k)
        pc, ps = spec_prod[:, cos_at], spec_prod[:, sin_at]
        fc, fs = spec_sf[:, cos_at], spec_sf[:, sin_at]
        waves[0:cb, cos_at] = (fc * c + fs * s).astype(BF16)
        waves[0:cb, sin_at] = (fc * s - fs * c).astype(BF16)
        waves[cb : 2 * cb, cos_at] = (pc * c + ps * s).astype(BF16)
        waves[cb : 2 * cb, sin_at] = (pc * s - ps * c).astype(BF16)
        return carry

    lax.fori_loop(0, seq // kt, gate_step, 0, unroll=True)

    terms = dot(waves[cb : 2 * cb, :], inv[:, 0:taps]) * (1.0 / (seq * math.sqrt(seq)))
    tx_taps[...] = terms.astype(BF16)
    taps_rx[own_rows, :] = tx_taps[...]
    pair = me + 1 - 2 * lax.rem(me, 2)

    def taps_copy(place, source, target_rows, peer):
        copy = pltpu.make_async_remote_copy(
            src_ref=source,
            dst_ref=taps_rx.at[target_rows],
            send_sem=taps_send.at[place],
            recv_sem=taps_recv.at[place],
            device_id=(peer, col),
            device_id_type=MESH,
        )
        copy.start()
        return copy

    far = [
        taps_copy(d - 1, tx_taps, own_rows, lax.rem(me + 2 * d, n)) for d in range(1, n // 2)
    ]
    near = [taps_copy(n // 2 - 1, tx_taps, own_rows, pair)]

    def short_grad(step, carry):
        put(tx_bone, step, dot(waves[0:cb, :], inv[:, at_tokens(step)]) * (1.0 / seq))
        return carry

    lax.fori_loop(0, n // 2, short_grad, 0, unroll=True)
    exchange("bone", lambda peer: tx_bone.at[peer], bone_out.at[own_rows])
    keep(tx_bone.at[me], bone_out.at[own_rows])

    def finish(place, target, values):
        results[place] = values.T.astype(BF16)
        keep(results.at[place], target)

    arrived("smix")
    arrived("lmix")
    finish(0, lq_grad, grad[...].astype(F32) * lmix_rx[...].astype(F32))
    arrived("back")
    back = back_rx[...].astype(F32).T
    mix = smix_rx[...].astype(F32).T
    mixed = (sq[...].astype(F32) * mix).astype(BF16).astype(F32)
    results[1] = (back * mixed).astype(BF16)
    keep(results.at[1], lk_grad)
    mixed_grad = (back * lk[...].astype(F32)).astype(BF16).astype(F32)
    results[2] = (mixed_grad * mix).astype(BF16)
    keep(results.at[2], sq_grad)
    arrived("filt")
    finish(3, lf_grad, filt_rx[...].astype(F32))

    for d in range(1, n // 2):
        far[d - 1].wait_recv()
        source = row_block(lax.rem(me + n - 2 * d, n))
        near.append(taps_copy(n // 2 - 1 + d, taps_rx.at[source], source, pair))
    for copy in near:
        copy.wait_recv()
    keep(taps_rx, taps_out)

    arrived("bone")
    for part in PARTS:
        for copy in sent[part]:
            copy.wait_send()
    for copy in og_far + og_near + far + near:
        copy.wait_send()
    for copy in kept:
        copy.wait()


def finish_kernel(
    sq_done, lq_done, lk_done, lf_done, bone, taps, sk, sv,
    sq_grad, sk_grad, sv_grad, sf_grad, lq_grad, lk_grad, lf_grad,
    bone_v, taps_v, sk_v, sv_v, sk_out, sv_out, sf_out, done_v, move_sem,
):
    def move(place, source, target):
        copy = pltpu.make_async_copy(source, target, move_sem.at[place])
        copy.start()
        return copy

    loads = [
        move(place, source, target)
        for place, (source, target) in enumerate(
            ((bone, bone_v), (sv, sv_v), (sk, sk_v), (taps, taps_v))
        )
    ]
    done = [
        move(4 + place, source, done_v.at[place])
        for place, source in enumerate((sq_done, lq_done, lk_done, lf_done))
    ]
    moves = []
    for place, target in enumerate((sq_grad, lq_grad, lk_grad, lf_grad)):
        done[place].wait()
        moves.append(move(11 + place, done_v.at[place], target))
    loads[0].wait()
    back_one = bone_v[...].astype(F32).T
    loads[1].wait()
    sk_out[...] = (back_one * sv_v[...].astype(F32)).astype(BF16)
    moves.append(move(8, sk_out, sk_grad))
    loads[2].wait()
    sv_out[...] = (back_one * sk_v[...].astype(F32)).astype(BF16)
    moves.append(move(9, sv_out, sv_grad))
    loads[3].wait()
    sf_out[...] = flipped(taps_v[...])
    moves.append(move(10, sf_out, sf_grad))
    for copy in moves:
        copy.wait()


def dense_body(
    n, m, sq, sk, sv, sf, lq, lk, lf, weight, og
):
    rows, chans = sq.shape
    taps = sf.shape[0]
    seq = rows * n
    cb = chans // n
    forward, inverse = wave_tables(seq)
    hbm = pl.BlockSpec(memory_space=pltpu.HBM)
    tokens = jax.ShapeDtypeStruct((rows, chans), BF16)
    turned = jax.ShapeDtypeStruct((chans, rows), BF16)
    blocks = pltpu.VMEM((n, cb, rows), BF16)
    spectrum = pltpu.VMEM((cb, 2 * seq), F32)
    sent_on = pl.pallas_call(
        functools.partial(operator_kernel, n, m),
        out_shape=[tokens] * 4 + [turned, jax.ShapeDtypeStruct((chans, taps), BF16)],
        in_specs=[hbm] * 11,
        out_specs=[hbm] * 6,
        scratch_shapes=[
            pltpu.VMEM((chans, rows), BF16),
            pltpu.VMEM((chans, rows), BF16),
            pltpu.VMEM((chans, rows), BF16),
            pltpu.VMEM((chans, rows), BF16),
            pltpu.VMEM((chans, taps), BF16),
            pltpu.VMEM((4, rows, chans), BF16),
            pltpu.VMEM((rows, chans), BF16),
            pltpu.VMEM((rows, chans), BF16),
            pltpu.VMEM((rows, chans), BF16),
            pltpu.VMEM((rows, chans), BF16),
            pltpu.VMEM((taps, chans), BF16),
            pltpu.VMEM((rows, chans), BF16),
            pltpu.VMEM((rows, chans), BF16),
            pltpu.VMEM((rows, chans), BF16),
            pltpu.VMEM((chans, rows), BF16),
            pltpu.VMEM(weight.shape, BF16),
            pltpu.VMEM(forward.shape, BF16),
            pltpu.VMEM(inverse.shape, BF16),
            pltpu.VMEM((m - 1, rows, chans), BF16),
            pltpu.VMEM((chans, rows), BF16),
            pltpu.VMEM((2, chans, rows), BF16),
            pltpu.VMEM((chans, rows), BF16),
            blocks,
            pltpu.VMEM((n, 2, cb, rows), BF16),
            blocks,
            blocks, blocks, blocks, blocks, blocks,
            pltpu.VMEM((cb, taps), BF16),
            pltpu.VMEM((chans, taps), BF16),
            pltpu.VMEM((2 * cb, seq), BF16),
            pltpu.VMEM((cb, seq), F32),
            spectrum, spectrum, spectrum,
            pltpu.VMEM((3 * cb, 2 * seq), BF16),
            pltpu.SemaphoreType.DMA((11,)),
            pltpu.SemaphoreType.DMA((6,)),
            pltpu.SemaphoreType.DMA((m - 1,)),
            pltpu.SemaphoreType.DMA((m - 1,)),
            pltpu.SemaphoreType.DMA((n - 1,)),
            pltpu.SemaphoreType.DMA((n - 1,)),
            pltpu.SemaphoreType.DMA((len(PARTS), n - 1)),
            pltpu.SemaphoreType.DMA((len(PARTS), n - 1)),
        ],
        compiler_params=pltpu.CompilerParams(
            collective_id=0, has_side_effects=True, vmem_limit_bytes=VMEM_GRANT
        ),
    )(sq, sk, sv, sf, lq, lk, lf, og, weight, jnp.asarray(forward), jnp.asarray(inverse))
    short = jax.ShapeDtypeStruct((taps, chans), BF16)
    return pl.pallas_call(
        finish_kernel,
        out_shape=[tokens] * 3 + [short] + [tokens] * 3,
        in_specs=[hbm] * 8,
        out_specs=[hbm] * 7,
        scratch_shapes=[
            pltpu.VMEM((chans, rows), BF16),
            pltpu.VMEM((chans, taps), BF16),
            pltpu.VMEM((rows, chans), BF16),
            pltpu.VMEM((rows, chans), BF16),
            pltpu.VMEM((rows, chans), BF16),
            pltpu.VMEM((rows, chans), BF16),
            pltpu.VMEM((taps, chans), BF16),
            pltpu.VMEM((4, rows, chans), BF16),
            pltpu.SemaphoreType.DMA((15,)),
        ],
        compiler_params=pltpu.CompilerParams(vmem_limit_bytes=VMEM_GRANT),
    )(*sent_on, sk, sv)


def body(n, m, *arrays):
    rows, chans = arrays[0].shape
    taps = arrays[3].shape[0]
    dense = (
        rows * n <= LONGEST_DENSE
        and rows % 128 == 0
        and taps % 128 == 0
        and taps <= rows * n
        and n > 1
        and n % 2 == 0
        and m > 1
        and m % 2 == 0
        and chans % (16 * n) == 0
        and chans % 128 == 0
    )
    if dense:
        return tuple(dense_body(n, m, *arrays))
    return general_body(*arrays)


def solution(mesh):
    in_specs = (
        P("ctx", "tp"),
        P("ctx", "tp"),
        P("ctx", "tp"),
        P(None, "tp"),
        P("ctx", "tp"),
        P("ctx", "tp"),
        P("ctx", "tp"),
        P("tp", None),
        P("ctx", "tp"),
    )
    out_specs = (
        P("ctx", "tp"),
        P("ctx", "tp"),
        P("ctx", "tp"),
        P(None, "tp"),
        P("ctx", "tp"),
        P("ctx", "tp"),
        P("ctx", "tp"),
    )
    return jax.shard_map(
        functools.partial(body, mesh.shape["ctx"], mesh.shape["tp"]), mesh=mesh, in_specs=in_specs, out_specs=out_specs, check_vma=False)
```

```python
import functools
import math

import jax
import jax.numpy as jnp
import ml_dtypes
import numpy as np
from jax import lax
from jax.experimental import pallas as pl
from jax.experimental.pallas import tpu as pltpu
from jax.sharding import PartitionSpec as P

MESH = pl.DeviceIdType.MESH
BF16 = jnp.bfloat16
F32 = jnp.float32
LONGEST_DENSE = 2048
VMEM_GRANT = 60 * 1024 * 1024
PARTS = ("prod", "gates", "grad", "smix", "lmix", "filt", "back", "bone")


def passed_along(block, axis, distance):
    devices = range(lax.axis_size(axis))
    route = [(i - distance, i) for i in devices if i - distance in devices]
    return lax.ppermute(block, axis, route)


def angle_tables(blocks, inner):
    size_one = 2 * blocks
    whole = size_one * inner
    first = (
        lax.broadcasted_iota(jnp.int32, (size_one, blocks), 0)
        * lax.broadcasted_iota(jnp.int32, (size_one, blocks), 1)
        % size_one
    )
    phase_one = first.astype(jnp.float32) * (2.0 * math.pi / size_one)
    twist = (
        lax.broadcasted_iota(jnp.int32, (size_one, inner), 0)
        * lax.broadcasted_iota(jnp.int32, (size_one, inner), 1)
        % whole
    )
    phase_twist = twist.astype(jnp.float32) * (2.0 * math.pi / whole)
    second = (
        lax.broadcasted_iota(jnp.int32, (inner, inner), 0)
        * lax.broadcasted_iota(jnp.int32, (inner, inner), 1)
        % inner
    )
    phase_two = second.astype(jnp.float32) * (2.0 * math.pi / inner)
    return (
        jnp.cos(phase_one),
        jnp.sin(phase_one),
        jnp.cos(phase_twist)[:, None, :],
        jnp.sin(phase_twist)[:, None, :],
        jnp.cos(phase_two),
        jnp.sin(phase_two),
        whole,
    )


def spectrum(values, tables):
    cos_one, sin_one, cos_twist, sin_twist, cos_two, sin_two, whole = tables
    highest = lax.Precision.HIGHEST
    real_a = jnp.einsum("kn,ncm->kcm", cos_one, values, precision=highest)
    imag_a = -jnp.einsum("kn,ncm->kcm", sin_one, values, precision=highest)
    real_b = real_a * cos_twist + imag_a * sin_twist
    imag_b = imag_a * cos_twist - real_a * sin_twist
    real_c = jnp.einsum("kcm,mq->kcq", real_b, cos_two, precision=highest) + jnp.einsum(
        "kcm,mq->kcq", imag_b, sin_two, precision=highest
    )
    imag_c = jnp.einsum("kcm,mq->kcq", imag_b, cos_two, precision=highest) - jnp.einsum(
        "kcm,mq->kcq", real_b, sin_two, precision=highest
    )
    return (real_c, imag_c)


def restore(real_in, imag_in, tables, both):
    cos_one, sin_one, cos_twist, sin_twist, cos_two, sin_two, whole = tables
    highest = lax.Precision.HIGHEST
    real_p = jnp.einsum("kcq,qm->kcm", real_in, cos_two, precision=highest) - jnp.einsum(
        "kcq,qm->kcm", imag_in, sin_two, precision=highest
    )
    imag_p = jnp.einsum("kcq,qm->kcm", imag_in, cos_two, precision=highest) + jnp.einsum(
        "kcq,qm->kcm", real_in, sin_two, precision=highest
    )
    real_q = real_p * cos_twist - imag_p * sin_twist
    imag_q = imag_p * cos_twist + real_p * sin_twist
    real_out = (
        jnp.einsum("kn,kcm->ncm", cos_one, real_q, precision=highest)
        - jnp.einsum("kn,kcm->ncm", sin_one, imag_q, precision=highest)
    ) / whole
    if both:
        imag_out = (
            jnp.einsum("kn,kcm->ncm", cos_one, imag_q, precision=highest)
            + jnp.einsum("kn,kcm->ncm", sin_one, real_q, precision=highest)
        ) / whole
        return (real_out, imag_out)
    return real_out


def spectral(product, gated, filter_in):
    blocks, count, inner = product.shape
    tables = angle_tables(blocks, inner)
    real_u, imag_u = spectrum(product.astype(jnp.float32), tables)
    real_g, imag_g = spectrum(gated.astype(jnp.float32), tables)
    real_h, imag_h = spectrum(filter_in.astype(jnp.float32), tables)
    real_pair = real_h * real_u - imag_h * imag_u - real_h * imag_g + imag_h * real_g
    imag_pair = real_h * imag_u + imag_h * real_u + real_h * real_g + imag_h * imag_g
    conv_part, back_part = restore(real_pair, imag_pair, tables, True)
    filter_part = restore(
        real_u * real_g + imag_u * imag_g, real_u * imag_g - imag_u * real_g, tables, False
    )
    return (conv_part, back_part, filter_part)


def tap_sum(extended, weights, token_rows, causal):
    filter_taps, channels = weights.shape

    def group_step(group, total):
        for inner in range(8):
            place = group * 8 + inner
            weight_row = lax.dynamic_index_in_dim(weights, place, 0, keepdims=False).astype(
                jnp.float32
            )
            start = filter_taps - 1 - place if causal else place
            shifted = lax.dynamic_slice_in_dim(extended, start, token_rows, 0).astype(jnp.float32)
            total = total + weight_row[None, :] * shifted
        return total

    return lax.fori_loop(
        0, filter_taps // 8, group_step, jnp.zeros((token_rows, channels), jnp.float32)
    )


def filter_terms(extended, grads, filter_taps):
    token_rows, channels = grads.shape

    def group_terms(group):
        partials = []
        for inner in range(8):
            place = group * 8 + inner
            shifted = lax.dynamic_slice_in_dim(
                extended, filter_taps - 1 - place, token_rows, 0
            ).astype(jnp.float32)
            partials.append(jnp.sum(grads * shifted, axis=0))
        return jnp.stack(partials)

    stacked = lax.map(group_terms, jnp.arange(filter_taps // 8, dtype=jnp.int32))
    return stacked.reshape(filter_taps, channels)


def general_body(
    short_query,
    short_key,
    short_value,
    short_filter,
    long_query,
    long_key,
    long_filter,
    out_weight,
    out_grad,
):
    token_rows, channels = short_query.shape
    groups = lax.axis_size("ctx")
    seq_len = token_rows * groups
    scaling = 1.0 / math.sqrt(seq_len)
    filter_taps = short_filter.shape[0]
    product_one = (short_key.astype(jnp.float32) * short_value.astype(jnp.float32)).astype(
        jnp.bfloat16
    )
    before = passed_along(product_one[token_rows - (filter_taps - 1) :], "ctx", 1)
    extended_prod = jnp.concatenate([before, product_one], axis=0)
    short_mix = tap_sum(extended_prod, short_filter, token_rows, True)
    mixed = (short_query.astype(jnp.float32) * short_mix).astype(jnp.bfloat16)
    grad_two = lax.dot_general(
        lax.all_gather(out_grad, "tp", axis=1, tiled=True),
        out_weight,
        (((1,), (1,)), ((), ())),
        preferred_element_type=jnp.float32,
    ).astype(jnp.bfloat16)

    def to_channels(values):
        return values.T.reshape(groups, channels // groups, token_rows)

    def to_tokens(values):
        return values.reshape(channels, token_rows).T

    product_two = (long_key.astype(jnp.float32) * mixed.astype(jnp.float32)).astype(jnp.bfloat16)
    gated_two = (grad_two.astype(jnp.float32) * long_query.astype(jnp.float32)).astype(jnp.bfloat16)
    conv_part, back_part, filter_part = spectral(
        lax.all_to_all(to_channels(product_two), "ctx", split_axis=0, concat_axis=0, tiled=True),
        lax.all_to_all(to_channels(gated_two), "ctx", split_axis=0, concat_axis=0, tiled=True),
        lax.all_to_all(to_channels(long_filter), "ctx", split_axis=0, concat_axis=0, tiled=True),
    )
    long_mix = lax.all_to_all(conv_part, "ctx", split_axis=0, concat_axis=0, tiled=True)
    back_two = lax.all_to_all(back_part, "ctx", split_axis=0, concat_axis=0, tiled=True)
    filter_two = lax.all_to_all(filter_part, "ctx", split_axis=0, concat_axis=0, tiled=True)
    long_mix = to_tokens(long_mix)
    back_two = to_tokens(back_two)
    filter_two = to_tokens(filter_two)
    long_query_grad = (grad_two.astype(jnp.float32) * long_mix).astype(jnp.bfloat16)
    long_key_grad = (back_two * mixed.astype(jnp.float32)).astype(jnp.bfloat16)
    mixed_grad = (back_two * long_key.astype(jnp.float32)).astype(jnp.bfloat16)
    long_filter_grad = (filter_two * scaling).astype(jnp.bfloat16)
    gated_one = (mixed_grad.astype(jnp.float32) * short_query.astype(jnp.float32)).astype(
        jnp.bfloat16
    )
    short_query_grad = (mixed_grad.astype(jnp.float32) * short_mix).astype(jnp.bfloat16)
    after = passed_along(gated_one[: filter_taps - 1], "ctx", -1)
    extended_grad = jnp.concatenate([gated_one, after], axis=0)
    back_one = tap_sum(extended_grad, short_filter, token_rows, False)
    short_key_grad = (back_one * short_value.astype(jnp.float32)).astype(jnp.bfloat16)
    short_value_grad = (back_one * short_key.astype(jnp.float32)).astype(jnp.bfloat16)
    local_terms = filter_terms(extended_prod, gated_one.astype(jnp.float32), filter_taps)
    filter_one = lax.psum(local_terms, "ctx")
    short_filter_grad = (filter_one * scaling).astype(jnp.bfloat16)
    return (
        short_query_grad,
        short_key_grad,
        short_value_grad,
        short_filter_grad,
        long_query_grad,
        long_key_grad,
        long_filter_grad,
    )


def wave_tables(seq_len):
    time = np.arange(seq_len, dtype=np.int64)[:, None]
    odd = 2 * np.arange(seq_len, dtype=np.int64)[None, :] + 1
    phase = (time * odd % (4 * seq_len)).astype(np.float64) * (math.pi / (2 * seq_len))
    forward = np.concatenate([np.cos(phase), np.sin(phase)], axis=1)
    return (
        forward.astype(ml_dtypes.bfloat16),
        np.ascontiguousarray(forward.T).astype(ml_dtypes.bfloat16),
    )


def dot(a, b):
    return jnp.dot(a, b, preferred_element_type=F32)


def flipped(block):
    return block.astype(F32).T.astype(BF16)


def operator_kernel(
    n, m,
    sq_in, sk_in, sv_in, sf_in, lq_in, lk_in, lf_in, og_in, weight, forward, inverse,
    sq_grad, lq_grad, lk_grad, lf_grad, bone_out, taps_out,
    smix_rx, lmix_rx, filt_rx, back_rx, taps_rx, results, sq, sk, sv, lk, sf, lq, lf, og, grad, weight_v, fwd, inv, og_rx, tx_prod, tx_gates, tx_grad, rx_prod, rx_gates, rx_grad,
    tx_smix, tx_lmix, tx_filt, tx_back, tx_bone, tx_taps, filter_t, signals, smix,
    spec_prod, spec_sf, spec_u, spec_h, waves, load_sem, own_sem, og_send, og_recv, taps_send, taps_recv,
    send, recv,
):
    me = lax.axis_index("ctx")
    col = lax.axis_index("tp")
    rows, chans = sq.shape
    cb = chans // n
    taps = sf.shape[0]
    seq = rows * n
    tile = 2 * rows
    kt = 256

    barrier = pltpu.get_barrier_semaphore()
    for d in range(1, n):
        pl.semaphore_signal(
            barrier, inc=1, device_id=(lax.rem(me + d, n), col), device_id_type=MESH
        )
    for d in range(1, m):
        pl.semaphore_signal(
            barrier, inc=1, device_id=(me, lax.rem(col + d, m)), device_id_type=MESH
        )

    loads = {}
    for place, (name, source, target) in enumerate((
        ("sk", sk_in, sk), ("sv", sv_in, sv), ("og", og_in, og), ("lf", lf_in, lf),
        ("lk", lk_in, lk), ("sq", sq_in, sq), ("sf", sf_in, sf), ("fwd", forward, fwd),
        ("lq", lq_in, lq), ("weight", weight, weight_v), ("inv", inverse, inv),
    )):
        loads[name] = pltpu.make_async_copy(source, target, load_sem.at[place])
        loads[name].start()

    loads["sk"].wait()
    loads["sv"].wait()
    tx_prod[...] = (sk[...].astype(F32) * sv[...].astype(F32)).T.astype(BF16)
    loads["og"].wait()
    pl.semaphore_wait(barrier, n + m - 2)

    col_pair = col + 1 - 2 * lax.rem(col, 2)

    def og_copy(slot, source, peer):
        copy = pltpu.make_async_remote_copy(
            src_ref=source,
            dst_ref=og_rx.at[slot],
            send_sem=og_send.at[slot],
            recv_sem=og_recv.at[slot],
            device_id=(me, peer),
            device_id_type=MESH,
        )
        copy.start()
        return copy

    og_far = [og_copy(d, og, lax.rem(col + 2 * d, m)) for d in range(1, m // 2)]
    og_near = [og_copy(0, og, col_pair)]

    own_rows = pl.ds(pl.multiple_of(me * cb, cb), cb)
    sent = {}

    def exchange(part, source, target):
        place = PARTS.index(part)
        copies = []
        for d in range(1, n):
            peer = lax.rem(me + d, n)
            copy = pltpu.make_async_remote_copy(
                src_ref=source(peer),
                dst_ref=target,
                send_sem=send.at[place, d - 1],
                recv_sem=recv.at[place, d - 1],
                device_id=(peer, col),
                device_id_type=MESH,
            )
            copy.start()
            copies.append(copy)
        sent[part] = copies

    kept = []

    def keep(source, target):
        copy = pltpu.make_async_copy(source, target, own_sem.at[len(kept)])
        copy.start()
        kept.append(copy)

    def arrived(part):
        for copy in sent[part]:
            copy.wait_recv()

    def row_block(peer):
        return pl.ds(pl.multiple_of(peer * cb, cb), cb)

    exchange("prod", lambda peer: tx_prod.at[row_block(peer)], rx_prod.at[me])
    rx_prod[me] = tx_prod[own_rows]
    loads["lf"].wait()
    tx_gates[0] = flipped(lf[...])
    loads["lk"].wait()
    loads["sq"].wait()
    tx_gates[1] = (lk[...].astype(F32) * sq[...].astype(F32)).T.astype(BF16)
    exchange("gates", lambda peer: tx_gates.at[:, row_block(peer)], rx_gates.at[me])
    for place in range(2):
        rx_gates[me, place] = tx_gates[place, own_rows]
    loads["sf"].wait()
    filter_t[...] = flipped(sf[...])

    def tiles(k):
        start = pl.multiple_of(k * kt, kt)
        return pl.ds(start, kt), pl.ds(pl.multiple_of(seq + start, kt), kt)

    def halves(rows_in, depth, k):
        cos_at, sin_at = tiles(k)
        return dot(rows_in, fwd[:depth, cos_at]), dot(rows_in, fwd[:depth, sin_at])

    for d in range(1, m // 2):
        og_far[d - 1].wait_recv()
        og_near.append(og_copy(m // 2 - 1 + d, og_rx.at[d], col_pair))

    arrived("prod")
    for s in range(n):
        signals[0:cb, s * rows : (s + 1) * rows] = rx_prod[s]
    loads["fwd"].wait()

    def short_step(k, carry):
        cos_at, sin_at = tiles(k)
        pc, ps = halves(signals[0:cb, :], seq, k)
        fc, fs = halves(filter_t[own_rows, :], taps, k)
        spec_prod[:, cos_at] = pc
        spec_prod[:, sin_at] = ps
        spec_sf[:, cos_at] = fc
        spec_sf[:, sin_at] = fs
        waves[0:cb, cos_at] = (pc * fc - ps * fs).astype(BF16)
        waves[0:cb, sin_at] = (pc * fs + ps * fc).astype(BF16)
        return carry

    lax.fori_loop(0, seq // kt, short_step, 0, unroll=True)
    loads["inv"].wait()

    def at_tokens(step):
        return pl.ds(pl.multiple_of(step * tile, tile), tile)

    def put(target, step, values):
        for b in range(2):
            target[step * 2 + b] = values[:, b * rows : (b + 1) * rows].astype(BF16)

    def short_back(step, carry):
        mix = dot(waves[0:cb, :], inv[:, at_tokens(step)]) * (1.0 / seq)
        smix[:, at_tokens(step)] = mix
        put(tx_smix, step, mix)
        return carry

    lax.fori_loop(0, n // 2, short_back, 0, unroll=True)

    loads["weight"].wait()
    loads["lq"].wait()
    def projected(owner, block):
        features = pl.ds(pl.multiple_of(owner * chans, chans), chans)
        return lax.dot_general(
            weight_v[:, features], block, (((1,), (1,)), ((), ())), preferred_element_type=F32
        )

    total = projected(col, og[...])
    for d in range(1, m // 2):
        total = total + projected(lax.rem(col + m - 2 * d, m), og_rx[d])
    for place, copy in enumerate(og_near):
        copy.wait_recv()
        owner = lax.rem(col_pair + m - 2 * place, m)
        total = total + projected(owner, og_rx[0 if place == 0 else m // 2 - 1 + place])
    grad[...] = total.astype(BF16)
    tx_grad[...] = (grad[...].astype(F32) * lq[...].astype(F32).T).astype(BF16)
    exchange("grad", lambda peer: tx_grad.at[row_block(peer)], rx_grad.at[me])
    rx_grad[me] = tx_grad[own_rows]
    exchange("smix", lambda peer: tx_smix.at[peer], smix_rx.at[own_rows])
    smix_rx[own_rows, :] = tx_smix[me]

    arrived("gates")
    for s in range(n):
        at = slice(s * rows, (s + 1) * rows)
        signals[0:cb, at] = (rx_gates[s, 1].astype(F32) * smix[:, at]).astype(BF16)
        signals[cb : 2 * cb, at] = rx_gates[s, 0]

    def long_step(k, carry):
        cos_at, sin_at = tiles(k)
        c, s = halves(signals[0 : 2 * cb, :], seq, k)
        spec_u[:, cos_at] = c[0:cb]
        spec_u[:, sin_at] = s[0:cb]
        spec_h[:, cos_at] = c[cb:]
        spec_h[:, sin_at] = s[cb:]
        waves[0:cb, cos_at] = (c[0:cb] * c[cb:] - s[0:cb] * s[cb:]).astype(BF16)
        waves[0:cb, sin_at] = (c[0:cb] * s[cb:] + s[0:cb] * c[cb:]).astype(BF16)
        return carry

    lax.fori_loop(0, seq // kt, long_step, 0, unroll=True)

    def mix_back(step, carry):
        put(tx_lmix, step, dot(waves[0:cb, :], inv[:, at_tokens(step)]) * (1.0 / seq))
        return carry

    lax.fori_loop(0, n // 2, mix_back, 0, unroll=True)
    exchange("lmix", lambda peer: tx_lmix.at[peer], lmix_rx.at[own_rows])
    lmix_rx[own_rows, :] = tx_lmix[me]

    arrived("grad")
    for s in range(n):
        signals[2 * cb : 3 * cb, s * rows : (s + 1) * rows] = rx_grad[s]

    def grad_step(k, carry):
        cos_at, sin_at = tiles(k)
        c, s = halves(signals[2 * cb : 3 * cb, :], seq, k)
        uc, us = spec_u[:, cos_at], spec_u[:, sin_at]
        hc, hs = spec_h[:, cos_at], spec_h[:, sin_at]
        waves[cb : 2 * cb, cos_at] = (hc * c + hs * s).astype(BF16)
        waves[cb : 2 * cb, sin_at] = (hc * s - hs * c).astype(BF16)
        waves[2 * cb : 3 * cb, cos_at] = (uc * c + us * s).astype(BF16)
        waves[2 * cb : 3 * cb, sin_at] = (uc * s - us * c).astype(BF16)
        return carry

    lax.fori_loop(0, seq // kt, grad_step, 0, unroll=True)

    def long_back(step, carry):
        mixes = dot(waves[cb:, :], inv[:, at_tokens(step)]) * (1.0 / seq)
        put(tx_back, step, mixes[0:cb])
        put(tx_filt, step, mixes[cb:] * (1.0 / math.sqrt(seq)))
        smix[:, at_tokens(step)] = mixes[0:cb]
        return carry

    lax.fori_loop(0, n // 2, long_back, 0, unroll=True)
    for part, source, target in (
        ("back", tx_back, back_rx), ("filt", tx_filt, filt_rx)
    ):
        exchange(part, lambda peer, source=source: source.at[peer], target.at[own_rows])
        target[own_rows, :] = source[me]

    for s in range(n):
        at = slice(s * rows, (s + 1) * rows)
        signals[0:cb, at] = (smix[:, at] * rx_gates[s, 1].astype(F32)).astype(BF16)

    def gate_step(k, carry):
        cos_at, sin_at = tiles(k)
        c, s = halves(signals[0:cb, :], seq, k)
        pc, ps = spec_prod[:, cos_at], spec_prod[:, sin_at]
        fc, fs = spec_sf[:, cos_at], spec_sf[:, sin_at]
        waves[0:cb, cos_at] = (fc * c + fs * s).astype(BF16)
        waves[0:cb, sin_at] = (fc * s - fs * c).astype(BF16)
        waves[cb : 2 * cb, cos_at] = (pc * c + ps * s).astype(BF16)
        waves[cb : 2 * cb, sin_at] = (pc * s - ps * c).astype(BF16)
        return carry

    lax.fori_loop(0, seq // kt, gate_step, 0, unroll=True)

    terms = dot(waves[cb : 2 * cb, :], inv[:, 0:taps]) * (1.0 / (seq * math.sqrt(seq)))
    tx_taps[...] = terms.astype(BF16)
    taps_rx[own_rows, :] = tx_taps[...]
    pair = me + 1 - 2 * lax.rem(me, 2)

    def taps_copy(place, source, target_rows, peer):
        copy = pltpu.make_async_remote_copy(
            src_ref=source,
            dst_ref=taps_rx.at[target_rows],
            send_sem=taps_send.at[place],
            recv_sem=taps_recv.at[place],
            device_id=(peer, col),
            device_id_type=MESH,
        )
        copy.start()
        return copy

    far = [
        taps_copy(d - 1, tx_taps, own_rows, lax.rem(me + 2 * d, n)) for d in range(1, n // 2)
    ]
    near = [taps_copy(n // 2 - 1, tx_taps, own_rows, pair)]

    def short_grad(step, carry):
        put(tx_bone, step, dot(waves[0:cb, :], inv[:, at_tokens(step)]) * (1.0 / seq))
        return carry

    lax.fori_loop(0, n // 2, short_grad, 0, unroll=True)
    exchange("bone", lambda peer: tx_bone.at[peer], bone_out.at[own_rows])
    keep(tx_bone.at[me], bone_out.at[own_rows])

    def finish(place, target, values):
        results[place] = values.T.astype(BF16)
        keep(results.at[place], target)

    arrived("smix")
    arrived("lmix")
    finish(0, lq_grad, grad[...].astype(F32) * lmix_rx[...].astype(F32))
    for d in range(1, n // 2):
        far[d - 1].wait_recv()
        source = row_block(lax.rem(me + n - 2 * d, n))
        near.append(taps_copy(n // 2 - 1 + d, taps_rx.at[source], source, pair))
    arrived("back")
    back = back_rx[...].astype(F32).T
    mix = smix_rx[...].astype(F32).T
    mixed = (sq[...].astype(F32) * mix).astype(BF16).astype(F32)
    results[1] = (back * mixed).astype(BF16)
    keep(results.at[1], lk_grad)
    mixed_grad = (back * lk[...].astype(F32)).astype(BF16).astype(F32)
    results[2] = (mixed_grad * mix).astype(BF16)
    keep(results.at[2], sq_grad)
    arrived("filt")
    finish(3, lf_grad, filt_rx[...].astype(F32))

    for copy in near:
        copy.wait_recv()
    keep(taps_rx, taps_out)

    arrived("bone")
    for part in PARTS:
        for copy in sent[part]:
            copy.wait_send()
    for copy in og_far + og_near + far + near:
        copy.wait_send()
    for copy in kept:
        copy.wait()


def finish_kernel(
    sq_done, lq_done, lk_done, lf_done, bone, taps, sk, sv,
    sq_grad, sk_grad, sv_grad, sf_grad, lq_grad, lk_grad, lf_grad,
    bone_v, taps_v, sk_v, sv_v, sk_out, sv_out, sf_out, done_v, move_sem,
):
    def move(place, source, target):
        copy = pltpu.make_async_copy(source, target, move_sem.at[place])
        copy.start()
        return copy

    loads = [
        move(place, source, target)
        for place, (source, target) in enumerate(
            ((bone, bone_v), (sv, sv_v), (sk, sk_v), (taps, taps_v))
        )
    ]
    done = [
        move(4 + place, source, done_v.at[place])
        for place, source in enumerate((sq_done, lq_done, lk_done, lf_done))
    ]
    moves = []
    for place, target in enumerate((sq_grad, lq_grad, lk_grad, lf_grad)):
        done[place].wait()
        moves.append(move(11 + place, done_v.at[place], target))
    loads[0].wait()
    back_one = bone_v[...].astype(F32).T
    loads[1].wait()
    sk_out[...] = (back_one * sv_v[...].astype(F32)).astype(BF16)
    moves.append(move(8, sk_out, sk_grad))
    loads[2].wait()
    sv_out[...] = (back_one * sk_v[...].astype(F32)).astype(BF16)
    moves.append(move(9, sv_out, sv_grad))
    loads[3].wait()
    sf_out[...] = flipped(taps_v[...])
    moves.append(move(10, sf_out, sf_grad))
    for copy in moves:
        copy.wait()


def dense_body(
    n, m, sq, sk, sv, sf, lq, lk, lf, weight, og
):
    rows, chans = sq.shape
    taps = sf.shape[0]
    seq = rows * n
    cb = chans // n
    forward, inverse = wave_tables(seq)
    hbm = pl.BlockSpec(memory_space=pltpu.HBM)
    tokens = jax.ShapeDtypeStruct((rows, chans), BF16)
    turned = jax.ShapeDtypeStruct((chans, rows), BF16)
    blocks = pltpu.VMEM((n, cb, rows), BF16)
    spectrum = pltpu.VMEM((cb, 2 * seq), F32)
    sent_on = pl.pallas_call(
        functools.partial(operator_kernel, n, m),
        out_shape=[tokens] * 4 + [turned, jax.ShapeDtypeStruct((chans, taps), BF16)],
        in_specs=[hbm] * 11,
        out_specs=[hbm] * 6,
        scratch_shapes=[
            pltpu.VMEM((chans, rows), BF16),
            pltpu.VMEM((chans, rows), BF16),
            pltpu.VMEM((chans, rows), BF16),
            pltpu.VMEM((chans, rows), BF16),
            pltpu.VMEM((chans, taps), BF16),
            pltpu.VMEM((4, rows, chans), BF16),
            pltpu.VMEM((rows, chans), BF16),
            pltpu.VMEM((rows, chans), BF16),
            pltpu.VMEM((rows, chans), BF16),
            pltpu.VMEM((rows, chans), BF16),
            pltpu.VMEM((taps, chans), BF16),
            pltpu.VMEM((rows, chans), BF16),
            pltpu.VMEM((rows, chans), BF16),
            pltpu.VMEM((rows, chans), BF16),
            pltpu.VMEM((chans, rows), BF16),
            pltpu.VMEM(weight.shape, BF16),
            pltpu.VMEM(forward.shape, BF16),
            pltpu.VMEM(inverse.shape, BF16),
            pltpu.VMEM((m - 1, rows, chans), BF16),
            pltpu.VMEM((chans, rows), BF16),
            pltpu.VMEM((2, chans, rows), BF16),
            pltpu.VMEM((chans, rows), BF16),
            blocks,
            pltpu.VMEM((n, 2, cb, rows), BF16),
            blocks,
            blocks, blocks, blocks, blocks, blocks,
            pltpu.VMEM((cb, taps), BF16),
            pltpu.VMEM((chans, taps), BF16),
            pltpu.VMEM((3 * cb, seq), BF16),
            pltpu.VMEM((cb, seq), F32),
            spectrum, spectrum, spectrum, spectrum,
            pltpu.VMEM((3 * cb, 2 * seq), BF16),
            pltpu.SemaphoreType.DMA((11,)),
            pltpu.SemaphoreType.DMA((6,)),
            pltpu.SemaphoreType.DMA((m - 1,)),
            pltpu.SemaphoreType.DMA((m - 1,)),
            pltpu.SemaphoreType.DMA((n - 1,)),
            pltpu.SemaphoreType.DMA((n - 1,)),
            pltpu.SemaphoreType.DMA((len(PARTS), n - 1)),
            pltpu.SemaphoreType.DMA((len(PARTS), n - 1)),
        ],
        compiler_params=pltpu.CompilerParams(
            collective_id=0, has_side_effects=True, vmem_limit_bytes=VMEM_GRANT
        ),
    )(sq, sk, sv, sf, lq, lk, lf, og, weight, jnp.asarray(forward), jnp.asarray(inverse))
    short = jax.ShapeDtypeStruct((taps, chans), BF16)
    return pl.pallas_call(
        finish_kernel,
        out_shape=[tokens] * 3 + [short] + [tokens] * 3,
        in_specs=[hbm] * 8,
        out_specs=[hbm] * 7,
        scratch_shapes=[
            pltpu.VMEM((chans, rows), BF16),
            pltpu.VMEM((chans, taps), BF16),
            pltpu.VMEM((rows, chans), BF16),
            pltpu.VMEM((rows, chans), BF16),
            pltpu.VMEM((rows, chans), BF16),
            pltpu.VMEM((rows, chans), BF16),
            pltpu.VMEM((taps, chans), BF16),
            pltpu.VMEM((4, rows, chans), BF16),
            pltpu.SemaphoreType.DMA((15,)),
        ],
        compiler_params=pltpu.CompilerParams(vmem_limit_bytes=VMEM_GRANT),
    )(*sent_on, sk, sv)


def body(n, m, *arrays):
    rows, chans = arrays[0].shape
    taps = arrays[3].shape[0]
    dense = (
        rows * n <= LONGEST_DENSE
        and rows % 128 == 0
        and taps % 128 == 0
        and taps <= rows * n
        and n > 1
        and n % 2 == 0
        and m > 1
        and m % 2 == 0
        and chans % (16 * n) == 0
        and chans % 128 == 0
    )
    if dense:
        return tuple(dense_body(n, m, *arrays))
    return general_body(*arrays)


def solution(mesh):
    in_specs = (
        P("ctx", "tp"),
        P("ctx", "tp"),
        P("ctx", "tp"),
        P(None, "tp"),
        P("ctx", "tp"),
        P("ctx", "tp"),
        P("ctx", "tp"),
        P("tp", None),
        P("ctx", "tp"),
    )
    out_specs = (
        P("ctx", "tp"),
        P("ctx", "tp"),
        P("ctx", "tp"),
        P(None, "tp"),
        P("ctx", "tp"),
        P("ctx", "tp"),
        P("ctx", "tp"),
    )
    return jax.shard_map(
        functools.partial(body, mesh.shape["ctx"], mesh.shape["tp"]), mesh=mesh, in_specs=in_specs, out_specs=out_specs, check_vma=False)
```
